256 devices in a mesh: lon: 32 (over y_lo, z, core), lat: 8 (over y_hi, x).
Axes of the slice: x: 4, y: 4 (y_hi: 2, y_lo: 2; y = y_hi * 2 + y_lo), z: 8, core: 2. Of those that a mesh axis runs over, the one named last changes fastest.
Arguments:
- field: bfloat16 [512, 128, 512], P('lon', 'lat'), may hold values from -6 to 6
- cotangent: bfloat16 [512, 128, 512], P('lon', 'lat'), may hold values from -6 to 6
- land_sea: int32 [512, 128], P('lon', 'lat'), may hold values 0 or 1
- fold_partner: int32 [512], replicated, may hold values from 0 to 511, as said below
- depth_kernel: float32 [49, 512], replicated, may hold values from -0.875 to 0.875
- norm_gain: float32 [512], replicated, may hold values from 0.5 to 1.5
- w_up: bfloat16 [512, 2048], replicated, may hold values from -0.25 to 0.25
- b_up: float32 [2048], replicated, may hold values from -3 to 3
- w_down: bfloat16 [2048, 512], replicated, may hold values from -0.125 to 0.125
Outputs:
- grad_field: bfloat16 [512, 128, 512], P('lon', 'lat')
- grad_up: float32 [512, 2048], P(('lon', 'lat'))
- grad_down: float32 [2048, 512], P(('lon', 'lat'))
- grad_kernel: float32 [49, 512], replicated
- grad_gain: float32 [512], replicated
- grad_bias: float32 [2048], replicated
The draws below stay inside these ranges and needn't reach their ends.
Inputs may be any that keep to these rules, and one draw needn't show every extreme that they name: fold_partner[j] = (fold_partner[0] - j) mod 512 for every column j, a mirror of the columns; 511 - fold_partner[0] is at least 16 and not a multiple of 16.
All inputs are finite; a program needn't handle non-finite values. No bound on the sum of `land_sea` on one device may be relied on, other than what follows from the above.
Results may differ from the reference program's by a relative error of at most 0.013.
Values may be sent and summed in bfloat16 or wider, within the bound.
No kernel may reach another device: no remote copies, remote signals or barrier semaphores. Data moves between devices by JAX's collectives and lax.ppermute only.
A program may use at most 128 MiB of HBM per device.

```python
import jax
import jax.numpy as jnp
from jax import lax

C = 512
HID = 2048
KS = 7
TX = 16
TY = 16
NX = 512
NY = 128


def draw_fold_partner(key, part):
    key = jax.random.fold_in(key, 7)
    tile_key, inner_key = jax.random.split(key)
    tile_count = NX // TX
    tile_steps = jax.random.randint(tile_key, (), 1, tile_count, dtype=jnp.int32)
    within = jax.random.randint(inner_key, (), 1, TX, dtype=jnp.int32)
    offset = NX - 1 - (tile_steps * TX + within)
    columns = jnp.arange(NX, dtype=jnp.int32)
    return jnp.mod(offset - columns, NX).astype(jnp.int32)


def set_ends(values, stream_key, low, largest):
    index_at = [jax.random.randint(jax.random.fold_in(stream_key, axis), (), 0, length) for axis, length in enumerate(values.shape)]
    main_axis = values.shape.index(max(values.shape))
    next_to = index_at[:main_axis] + [(index_at[main_axis] + 1) % values.shape[main_axis]] + index_at[main_axis + 1:]
    return values.at[tuple(index_at)].set(low).at[tuple(next_to)].set(largest)


def steps_of(key, shape, cuts, low, top_value):
    loudness = 1.0
    for axis_at, parts in cuts:
        draws = jax.random.uniform(jax.random.fold_in(jax.random.fold_in(key, 6), axis_at), (parts,), jnp.float32, low / len(cuts), top_value / len(cuts))
        loudness = loudness * jnp.repeat(jnp.exp(draws), shape[axis_at] // parts).reshape((-1,) + (1,) * (len(shape) - 1 - axis_at))
    return loudness


def gaussian(stream_key, shape, deviation, most, shards=(), held_as=jnp.bfloat16):
    level = steps_of(stream_key, shape, shards, -0.22, 0.18) if shards else 1.0
    result = jax.random.normal(stream_key, shape, jnp.float32) * deviation * level
    return jnp.minimum(jnp.maximum(result, -most), most).astype(held_as)


def setup_inputs(seed: int = 0) -> dict:
    streams_of = jax.random.split(jax.random.key(seed), 10)
    return {
        "field": gaussian(streams_of[0], (NX, NY, C), 1.0, 6.0, ((0, 32), (1, 8))),
        "cotangent": gaussian(streams_of[1], (NX, NY, C), 1.0, 6.0, ((0, 32), (1, 8))),
        "land_sea": set_ends((jax.random.randint(streams_of[2], (NX, NY), 0, 4) < 3).astype(jnp.int32), jax.random.fold_in(streams_of[2], 1), 0, 1),
        "fold_partner": draw_fold_partner(jax.random.fold_in(streams_of[9], 71), 0),
        "depth_kernel": gaussian(streams_of[4], (KS * KS, C), (KS * KS) ** -0.5, 0.875, (), jnp.float32),
        "norm_gain": jnp.clip(1.0 + 0.1 * jax.random.normal(streams_of[5], (C,), jnp.float32), 0.5, 1.5),
        "w_up": gaussian(streams_of[6], (C, HID), C ** -0.5, 0.25),
        "b_up": gaussian(streams_of[7], (HID,), 0.5, 3.0, (), jnp.float32),
        "w_down": gaussian(streams_of[8], (HID, C), HID ** -0.5, 0.125),
    }


def build_ext(flat, partner):
    top_band = flat[:, NY - 3:, :][partner][:, ::-1, :]
    zero_band = jnp.zeros((NX, 3, C), jnp.float32)
    column = jnp.concatenate([zero_band, flat, top_band], axis=1)
    return jnp.concatenate([column[NX - 3:], column, column[:3]], axis=0)

def conv_depth(extended, kernel):
    cols_out = extended.shape[0] - 6
    rows_out = extended.shape[1] - 6
    total = jnp.zeros((cols_out, rows_out, extended.shape[2]), jnp.float32)
    for row_off in range(7):
        for col_off in range(7):
            piece = extended[row_off:row_off + cols_out, col_off:col_off + rows_out, :].astype(jnp.float32)
            total = total + piece * kernel[row_off * 7 + col_off]
    return total

def layer_norm(rows, gain):
    center = rows - lax.optimization_barrier(jnp.mean(rows, axis=-1, keepdims=True))
    spread = lax.optimization_barrier(jnp.mean(center * center, axis=-1, keepdims=True))
    return center * lax.rsqrt(spread + 1e-06) * gain

def pointwise(mixed_rows, gain, w_up, b_up, w_down, d_out):
    normed_f, norm_back = jax.vjp(layer_norm, mixed_rows, gain)
    normed = normed_f.astype(jnp.bfloat16)
    upper = jnp.dot(normed, w_up, preferred_element_type=jnp.float32) + b_up
    active_f, gelu_back = jax.vjp(lambda v: jax.nn.gelu(v, approximate=True), upper)
    active = active_f.astype(jnp.bfloat16)
    d_active = lax.dot_general(d_out, w_down, (((1,), (1,)), ((), ())), preferred_element_type=jnp.float32)
    d_upper = gelu_back(d_active)[0].astype(jnp.bfloat16)
    d_normed = lax.dot_general(d_upper, w_up, (((1,), (1,)), ((), ())), preferred_element_type=jnp.float32)
    d_mixed, d_gain = norm_back(d_normed)
    return (normed, active, d_upper, d_mixed, d_gain)

def reference(field, cotangent, land_sea, fold_partner, depth_kernel, norm_gain, w_up, b_up, w_down):
    flat = field.astype(jnp.float32)
    extended, ext_back = jax.vjp(lambda v: build_ext(v, fold_partner), flat)
    mixed, conv_back = jax.vjp(conv_depth, extended, depth_kernel)
    block = TX * TY
    count = NX * NY // block
    mixed_rows = mixed.reshape(count, block, C)
    d_out = (cotangent * land_sea[:, :, None].astype(jnp.bfloat16)).reshape(count, block, C)

    def step(carry, pair):
        acc_up, acc_down, acc_bias, acc_gain = carry
        rows, d_rows = pair
        normed, active, d_upper, d_mixed, d_gain = pointwise(rows, norm_gain, w_up, b_up, w_down, d_rows)
        acc_up = acc_up + lax.dot_general(normed, d_upper, (((0,), (0,)), ((), ())), preferred_element_type=jnp.float32)
        acc_down = acc_down + lax.dot_general(active, d_rows, (((0,), (0,)), ((), ())), preferred_element_type=jnp.float32)
        acc_bias = acc_bias + lax.optimization_barrier(jnp.sum(d_upper.astype(jnp.float32), axis=0))
        acc_gain = acc_gain + d_gain
        return ((acc_up, acc_down, acc_bias, acc_gain), d_mixed)
    start = (jnp.zeros((C, HID), jnp.float32), jnp.zeros((HID, C), jnp.float32), jnp.zeros((HID,), jnp.float32), jnp.zeros((C,), jnp.float32))
    (grad_up, grad_down, grad_bias, grad_gain), d_mixed = lax.scan(step, start, (mixed_rows, d_out))
    grad_ext, grad_kernel = conv_back(d_mixed.reshape(NX, NY, C))
    grad_flat = ext_back(grad_ext)[0]
    grad_field = (cotangent.astype(jnp.float32) + grad_flat).astype(jnp.bfloat16)
    return (grad_field, grad_up, grad_down, grad_kernel, grad_gain, grad_bias)
```

```python
import jax
import jax.numpy as jnp
from jax import lax
from jax.sharding import PartitionSpec as P


def extended_2(cells, sides, width, closed):
    for axis, dim in sides:
        count = lax.axis_size(axis)
        ends = count if closed else count - 1
        head = lax.slice_in_dim(cells, 0, width, axis=dim)
        tail = lax.slice_in_dim(cells, cells.shape[dim] - width, cells.shape[dim], axis=dim)
        cells = jnp.concatenate(
            [
                lax.ppermute(tail, axis, [(i, (i + 1) % count) for i in range(ends)]),
                cells,
                lax.ppermute(head, axis, [((i + 1) % count, i) for i in range(ends)]),
            ],
            axis=dim,
        )
    return cells


def conv_depth(extended, kernel):
    cols_out = extended.shape[0] - 6
    rows_out = extended.shape[1] - 6
    total = jnp.zeros((cols_out, rows_out, extended.shape[2]), jnp.float32)
    for row_off in range(7):
        for col_off in range(7):
            piece = extended[row_off : row_off + cols_out, col_off : col_off + rows_out, :]
            total = total + piece * kernel[row_off * 7 + col_off]
    return total


def layer_norm(rows, gain):
    center = rows - jnp.mean(rows, axis=-1, keepdims=True)
    spread = jnp.mean(center * center, axis=-1, keepdims=True)
    return center * lax.rsqrt(spread + 1e-06) * gain


def pointwise(mixed_rows, gain, w_up, b_up, w_down, d_out):
    normed_f, norm_back = jax.vjp(layer_norm, mixed_rows, gain)
    normed = normed_f.astype(jnp.bfloat16)
    upper = jnp.dot(normed, w_up, preferred_element_type=jnp.float32) + b_up
    active_f, gelu_back = jax.vjp(lambda v: jax.nn.gelu(v, approximate=True), upper)
    active = active_f.astype(jnp.bfloat16)
    d_active = lax.dot_general(
        d_out, w_down, (((1,), (1,)), ((), ())), preferred_element_type=jnp.float32
    )
    d_upper = gelu_back(d_active)[0].astype(jnp.bfloat16)
    d_normed = lax.dot_general(
        d_upper, w_up, (((1,), (1,)), ((), ())), preferred_element_type=jnp.float32
    )
    d_mixed, d_gain = norm_back(d_normed)
    return (normed, active, d_upper, d_mixed, d_gain)


DEVICES = ("lon", "lat")


def send(value, mask):
    return lax.ppermute(value, DEVICES, [(i, i ^ mask) for i in range(256)])


def tree_sum(parts):
    while len(parts) > 1:
        parts = [parts[i] + parts[i + 1] for i in range(0, len(parts), 2)]
    return parts[0]


def scatter_stage(chunks, place, masks):
    narrow = chunks.astype(jnp.bfloat16)
    parts = [lax.dynamic_index_in_dim(chunks, place, 0, False)]
    for k, mask in enumerate(masks):
        piece = lax.dynamic_index_in_dim(narrow, place ^ (k + 1), 0, False)
        parts.append(send(piece, mask).astype(jnp.float32))
    return tree_sum(parts)


def whole_stage(value, masks):
    return tree_sum([value] + [send(value, mask) for mask in masks])


X_MASKS = (1, 2, 3)
Y_MASKS = (128, 4, 132)
Z_MASKS = (64, 32, 16)
CORE_MASK = 8


def mirror_tiles(value, half_turn):
    def branch(k):
        pairs = [(e * 8 + 7, ((2 * k - e) % 32) * 8 + 7) for e in range(32)]
        return lambda v: lax.ppermute(v, DEVICES, pairs)

    return lax.switch(half_turn, [branch(k) for k in range(16)], value)


def to_next(value):
    return lax.ppermute(value, "lon", [(i, (i + 1) % 32) for i in range(32)])


def to_previous(value):
    return lax.ppermute(value, "lon", [((i + 1) % 32, i) for i in range(32)])


def per_device(
    field, cotangent, land_sea, fold_partner, depth_kernel, norm_gain, w_up, b_up, w_down
):
    width_lon, width_lat, channels = field.shape
    lon_at = lax.axis_index("lon")
    lat_at = lax.axis_index("lat")
    core = lon_at % 2
    z_at = (lon_at // 2) % 8
    y_at = (lat_at // 4) * 2 + lon_at // 16
    x_at = lat_at % 4
    is_north = lat_at == lax.axis_size("lat") - 1
    north_scale = is_north.astype(jnp.float32)
    from_end = 511 - fold_partner[0]
    turn = 31 - from_end // 16
    shift = 16 - from_end % 16

    lat_ext = extended_2(field, (("lat", 1),), 3, False)
    top_rows = field[:, width_lat - 3 :, :]
    mine = mirror_tiles(top_rows, turn // 2)
    from_next = to_previous(mine)
    from_previous = to_next(mine)
    even = turn % 2 == 0
    low = jnp.where(even, from_next, mine)
    high = jnp.where(even, mine, from_previous)
    facing = lax.dynamic_slice_in_dim(jnp.concatenate([low, high], axis=0), shift, 16, axis=0)
    fold_band = facing[::-1, ::-1, :]
    upper_rim = jnp.where(is_north, fold_band, lat_ext[:, width_lat + 3 :, :])
    lat_ext = jnp.concatenate([lat_ext[:, : width_lat + 3, :], upper_rim], axis=1)
    extended = extended_2(lat_ext, (("lon", 0),), 3, True)
    mixed, conv_back = jax.vjp(conv_depth, extended.astype(jnp.float32), depth_kernel)
    tokens = width_lon * width_lat
    mixed_rows = mixed.reshape(tokens, channels)
    d_out = cotangent.reshape(tokens, channels) * land_sea.reshape(tokens, 1).astype(jnp.bfloat16)
    normed, active, d_upper, d_mixed, d_gain = pointwise(
        mixed_rows, norm_gain, w_up, b_up, w_down, d_out
    )
    grad_bias = jnp.sum(d_upper.astype(jnp.float32), axis=0)

    down = lax.dot_general(
        active, d_out, (((0,), (0,)), ((), ())), preferred_element_type=jnp.float32
    ).reshape(2, 8, 2, 2, 4, 8, 512)
    down = scatter_stage(down.transpose(2, 4, 3, 0, 1, 5, 6), core, (CORE_MASK,))
    up = lax.dot_general(
        normed, d_upper, (((0,), (0,)), ((), ())), preferred_element_type=jnp.float32
    ).reshape(2, 8, 2, 2, 4, 2, 2048)
    up = scatter_stage(up.transpose(2, 3, 0, 4, 1, 5, 6), core, (CORE_MASK,))
    down = scatter_stage(down, x_at, X_MASKS)
    up = scatter_stage(up.reshape(4, 4, 8, 2, 2048), y_at, Y_MASKS)
    down = scatter_stage(down.reshape(4, 8, 8, 512), y_at, Y_MASKS)
    up = scatter_stage(up, x_at, X_MASKS)
    both = jnp.concatenate([down.reshape(8, 8, 512), up.reshape(8, 8, 512)], axis=1)
    for bit, mask in zip((2, 1, 0), Z_MASKS):
        pair = both.reshape((2, both.shape[0] // 2) + both.shape[1:])
        both = scatter_stage(pair, (z_at >> bit) & 1, (mask,))
    both = both[0]
    grad_down = both[:8]
    grad_up = both[8:].reshape(2, 2048)

    grad_ext, grad_kernel = conv_back(d_mixed.reshape(width_lon, width_lat, channels))

    small = jnp.concatenate(
        [
            grad_kernel,
            d_gain.reshape(1, 512),
            grad_bias.reshape(4, 512),
            jnp.zeros((2, 512), jnp.float32),
        ],
        axis=0,
    ).reshape(2, 28, 512)
    half = lax.dynamic_index_in_dim(small, core, 0, False) + send(
        lax.dynamic_index_in_dim(small, 1 - core, 0, False), CORE_MASK
    )
    half = whole_stage(half, X_MASKS)
    half = whole_stage(half, Y_MASKS)
    for mask in Z_MASKS:
        half = whole_stage(half, (mask,))
    other = send(half, CORE_MASK)
    small = jnp.where(
        core == 0,
        jnp.concatenate([half, other], axis=0),
        jnp.concatenate([other, half], axis=0),
    )
    grad_kernel = small[:49]
    grad_gain = small[49]
    grad_bias = small[50:54].reshape(2048)

    lon_recv = extended_2(grad_ext.astype(jnp.bfloat16), (("lon", 0),), 3, True).astype(
        grad_ext.dtype
    )
    by_cols = grad_ext[3 : width_lon + 3]
    by_cols = by_cols.at[0:3].add(lon_recv[0:3])
    by_cols = by_cols.at[width_lon - 3 :].add(lon_recv[width_lon + 9 : width_lon + 12])
    fold_strip = by_cols[:, width_lat + 3 :, :] * north_scale
    lat_recv = extended_2(by_cols.astype(jnp.bfloat16), (("lat", 1),), 3, False).astype(
        by_cols.dtype
    )
    owned = by_cols[:, 3 : width_lat + 3, :]
    owned = owned.at[:, 0:3, :].add(lat_recv[:, 0:3, :])
    owned = owned.at[:, width_lat - 3 :, :].add(lat_recv[:, width_lat + 9 : width_lat + 12, :])
    spread = lax.dynamic_update_slice_in_dim(
        jnp.zeros((32, 3, channels), jnp.bfloat16),
        fold_strip[::-1, ::-1, :].astype(jnp.bfloat16),
        shift,
        axis=0,
    )
    none = jnp.zeros_like(spread[:16])
    mine = jnp.where(even, spread[16:], spread[:16])
    mine = mine + to_next(jnp.where(even, spread[:16], none))
    mine = mine + to_previous(jnp.where(even, none, spread[16:]))
    owned = owned.at[:, width_lat - 3 :, :].add(
        mirror_tiles(mine, turn // 2).astype(jnp.float32)
    )
    grad_field = (cotangent.astype(jnp.float32) + owned).astype(jnp.bfloat16)
    return (grad_field, grad_up, grad_down, grad_kernel, grad_gain, grad_bias)


def solution(mesh):
    placed = (
        P("lon", "lat", None),
        P("lon", "lat", None),
        P("lon", "lat"),
        P(),
        P(),
        P(),
        P(),
        P(),
        P(),
    )
    return jax.shard_map(
        per_device,
        mesh=mesh,
        in_specs=placed,
        out_specs=(
            P("lon", "lat", None),
            P(("lon", "lat"), None),
            P(("lon", "lat"), None),
            P(),
            P(),
            P(),
        ),
        check_vma=False,
    )
```

```python
import jax
import jax.numpy as jnp
from jax import lax
from jax.experimental import pallas as pl
from jax.experimental.pallas import tpu as pltpu
from jax.sharding import PartitionSpec as P


def extended_2(cells, sides, width, closed):
    for axis, dim in sides:
        count = lax.axis_size(axis)
        ends = count if closed else count - 1
        head = lax.slice_in_dim(cells, 0, width, axis=dim)
        tail = lax.slice_in_dim(cells, cells.shape[dim] - width, cells.shape[dim], axis=dim)
        cells = jnp.concatenate(
            [
                lax.ppermute(tail, axis, [(i, (i + 1) % count) for i in range(ends)]),
                cells,
                lax.ppermute(head, axis, [((i + 1) % count, i) for i in range(ends)]),
            ],
            axis=dim,
        )
    return cells


DEVICES = ("lon", "lat")


def send(value, mask):
    return lax.ppermute(value, DEVICES, [(i, i ^ mask) for i in range(256)])


def tree_sum(parts):
    while len(parts) > 1:
        parts = [parts[i] + parts[i + 1] for i in range(0, len(parts), 2)]
    return parts[0]


def scatter_stage(chunks, masks):
    parts = [chunks[0]]
    for k, mask in enumerate(masks):
        parts.append(send(chunks[k + 1].astype(jnp.bfloat16), mask).astype(jnp.float32))
    return tree_sum(parts)


def halving_stage(chunks, bit, mask):
    keep = lax.dynamic_index_in_dim(chunks, bit, 0, False)
    give = lax.dynamic_index_in_dim(chunks, 1 - bit, 0, False).astype(jnp.bfloat16)
    return keep + send(give, mask).astype(jnp.float32)


def whole_stage(value, masks):
    return tree_sum([value] + [send(value, mask) for mask in masks])


X_MASKS = (1, 2, 3)
Y_MASKS = (128, 4, 132)
Z_MASKS = (64, 32, 16)
CORE_MASK = 8


def mirror_tiles(value, half_turn):
    def branch(k):
        pairs = [(e * 8 + 7, ((2 * k - e) % 32) * 8 + 7) for e in range(32)]
        return lambda v: lax.ppermute(v, DEVICES, pairs)

    return lax.switch(half_turn, [branch(k) for k in range(16)], value)


def to_next(value):
    return lax.ppermute(value, "lon", [(i, (i + 1) % 32) for i in range(32)])


def to_previous(value):
    return lax.ppermute(value, "lon", [((i + 1) % 32, i) for i in range(32)])


ROOT_2_PI = 0.7978845608028654
CUBIC = 0.044715
F32 = jnp.float32
BF16 = jnp.bfloat16


def spread_rows(ext_ref, wide, shifted):
    wide[...] = ext_ref[...].astype(F32)
    for b in range(7):
        shifted[b] = wide[:, b : b + 16, :]


def forward_kernel(
    at_ref, ext_ref, kern_ref, gain_ref, w_up_ref, b_up_ref, d_out_ref, d_act_ref, order_ref,
    mixed_ref, d_upper_ref, bias_ref, keep_ref, send_ref,
    wide, shifted, normed, ordered, upper, active, tile,
):
    core, x_at, y_at = at_ref[0], at_ref[1], at_ref[2]
    spread_rows(ext_ref, wide, shifted)

    def conv_step(step, carry):
        lanes = pl.ds(pl.multiple_of((step // 2) * 128, 128), 128)
        first = (step % 2) * 8
        total = jnp.zeros((8, 16, 128), F32)
        for a in range(7):
            for b in range(7):
                weight = kern_ref[pl.ds(a * 7 + b, 1), lanes]
                total = total + shifted[b, pl.ds(first + a, 8), :, lanes] * weight.reshape(1, 1, 128)
        mixed_ref[pl.ds(pl.multiple_of(first * 16, 128), 128), lanes] = total.reshape(128, 128)
        return carry

    lax.fori_loop(0, 8, conv_step, 0)

    def norm_step(step, carry):
        rows = pl.ds(pl.multiple_of(step * 32, 32), 32)
        cells = mixed_ref[rows, :]
        center = cells - jnp.mean(cells, axis=-1, keepdims=True)
        spread = jnp.mean(center * center, axis=-1, keepdims=True)
        normed[rows, :] = (center * lax.rsqrt(spread + 1e-6) * gain_ref[...]).astype(BF16)
        return carry

    lax.fori_loop(0, 8, norm_step, 0)
    ordered[...] = jnp.dot(normed[...], order_ref[...], preferred_element_type=F32).astype(BF16)

    for t in range(4):
        lanes = slice(t * 512, t * 512 + 512)
        upper[...] = jnp.dot(normed[...], w_up_ref[:, lanes], preferred_element_type=F32)

        def gelu_step(step, bias):
            rows = pl.ds(pl.multiple_of(step * 32, 32), 32)
            u = upper[rows, :] + b_up_ref[:, lanes]
            square = u * u
            th = jnp.tanh(ROOT_2_PI * (u + CUBIC * (square * u)))
            half = 0.5 * (1.0 + th)
            active[rows, :] = (u * half).astype(BF16)
            slope = half + (0.5 * ROOT_2_PI) * u * (1.0 - th * th) * (1.0 + (3.0 * CUBIC) * square)
            d_up = (d_act_ref[rows, lanes] * slope).astype(BF16)
            d_upper_ref[rows, lanes] = d_up
            return bias + jnp.sum(d_up.astype(F32), axis=0, keepdims=True)

        bias_ref[t : t + 1, :] = lax.fori_loop(0, 8, gelu_step, jnp.zeros((1, 512), F32))
        tile[...] = lax.dot_general(
            active[...], d_out_ref[...], (((0,), (0,)), ((), ())), preferred_element_type=F32
        )
        for y_hi in range(2):
            k_y = (y_hi * 2 + t // 2) ^ y_at
            for k_x in range(4):
                base = y_hi * 32 + (k_x ^ x_at) * 8
                for mine in range(2):
                    at = base + ((1 - core) if mine == 0 else core) * 64
                    piece = jnp.concatenate(
                        [tile[pl.ds(pl.multiple_of(at + zz * 128, 8), 8), :] for zz in range(4)],
                        axis=0,
                    )
                    rows = pl.ds(pl.multiple_of(k_y * 64 + (t % 2) * 32, 32), 32)
                    if mine == 0:
                        send_ref[k_x, rows, :] = piece.astype(BF16)
                    else:
                        keep_ref[k_x, rows, :] = piece
        tile[...] = lax.dot_general(
            ordered[...], d_upper_ref[:, lanes], (((0,), (0,)), ((), ())),
            preferred_element_type=F32,
        )
        keep_ref[4 + t] = tile[:256, :]
        send_ref[4 + t] = tile[256:, :].astype(BF16)


def backward_kernel(
    ext_ref, mixed_ref, d_upper_ref, w_up_ref, gain_ref, kern_ref, bias_ref,
    small_ref, grad_ref, wide, shifted, d_normed, d_cells, moved,
):
    d_normed[...] = lax.dot_general(
        d_upper_ref[...], w_up_ref[...], (((1,), (1,)), ((), ())), preferred_element_type=F32
    )
    spread_rows(ext_ref, wide, shifted)

    def norm_step(step, gain_sum):
        rows = pl.ds(pl.multiple_of(step * 32, 32), 32)
        cells = mixed_ref[rows, :]
        center = cells - jnp.mean(cells, axis=-1, keepdims=True)
        spread = jnp.mean(center * center, axis=-1, keepdims=True)
        inverse = lax.rsqrt(spread + 1e-6)
        unit = center * inverse
        d = d_normed[rows, :]
        d_unit = d * gain_ref[...]
        along = jnp.mean(d_unit * unit, axis=-1, keepdims=True)
        d_center = (d_unit - unit * along) * inverse
        d_mixed = d_center - jnp.mean(d_center, axis=-1, keepdims=True)
        d_cells[pl.ds(step * 2, 2)] = d_mixed.reshape(2, 16, 512)
        return gain_sum + jnp.sum(d * unit, axis=0, keepdims=True)

    small_ref[49:50, :] = lax.fori_loop(0, 8, norm_step, jnp.zeros((1, 512), F32))
    small_ref[50:54, :] = bias_ref[0:4, :]
    small_ref[54:56, :] = jnp.zeros((2, 512), F32)
    moved[...] = jnp.zeros_like(moved)
    for b in range(7):
        moved[b, :, b : b + 16, :] = d_cells[...]

    def tap_step(step, carry):
        lanes = pl.ds(pl.multiple_of(step * 128, 128), 128)
        d = d_cells[:, :, lanes]
        for a in range(7):
            for b in range(7):
                product = shifted[b, a : a + 16, :, lanes] * d
                total = jnp.sum(product.reshape(32, 8, 128), axis=0)
                small_ref[a * 7 + b : a * 7 + b + 1, lanes] = jnp.sum(total, axis=0, keepdims=True)
        return carry

    lax.fori_loop(0, 4, tap_step, 0)

    def rim_step(step, carry):
        lanes = pl.ds(pl.multiple_of(step * 128, 128), 128)
        for start in range(0, 22, 4):
            group = range(start, min(start + 4, 22))
            totals = {i: jnp.zeros((24, 128), F32) for i in group}
            for a in range(7):
                used = [i for i in group if 0 <= i - a < 16]
                if not used:
                    continue
                for b in range(7):
                    weight = kern_ref[a * 7 + b : a * 7 + b + 1, lanes]
                    for i in used:
                        totals[i] = totals[i] + moved[b, i - a, :, lanes] * weight
            for i in group:
                grad_ref[i, :, lanes] = totals[i]
        return carry

    lax.fori_loop(0, 4, rim_step, 0)


VMEM_BYTES = 56 * 1024 * 1024


def run_forward(at, ext, kern, gain, w_up, b_up, d_out, d_act, order):
    shapes = [
        ((256, 512), F32), ((256, 2048), BF16), ((8, 512), F32),
        ((8, 256, 512), F32), ((8, 256, 512), BF16),
    ]
    return pl.pallas_call(
        forward_kernel,
        out_shape=[jax.ShapeDtypeStruct(s, d) for s, d in shapes],
        in_specs=[pl.BlockSpec(memory_space=pltpu.SMEM)]
        + [pl.BlockSpec(memory_space=pltpu.VMEM)] * 8,
        out_specs=[pl.BlockSpec(memory_space=pltpu.VMEM)] * 5,
        scratch_shapes=[
            pltpu.VMEM((22, 32, 512), F32), pltpu.VMEM((7, 22, 16, 512), F32),
            pltpu.VMEM((256, 512), BF16), pltpu.VMEM((256, 512), BF16),
            pltpu.VMEM((256, 512), F32), pltpu.VMEM((256, 512), BF16), pltpu.VMEM((512, 512), F32),
        ],
        compiler_params=pltpu.CompilerParams(vmem_limit_bytes=VMEM_BYTES),
        cost_estimate=pl.CostEstimate(
            flops=1700000000, bytes_accessed=16000000, transcendentals=600000
        ),
        name="forward",
    )(at, ext, kern, gain, w_up, b_up, d_out, d_act, order)


def run_backward(ext, mixed, d_upper, w_up, gain, kern, bias):
    return pl.pallas_call(
        backward_kernel,
        out_shape=[
            jax.ShapeDtypeStruct((56, 512), F32), jax.ShapeDtypeStruct((22, 24, 512), F32),
        ],
        in_specs=[pl.BlockSpec(memory_space=pltpu.VMEM)] * 7,
        out_specs=[pl.BlockSpec(memory_space=pltpu.VMEM)] * 2,
        scratch_shapes=[
            pltpu.VMEM((22, 32, 512), F32), pltpu.VMEM((7, 22, 16, 512), F32),
            pltpu.VMEM((256, 512), F32), pltpu.VMEM((16, 16, 512), F32),
            pltpu.VMEM((7, 16, 24, 512), F32),
        ],
        compiler_params=pltpu.CompilerParams(vmem_limit_bytes=VMEM_BYTES),
        cost_estimate=pl.CostEstimate(flops=560000000, bytes_accessed=8000000, transcendentals=300),
        name="backward",
    )(ext, mixed, d_upper, w_up, gain, kern, bias)


def per_device(
    field, cotangent, land_sea, fold_partner, depth_kernel, norm_gain, w_up, b_up, w_down
):
    width_lon, width_lat, channels = field.shape
    lon_at = lax.axis_index("lon")
    lat_at = lax.axis_index("lat")
    core = lon_at % 2
    z_at = (lon_at // 2) % 8
    y_at = (lat_at // 4) * 2 + lon_at // 16
    x_at = lat_at % 4
    is_north = lat_at == lax.axis_size("lat") - 1
    north_scale = is_north.astype(jnp.float32)
    from_end = 511 - fold_partner[0]
    turn = 31 - from_end // 16
    shift = 16 - from_end % 16

    lat_ext = extended_2(field, (("lat", 1),), 3, False)
    top_rows = field[:, width_lat - 3 :, :]
    mine = mirror_tiles(top_rows, turn // 2)
    from_next = to_previous(mine)
    from_previous = to_next(mine)
    even = turn % 2 == 0
    low = jnp.where(even, from_next, mine)
    high = jnp.where(even, mine, from_previous)
    facing = lax.dynamic_slice_in_dim(jnp.concatenate([low, high], axis=0), shift, 16, axis=0)
    fold_band = facing[::-1, ::-1, :]
    upper_rim = jnp.where(is_north, fold_band, lat_ext[:, width_lat + 3 :, :])
    lat_ext = jnp.concatenate([lat_ext[:, : width_lat + 3, :], upper_rim], axis=1)
    extended = extended_2(lat_ext, (("lon", 0),), 3, True)
    extended = jnp.pad(extended, ((0, 0), (0, 10), (0, 0)))
    tokens = width_lon * width_lat
    d_out = cotangent.reshape(tokens, channels) * land_sea.reshape(tokens, 1).astype(jnp.bfloat16)
    d_act = lax.dot_general(
        d_out, w_down, (((1,), (1,)), ((), ())), preferred_element_type=jnp.float32
    )
    row = jnp.arange(512, dtype=jnp.int32)
    block = row // 2
    y_of = ((block // 4) % 2) * 2 + block // 128
    goes_to = (
        ((block // 8) % 2 ^ core) * 256
        + (y_of ^ y_at) * 64
        + (block % 4 ^ x_at) * 16
        + (block // 16) % 8 * 2
        + row % 2
    )
    order = (goes_to[:, None] == row[None, :]).astype(jnp.bfloat16)
    at = jnp.stack([core, x_at, y_at]).astype(jnp.int32)
    gain = norm_gain.reshape(1, channels)
    mixed, d_upper, bias, keep, give = run_forward(
        at, extended, depth_kernel, gain, w_up, b_up.reshape(1, 2048), d_out, d_act, order
    )

    given = send(give, CORE_MASK)
    given, mixed = lax.optimization_barrier((given, mixed))
    both = keep + given.astype(jnp.float32)
    down = [both[k].reshape(4, 64, 512) for k in range(4)]
    up = [both[4:, k * 64 : k * 64 + 64].reshape(4, 4, 16, 512) for k in range(4)]
    down = scatter_stage(down, X_MASKS)
    up = scatter_stage(up, Y_MASKS)
    down = scatter_stage([down[k] for k in range(4)], Y_MASKS)
    up = scatter_stage([up[:, k] for k in range(4)], X_MASKS)
    up = up.reshape(4, 8, 2, 512).transpose(1, 2, 0, 3).reshape(8, 8, 512)
    both = jnp.concatenate([down.reshape(8, 8, 512), up], axis=1)
    for bit, mask in zip((2, 1, 0), Z_MASKS):
        pair = both.reshape((2, both.shape[0] // 2) + both.shape[1:])
        both = halving_stage(pair, (z_at >> bit) & 1, mask)
    grad_down = both[0, :8]
    grad_up = both[0, 8:].reshape(2, 2048)

    small, grad_ext = run_backward(
        extended, mixed, d_upper, w_up, gain, depth_kernel, bias
    )
    grad_ext = grad_ext[:, : width_lat + 6]

    small = small.reshape(2, 28, 512)
    half = lax.dynamic_index_in_dim(small, core, 0, False) + send(
        lax.dynamic_index_in_dim(small, 1 - core, 0, False), CORE_MASK
    )
    half = whole_stage(half, X_MASKS)
    half = whole_stage(half, Y_MASKS)
    for mask in Z_MASKS:
        half = whole_stage(half, (mask,))
    other = send(half, CORE_MASK)
    small = jnp.where(
        core == 0,
        jnp.concatenate([half, other], axis=0),
        jnp.concatenate([other, half], axis=0),
    )
    grad_kernel = small[:49]
    grad_gain = small[49]
    grad_bias = small[50:54].reshape(2048)

    lon_recv = extended_2(grad_ext.astype(jnp.bfloat16), (("lon", 0),), 3, True).astype(
        grad_ext.dtype
    )
    by_cols = grad_ext[3 : width_lon + 3]
    by_cols = by_cols.at[0:3].add(lon_recv[0:3])
    by_cols = by_cols.at[width_lon - 3 :].add(lon_recv[width_lon + 9 : width_lon + 12])
    fold_strip = by_cols[:, width_lat + 3 :, :] * north_scale
    lat_recv = extended_2(by_cols.astype(jnp.bfloat16), (("lat", 1),), 3, False).astype(
        by_cols.dtype
    )
    owned = by_cols[:, 3 : width_lat + 3, :]
    owned = owned.at[:, 0:3, :].add(lat_recv[:, 0:3, :])
    owned = owned.at[:, width_lat - 3 :, :].add(lat_recv[:, width_lat + 9 : width_lat + 12, :])
    spread = lax.dynamic_update_slice_in_dim(
        jnp.zeros((32, 3, channels), jnp.bfloat16),
        fold_strip[::-1, ::-1, :].astype(jnp.bfloat16),
        shift,
        axis=0,
    )
    none = jnp.zeros_like(spread[:16])
    mine = jnp.where(even, spread[16:], spread[:16])
    mine = mine + to_next(jnp.where(even, spread[:16], none))
    mine = mine + to_previous(jnp.where(even, none, spread[16:]))
    owned = owned.at[:, width_lat - 3 :, :].add(
        mirror_tiles(mine, turn // 2).astype(jnp.float32)
    )
    grad_field = (cotangent.astype(jnp.float32) + owned).astype(jnp.bfloat16)
    return (grad_field, grad_up, grad_down, grad_kernel, grad_gain, grad_bias)


def solution(mesh):
    placed = (
        P("lon", "lat", None),
        P("lon", "lat", None),
        P("lon", "lat"),
        P(),
        P(),
        P(),
        P(),
        P(),
        P(),
    )
    return jax.shard_map(
        per_device,
        mesh=mesh,
        in_specs=placed,
        out_specs=(
            P("lon", "lat", None),
            P(("lon", "lat"), None),
            P(("lon", "lat"), None),
            P(),
            P(),
            P(),
        ),
        check_vma=False,
    )
```

```python
import jax
import jax.numpy as jnp
from jax import lax
from jax.experimental import pallas as pl
from jax.experimental.pallas import tpu as pltpu
from jax.sharding import PartitionSpec as P


def extended_2(cells, sides, width, closed):
    for axis, dim in sides:
        count = lax.axis_size(axis)
        ends = count if closed else count - 1
        head = lax.slice_in_dim(cells, 0, width, axis=dim)
        tail = lax.slice_in_dim(cells, cells.shape[dim] - width, cells.shape[dim], axis=dim)
        cells = jnp.concatenate(
            [
                lax.ppermute(tail, axis, [(i, (i + 1) % count) for i in range(ends)]),
                cells,
                lax.ppermute(head, axis, [((i + 1) % count, i) for i in range(ends)]),
            ],
            axis=dim,
        )
    return cells


DEVICES = ("lon", "lat")


def send(value, mask):
    return lax.ppermute(value, DEVICES, [(i, i ^ mask) for i in range(256)])


def tree_sum(parts):
    while len(parts) > 1:
        parts = [parts[i] + parts[i + 1] for i in range(0, len(parts), 2)]
    return parts[0]


def whole_stage(value, masks):
    return tree_sum([value] + [send(value, mask) for mask in masks])


X_MASKS = (1, 2, 3)
Y_MASKS = (128, 4, 132)
Z_MASKS = (16, 32, 48, 64)
CORE_MASK = 8


def mirror_tiles(value, half_turn):
    def branch(k):
        pairs = [(e * 8 + 7, ((2 * k - e) % 32) * 8 + 7) for e in range(32)]
        return lambda v: lax.ppermute(v, DEVICES, pairs)

    return lax.switch(half_turn, [branch(k) for k in range(16)], value)


def to_next(value):
    return lax.ppermute(value, "lon", [(i, (i + 1) % 32) for i in range(32)])


def to_previous(value):
    return lax.ppermute(value, "lon", [((i + 1) % 32, i) for i in range(32)])


ROOT_2_PI = 0.7978845608028654
CUBIC = 0.044715
F32 = jnp.float32
BF16 = jnp.bfloat16


def spread_rows(ext_ref, wide, shifted):
    wide[...] = ext_ref[...].astype(F32)
    for b in range(7):
        shifted[b] = wide[:, b : b + 16, :]


def forward_kernel(
    at_ref, ext_ref, kern_ref, gain_ref, w_up_ref, b_up_ref, d_out_ref, d_act_ref, order_ref,
    mixed_ref, d_upper_ref, bias_ref, keep_ref, send_ref,
    wide, shifted, normed, ordered, upper, active, tile,
):
    core, x_at, y_at = at_ref[0], at_ref[1], at_ref[2]
    spread_rows(ext_ref, wide, shifted)

    def conv_step(step, carry):
        lanes = pl.ds(pl.multiple_of(step * 128, 128), 128)
        totals = [jnp.zeros((16, 128), F32)] * 16
        for b in range(7):
            weights = [kern_ref[a * 7 + b : a * 7 + b + 1, lanes] for a in range(7)]
            for r in range(22):
                cells = shifted[b, r, :, lanes]
                for a in range(max(0, r - 15), min(7, r + 1)):
                    totals[r - a] = totals[r - a] + cells * weights[a]
        for x in range(16):
            mixed_ref[x * 16 : x * 16 + 16, lanes] = totals[x]
        return carry

    lax.fori_loop(0, 4, conv_step, 0)

    def norm_step(step, carry):
        rows = pl.ds(pl.multiple_of(step * 32, 32), 32)
        cells = mixed_ref[rows, :]
        center = cells - jnp.mean(cells, axis=-1, keepdims=True)
        spread = jnp.mean(center * center, axis=-1, keepdims=True)
        normed[rows, :] = (center * lax.rsqrt(spread + 1e-6) * gain_ref[...]).astype(BF16)
        return carry

    lax.fori_loop(0, 8, norm_step, 0)
    ordered[...] = jnp.dot(normed[...], order_ref[...], preferred_element_type=F32).astype(BF16)

    for t in range(4):
        lanes = slice(t * 512, t * 512 + 512)
        upper[...] = jnp.dot(normed[...], w_up_ref[:, lanes], preferred_element_type=F32)

        def gelu_step(step, bias):
            rows = pl.ds(pl.multiple_of(step * 32, 32), 32)
            u = upper[rows, :] + b_up_ref[:, lanes]
            square = u * u
            th = jnp.tanh(ROOT_2_PI * (u + CUBIC * (square * u)))
            half = 0.5 * (1.0 + th)
            active[rows, :] = (u * half).astype(BF16)
            slope = half + (0.5 * ROOT_2_PI) * u * (1.0 - th * th) * (1.0 + (3.0 * CUBIC) * square)
            d_up = (d_act_ref[rows, lanes] * slope).astype(BF16)
            d_upper_ref[rows, lanes] = d_up
            return bias + jnp.sum(d_up.astype(F32), axis=0, keepdims=True)

        bias_ref[t : t + 1, :] = lax.fori_loop(0, 8, gelu_step, jnp.zeros((1, 512), F32))
        tile[...] = lax.dot_general(
            active[...], d_out_ref[...], (((0,), (0,)), ((), ())), preferred_element_type=F32
        )
        for y_hi in range(2):
            k_y = (y_hi * 2 + t // 2) ^ y_at
            for k_x in range(4):
                base = y_hi * 32 + (k_x ^ x_at) * 8
                for mine in range(2):
                    at = base + ((1 - core) if mine == 0 else core) * 64
                    piece = jnp.concatenate(
                        [tile[pl.ds(pl.multiple_of(at + zz * 128, 8), 8), :] for zz in range(4)],
                        axis=0,
                    )
                    rows = pl.ds(pl.multiple_of(k_y * 64 + (t % 2) * 32, 32), 32)
                    if mine == 0:
                        send_ref[k_x, rows, :] = piece.astype(BF16)
                    else:
                        keep_ref[k_x, rows, :] = piece
        tile[...] = lax.dot_general(
            ordered[...], d_upper_ref[:, lanes], (((0,), (0,)), ((), ())),
            preferred_element_type=F32,
        )
        rows = slice(256 + t * 64, 320 + t * 64)
        for k_x in range(4):
            keep_ref[k_x, rows, :] = tile[k_x * 64 : k_x * 64 + 64, :]
            send_ref[k_x, rows, :] = tile[256 + k_x * 64 : 320 + k_x * 64, :].astype(BF16)


def backward_kernel(
    ext_ref, mixed_ref, d_upper_ref, w_up_ref, gain_ref, kern_ref, bias_ref,
    small_ref, grad_ref, west_ref, east_ref, wide, shifted, d_normed, d_cells, moved,
):
    d_normed[...] = lax.dot_general(
        d_upper_ref[...], w_up_ref[...], (((1,), (1,)), ((), ())), preferred_element_type=F32
    )
    spread_rows(ext_ref, wide, shifted)

    def norm_step(step, gain_sum):
        rows = pl.ds(pl.multiple_of(step * 32, 32), 32)
        cells = mixed_ref[rows, :]
        center = cells - jnp.mean(cells, axis=-1, keepdims=True)
        spread = jnp.mean(center * center, axis=-1, keepdims=True)
        inverse = lax.rsqrt(spread + 1e-6)
        unit = center * inverse
        d = d_normed[rows, :]
        d_unit = d * gain_ref[...]
        along = jnp.mean(d_unit * unit, axis=-1, keepdims=True)
        d_center = (d_unit - unit * along) * inverse
        d_mixed = d_center - jnp.mean(d_center, axis=-1, keepdims=True)
        d_cells[pl.ds(step * 2, 2)] = d_mixed.reshape(2, 16, 512)
        return gain_sum + jnp.sum(d * unit, axis=0, keepdims=True)

    small_ref[49:50, :] = lax.fori_loop(0, 8, norm_step, jnp.zeros((1, 512), F32))
    small_ref[50:54, :] = bias_ref[0:4, :]
    small_ref[54:64, :] = jnp.zeros((10, 512), F32)
    moved[...] = jnp.zeros_like(moved)
    for b in range(7):
        moved[b, :, b : b + 16, :] = d_cells[...]

    def tap_step(step, carry):
        lanes = pl.ds(pl.multiple_of(step * 128, 128), 128)
        d = [d_cells[x, :, lanes] for x in range(16)]
        for b in range(7):
            totals = [jnp.zeros((8, 128), F32)] * 7
            for r in range(22):
                cells = shifted[b, r, :, lanes]
                for a in range(max(0, r - 15), min(7, r + 1)):
                    product = cells * d[r - a]
                    totals[a] = totals[a] + product[:8] + product[8:]
            for a in range(7):
                row = a * 7 + b
                small_ref[row : row + 1, lanes] = jnp.sum(totals[a], axis=0, keepdims=True)
        return carry

    lax.fori_loop(0, 4, tap_step, 0)

    def rim_step(step, carry):
        lanes = pl.ds(pl.multiple_of(step * 128, 128), 128)
        for q in range(3):
            rows = slice(q * 8, q * 8 + 8)
            totals = [jnp.zeros((8, 128), F32)] * 22
            for b in range(1 if q == 2 else 0, 7):
                weights = [kern_ref[a * 7 + b : a * 7 + b + 1, lanes] for a in range(7)]
                for x in range(16):
                    cells = moved[b, x, rows, lanes]
                    for a in range(7):
                        totals[x + a] = totals[x + a] + cells * weights[a]
            for i in range(22):
                grad_ref[i, rows, lanes] = totals[i]
        return carry

    lax.fori_loop(0, 4, rim_step, 0)
    filler = jnp.zeros((3, 8, 512), F32)
    west_ref[...] = jnp.concatenate([grad_ref[0:3], filler], axis=1).astype(BF16)
    east_ref[...] = jnp.concatenate([grad_ref[19:22], filler], axis=1).astype(BF16)


VMEM_BYTES = 30 * 1024 * 1024


def run_forward(at, ext, kern, gain, w_up, b_up, d_out, d_act, order):
    shapes = [
        ((256, 512), F32), ((256, 2048), BF16), ((8, 512), F32),
        ((4, 512, 512), F32), ((4, 512, 512), BF16),
    ]
    return pl.pallas_call(
        forward_kernel,
        out_shape=[jax.ShapeDtypeStruct(s, d) for s, d in shapes],
        in_specs=[pl.BlockSpec(memory_space=pltpu.SMEM)]
        + [pl.BlockSpec(memory_space=pltpu.VMEM)] * 8,
        out_specs=[pl.BlockSpec(memory_space=pltpu.VMEM)] * 5,
        scratch_shapes=[
            pltpu.VMEM((22, 32, 512), F32), pltpu.VMEM((7, 22, 16, 512), F32),
            pltpu.VMEM((256, 512), BF16), pltpu.VMEM((256, 512), BF16),
            pltpu.VMEM((256, 512), F32), pltpu.VMEM((256, 512), BF16), pltpu.VMEM((512, 512), F32),
        ],
        compiler_params=pltpu.CompilerParams(vmem_limit_bytes=VMEM_BYTES),
        cost_estimate=pl.CostEstimate(
            flops=14000000000, bytes_accessed=16000000, transcendentals=600000
        ),
        name="forward",
    )(at, ext, kern, gain, w_up, b_up, d_out, d_act, order)


def run_backward(ext, mixed, d_upper, w_up, gain, kern, bias):
    return pl.pallas_call(
        backward_kernel,
        out_shape=[
            jax.ShapeDtypeStruct((64, 512), F32), jax.ShapeDtypeStruct((22, 24, 512), F32),
            jax.ShapeDtypeStruct((3, 32, 512), BF16), jax.ShapeDtypeStruct((3, 32, 512), BF16),
        ],
        in_specs=[pl.BlockSpec(memory_space=pltpu.VMEM)] * 7,
        out_specs=[pl.BlockSpec(memory_space=pltpu.VMEM)] * 4,
        scratch_shapes=[
            pltpu.VMEM((22, 32, 512), F32), pltpu.VMEM((7, 22, 16, 512), F32),
            pltpu.VMEM((256, 512), F32), pltpu.VMEM((16, 16, 512), F32),
            pltpu.VMEM((7, 16, 24, 512), F32),
        ],
        compiler_params=pltpu.CompilerParams(vmem_limit_bytes=VMEM_BYTES),
        cost_estimate=pl.CostEstimate(flops=12000000000, bytes_accessed=8000000, transcendentals=300),
        name="backward",
    )(ext, mixed, d_upper, w_up, gain, kern, bias)


def first_sum_kernel(keep_ref, given_ref, own_ref, *give_refs):
    own_ref[...] = keep_ref[0] + given_ref[0].astype(F32)
    for k in range(3):
        give_refs[k][...] = (keep_ref[k + 1] + given_ref[k + 1].astype(F32)).astype(BF16)


def second_sum_kernel(own_ref, a_ref, b_ref, c_ref, half_ref, half_a, half_b, half_c, *outs):
    large_ref, terms_ref = outs[:2]
    half = (half_ref[...] + half_a[...]) + (half_b[...] + half_c[...])
    high = half.astype(BF16)
    low = (half - high.astype(F32)).astype(BF16)
    terms_ref[...] = high.astype(F32) + low.astype(F32)

    def total(rows):
        return (own_ref[rows, :] + a_ref[rows, :].astype(F32)) + (
            b_ref[rows, :].astype(F32) + c_ref[rows, :].astype(F32)
        )

    for k in range(4):
        pieces = [(slice(0, 64), slice(k * 64, k * 64 + 64))]
        for t in range(4):
            at = 256 + t * 64 + k * 16
            pieces.append((slice(64 + t * 16, 80 + t * 16), slice(at, at + 16)))
        for target, rows in pieces:
            if k == 0:
                large_ref[target, :] = total(rows)
            else:
                outs[1 + k][target, :] = total(rows).astype(BF16)
        if k:
            outs[1 + k][128:160, :] = high
            outs[1 + k][160:192, :] = low


def third_sum_kernel(at_ref, large_ref, terms_ref, a_ref, b_ref, c_ref, *outs):
    own_ref, half_ref, blocks = outs[0], outs[1], outs[5]
    low = at_ref[3] & 3

    def total(rows):
        return (large_ref[rows, :] + a_ref[rows, :].astype(F32)) + (
            b_ref[rows, :].astype(F32) + c_ref[rows, :].astype(F32)
        )

    def term(ref):
        return ref[128:160, :].astype(F32) + ref[160:192, :].astype(F32)

    half = (terms_ref[...] + term(a_ref)) + (term(b_ref) + term(c_ref))
    half_ref[...] = half
    down = total(slice(0, 64))
    up = total(slice(64, 128))
    for z in range(8):
        rows = [up[t * 16 + z * 2 : t * 16 + z * 2 + 2] for t in range(4)]
        blocks[z] = jnp.concatenate([down[z * 8 : z * 8 + 8]] + rows, axis=0)
    for k in range(4):
        for z_high in range(2):
            block = blocks[z_high * 4 + (low ^ k)]
            (own_ref if k == 0 else outs[1 + k])[z_high * 16 : z_high * 16 + 16, :] = block
        if k:
            outs[1 + k][32:64, :] = half


def fourth_sum_kernel(at_ref, own_ref, half_ref, a_ref, b_ref, c_ref, keep_ref, sum_ref, give_ref):
    high = at_ref[3] >> 2

    def total(rows):
        return (own_ref[rows, :] + a_ref[rows, :]) + (b_ref[rows, :] + c_ref[rows, :])

    rest = slice(32, 64)
    half = (half_ref[...] + a_ref[rest, :]) + (b_ref[rest, :] + c_ref[rest, :])
    keep_ref[...] = total(pl.ds(pl.multiple_of(high * 16, 16), 16))
    give_ref[0:16, :] = total(pl.ds(pl.multiple_of((1 - high) * 16, 16), 16))
    give_ref[16:48, :] = half
    sum_ref[...] = half


def last_sum_kernel(keep_ref, half_ref, got_ref, down_ref, up_ref, sum_ref):
    sum_ref[...] = half_ref[...] + got_ref[16:48, :]
    down_ref[...] = keep_ref[0:8, :] + got_ref[0:8, :]
    up = keep_ref[8:16, :] + got_ref[8:16, :]
    for t in range(4):
        up_ref[:, t * 512 : t * 512 + 512] = up[t * 2 : t * 2 + 2]


def local_call(kernel, shapes, operands, name, scalars=0, scratch=()):
    return pl.pallas_call(
        kernel,
        out_shape=[jax.ShapeDtypeStruct(s, d) for s, d in shapes],
        in_specs=[pl.BlockSpec(memory_space=pltpu.SMEM)] * scalars
        + [pl.BlockSpec(memory_space=pltpu.VMEM)] * (len(operands) - scalars),
        out_specs=[pl.BlockSpec(memory_space=pltpu.VMEM)] * len(shapes),
        scratch_shapes=list(scratch),
        compiler_params=pltpu.CompilerParams(vmem_limit_bytes=VMEM_BYTES),
        cost_estimate=pl.CostEstimate(flops=800000000, bytes_accessed=2000000, transcendentals=0),
        name=name,
    )(*operands)


def per_device(
    field, cotangent, land_sea, fold_partner, depth_kernel, norm_gain, w_up, b_up, w_down
):
    width_lon, width_lat, channels = field.shape
    lon_at = lax.axis_index("lon")
    lat_at = lax.axis_index("lat")
    core = lon_at % 2
    z_at = (lon_at // 2) % 8
    y_at = (lat_at // 4) * 2 + lon_at // 16
    x_at = lat_at % 4
    is_north = lat_at == lax.axis_size("lat") - 1
    from_end = 511 - fold_partner[0]
    turn = 31 - from_end // 16
    shift = 16 - from_end % 16

    lat_ext = extended_2(field, (("lat", 1),), 3, False)
    top_rows = field[:, width_lat - 3 :, :]
    mine = mirror_tiles(top_rows, turn // 2)
    from_next = to_previous(mine)
    from_previous = to_next(mine)
    even = turn % 2 == 0
    low = jnp.where(even, from_next, mine)
    high = jnp.where(even, mine, from_previous)
    facing = lax.dynamic_slice_in_dim(jnp.concatenate([low, high], axis=0), shift, 16, axis=0)
    fold_band = facing[::-1, ::-1, :]
    upper_rim = jnp.where(is_north, fold_band, lat_ext[:, width_lat + 3 :, :])
    lat_ext = jnp.concatenate([lat_ext[:, : width_lat + 3, :], upper_rim], axis=1)
    extended = extended_2(lat_ext, (("lon", 0),), 3, True)
    extended = jnp.pad(extended, ((0, 0), (0, 10), (0, 0)))
    tokens = width_lon * width_lat
    d_out = cotangent.reshape(tokens, channels) * land_sea.reshape(tokens, 1).astype(jnp.bfloat16)
    d_act = lax.dot_general(
        d_out, w_down, (((1,), (1,)), ((), ())), preferred_element_type=jnp.float32
    )
    row = jnp.arange(512, dtype=jnp.int32)
    block = row >> 1
    y_of = (((block >> 2) & 1) << 1) + (block >> 7)
    goes_to = (
        (((block >> 3) & 1) ^ core) * 256
        + ((block & 3) ^ x_at) * 64
        + (y_of ^ y_at) * 16
        + ((block >> 4) & 7) * 2
        + (row & 1)
    )
    order = (goes_to[:, None] == row[None, :]).astype(jnp.bfloat16)
    at = jnp.stack([core, x_at, y_at, z_at]).astype(jnp.int32)
    gain = norm_gain.reshape(1, channels)
    mixed, d_upper, bias, keep, give = run_forward(
        at, extended, depth_kernel, gain, w_up, b_up.reshape(1, 2048), d_out, d_act, order
    )

    given = send(give, CORE_MASK)
    own, *give = local_call(
        first_sum_kernel, [((512, 512), F32)] + [((512, 512), BF16)] * 3, [keep, given], "first_sum"
    )
    own, give, mixed = lax.optimization_barrier((own, give, mixed))
    taken = [send(piece, mask) for piece, mask in zip(give, X_MASKS)]

    small, grad_ext, west_rim, east_rim = run_backward(
        extended, mixed, d_upper, w_up, gain, depth_kernel, bias
    )

    small = small.reshape(2, 32, 512)
    half = lax.dynamic_index_in_dim(small, core, 0, False) + send(
        lax.dynamic_index_in_dim(small, 1 - core, 0, False), CORE_MASK
    )
    half, taken = lax.optimization_barrier((half, taken))
    halves = [half] + [send(half, mask) for mask in X_MASKS]

    rim = jnp.bfloat16
    from_west = to_next(east_rim)[:, :22].astype(jnp.float32)
    from_east = to_previous(west_rim)[:, :22].astype(jnp.float32)
    by_cols = (
        grad_ext[3:19, :22]
        + jnp.pad(from_west, ((0, 13), (0, 0), (0, 0)))
        + jnp.pad(from_east, ((13, 0), (0, 0), (0, 0)))
    )

    top_rim = by_cols[:, 19:22].astype(rim)
    from_south = lax.ppermute(top_rim, "lat", [(i, i + 1) for i in range(7)])
    from_north = lax.ppermute(by_cols[:, 0:3].astype(rim), "lat", [(i + 1, i) for i in range(7)])
    fold_strip = jnp.where(is_north, top_rim, jnp.zeros_like(top_rim))
    spread = lax.dynamic_update_slice_in_dim(
        jnp.zeros((32, 3, channels), rim), fold_strip[::-1, ::-1, :], shift, axis=0
    )
    none = jnp.zeros_like(spread[:16])
    mine = jnp.where(even, spread[16:], spread[:16])
    mine = mine + to_next(jnp.where(even, spread[:16], none))
    mine = mine + to_previous(jnp.where(even, none, spread[16:]))
    from_fold = mirror_tiles(mine, turn >> 1)

    large, terms, *give = local_call(
        second_sum_kernel,
        [((128, 512), F32), ((32, 512), F32)] + [((192, 512), BF16)] * 3,
        [own, *taken, *halves],
        "second_sum",
    )
    taken = [send(piece, mask) for piece, mask in zip(give, Y_MASKS)]

    own, half, *give = local_call(
        third_sum_kernel,
        [((32, 512), F32), ((32, 512), F32)] + [((64, 512), F32)] * 3,
        [at, large, terms, *taken],
        "third_sum",
        scalars=1,
        scratch=[pltpu.VMEM((8, 16, 512), F32)],
    )
    taken = [send(piece, mask) for piece, mask in zip(give, Z_MASKS[:3])]
    keep, half, give = local_call(
        fourth_sum_kernel,
        [((16, 512), F32), ((32, 512), F32), ((48, 512), F32)],
        [at, own, half, *taken],
        "fourth_sum",
        scalars=1,
    )
    grad_down, grad_up, half = local_call(
        last_sum_kernel,
        [((8, 512), F32), ((2, 2048), F32), ((32, 512), F32)],
        [keep, half, send(give, Z_MASKS[3])],
        "last_sum",
    )
    other = send(half, CORE_MASK)
    small = jnp.where(
        core == 0,
        jnp.concatenate([half, other], axis=0),
        jnp.concatenate([other, half], axis=0),
    )
    grad_kernel = small[:49]
    grad_gain = small[49]
    grad_bias = small[50:54].reshape(2048)

    from_south = jnp.pad(from_south, ((0, 0), (0, 13), (0, 0)))
    from_north = jnp.pad(from_north, ((0, 0), (13, 0), (0, 0)))
    from_fold = jnp.pad(from_fold, ((0, 0), (13, 0), (0, 0)))
    owned = by_cols[:, 3:19] + from_south.astype(jnp.float32) + from_north.astype(jnp.float32)
    owned = owned + from_fold.astype(jnp.float32)
    grad_field = (cotangent.astype(jnp.float32) + owned).astype(jnp.bfloat16)
    return (grad_field, grad_up, grad_down, grad_kernel, grad_gain, grad_bias)


def solution(mesh):
    placed = (
        P("lon", "lat", None),
        P("lon", "lat", None),
        P("lon", "lat"),
        P(),
        P(),
        P(),
        P(),
        P(),
        P(),
    )
    return jax.shard_map(
        per_device,
        mesh=mesh,
        in_specs=placed,
        out_specs=(
            P("lon", "lat", None),
            P(("lon", "lat"), None),
            P(("lon", "lat"), None),
            P(),
            P(),
            P(),
        ),
        check_vma=False,
    )
```

```python
import jax
import jax.numpy as jnp
from jax import lax
from jax.experimental import pallas as pl
from jax.experimental.pallas import tpu as pltpu
from jax.sharding import PartitionSpec as P


def extended_2(cells, sides, width, closed):
    for axis, dim in sides:
        count = lax.axis_size(axis)
        ends = count if closed else count - 1
        head = lax.slice_in_dim(cells, 0, width, axis=dim)
        tail = lax.slice_in_dim(cells, cells.shape[dim] - width, cells.shape[dim], axis=dim)
        cells = jnp.concatenate(
            [
                lax.ppermute(tail, axis, [(i, (i + 1) % count) for i in range(ends)]),
                cells,
                lax.ppermute(head, axis, [((i + 1) % count, i) for i in range(ends)]),
            ],
            axis=dim,
        )
    return cells


DEVICES = ("lon", "lat")


def send(value, mask):
    return lax.ppermute(value, DEVICES, [(i, i ^ mask) for i in range(256)])


def tree_sum(parts):
    while len(parts) > 1:
        parts = [parts[i] + parts[i + 1] for i in range(0, len(parts), 2)]
    return parts[0]


def whole_stage(value, masks):
    return tree_sum([value] + [send(value, mask) for mask in masks])


X_MASKS = (1, 2, 3)
Y_MASKS = (128, 4, 132)
Z_MASKS = (16, 32, 48, 64)
CORE_MASK = 8


def mirror_tiles(value, half_turn):
    def branch(k):
        pairs = [(e * 8 + 7, ((2 * k - e) % 32) * 8 + 7) for e in range(32)]
        return lambda v: lax.ppermute(v, DEVICES, pairs)

    return lax.switch(half_turn, [branch(k) for k in range(16)], value)


def to_next(value):
    return lax.ppermute(value, "lon", [(i, (i + 1) % 32) for i in range(32)])


def to_previous(value):
    return lax.ppermute(value, "lon", [((i + 1) % 32, i) for i in range(32)])


ROOT_2_PI = 0.7978845608028654
CUBIC = 0.044715
F32 = jnp.float32
BF16 = jnp.bfloat16


def spread_rows(ext_ref, wide, shifted):
    wide[...] = ext_ref[...].astype(F32)
    for b in range(7):
        shifted[b] = wide[:, b : b + 16, :]


def forward_kernel(
    at_ref, ext_ref, kern_ref, gain_ref, b_up_ref, d_out_ref, order_hbm, w_up_hbm, d_act_hbm,
    mixed_hbm, d_upper_hbm, bias_ref, own_hbm, keep_hbm, send_hbm,
    wide, shifted, normed, ordered, upper, active, tile, mixed_ref, order_ref, w_up_ref, d_act_ref,
    d_upper_ref, own, keep, give, sems,
):
    core, x_at, y_at = at_ref[0], at_ref[1], at_ref[2]
    loads = [
        pltpu.make_async_copy(order_hbm, order_ref, sems.at[0]),
        pltpu.make_async_copy(w_up_hbm, w_up_ref, sems.at[1]),
        pltpu.make_async_copy(d_act_hbm, d_act_ref, sems.at[2]),
    ]
    for load in loads:
        load.start()
    spread_rows(ext_ref, wide, shifted)

    def conv_step(step, carry):
        lanes = pl.ds(pl.multiple_of(step * 128, 128), 128)
        totals = [jnp.zeros((16, 128), F32)] * 16
        for b in range(7):
            weights = [kern_ref[a * 7 + b : a * 7 + b + 1, lanes] for a in range(7)]
            for r in range(22):
                cells = shifted[b, r, :, lanes]
                for a in range(max(0, r - 15), min(7, r + 1)):
                    totals[r - a] = totals[r - a] + cells * weights[a]
        for x in range(16):
            mixed_ref[x * 16 : x * 16 + 16, lanes] = totals[x]
        return carry

    lax.fori_loop(0, 4, conv_step, 0)

    def norm_step(step, carry):
        rows = pl.ds(pl.multiple_of(step * 32, 32), 32)
        cells = mixed_ref[rows, :]
        center = cells - jnp.mean(cells, axis=-1, keepdims=True)
        spread = jnp.mean(center * center, axis=-1, keepdims=True)
        normed[rows, :] = (center * lax.rsqrt(spread + 1e-6) * gain_ref[...]).astype(BF16)
        return carry

    lax.fori_loop(0, 8, norm_step, 0)
    stores = [pltpu.make_async_copy(mixed_ref, mixed_hbm, sems.at[3])]
    stores[0].start()
    for load in loads:
        load.wait()
    ordered[...] = jnp.dot(normed[...], order_ref[...], preferred_element_type=F32).astype(BF16)

    for t in range(4):
        lanes = slice(t * 512, t * 512 + 512)
        upper[...] = jnp.dot(normed[...], w_up_ref[:, lanes], preferred_element_type=F32)

        def gelu_step(step, bias):
            rows = pl.ds(pl.multiple_of(step * 32, 32), 32)
            u = upper[rows, :] + b_up_ref[:, lanes]
            square = u * u
            th = jnp.tanh(ROOT_2_PI * (u + CUBIC * (square * u)))
            half = 0.5 * (1.0 + th)
            active[rows, :] = (u * half).astype(BF16)
            slope = half + (0.5 * ROOT_2_PI) * u * (1.0 - th * th) * (1.0 + (3.0 * CUBIC) * square)
            d_up = (d_act_ref[rows, lanes] * slope).astype(BF16)
            d_upper_ref[rows, lanes] = d_up
            return bias + jnp.sum(d_up.astype(F32), axis=0, keepdims=True)

        bias_ref[t : t + 1, :] = lax.fori_loop(0, 8, gelu_step, jnp.zeros((1, 512), F32))
        if t == 3:
            stores.append(pltpu.make_async_copy(d_upper_ref, d_upper_hbm, sems.at[4]))
            stores[-1].start()
        tile[...] = lax.dot_general(
            active[...], d_out_ref[...], (((0,), (0,)), ((), ())), preferred_element_type=F32
        )
        for y_hi in range(2):
            k_y = (y_hi * 2 + t // 2) ^ y_at
            for k_x in range(4):
                base = y_hi * 32 + (k_x ^ x_at) * 8
                for mine in range(2):
                    at = base + ((1 - core) if mine == 0 else core) * 64
                    piece = jnp.concatenate(
                        [tile[pl.ds(pl.multiple_of(at + zz * 128, 8), 8), :] for zz in range(4)],
                        axis=0,
                    )
                    rows = pl.ds(pl.multiple_of(k_y * 64 + (t % 2) * 32, 32), 32)
                    if mine == 0:
                        give[k_x, rows, :] = piece.astype(BF16)
                    elif k_x == 0:
                        own[rows, :] = piece
                    else:
                        keep[k_x - 1, rows, :] = piece.astype(BF16)

    def store(at, source, target):
        stores.append(pltpu.make_async_copy(source, target, sems.at[at]))
        stores[-1].start()

    first, second = slice(0, 256), slice(256, 512)
    store(5, give.at[:, first], send_hbm.at[:, first])
    store(6, keep.at[:, first], keep_hbm.at[:, first])
    store(7, own.at[first], own_hbm.at[first])
    for t in range(4):
        lanes = slice(t * 512, t * 512 + 512)
        tile[...] = lax.dot_general(
            ordered[...], d_upper_ref[:, lanes], (((0,), (0,)), ((), ())),
            preferred_element_type=F32,
        )
        rows = slice(256 + t * 64, 320 + t * 64)
        own[rows, :] = tile[0:64, :]
        for k in range(4):
            give[k, rows, :] = tile[256 + k * 64 : 320 + k * 64, :].astype(BF16)
            if k:
                keep[k - 1, rows, :] = tile[k * 64 : k * 64 + 64, :].astype(BF16)
    store(8, give.at[:, second], send_hbm.at[:, second])
    store(9, keep.at[:, second], keep_hbm.at[:, second])
    store(10, own.at[second], own_hbm.at[second])
    for copy in stores:
        copy.wait()


def backward_kernel(
    ext_ref, mixed_ref, gain_ref, bias_ref, d_upper_hbm, w_up_hbm,
    small_ref, d_cells, wide, shifted, d_normed, d_upper_ref, w_up_ref, sems,
):
    loads = [
        pltpu.make_async_copy(d_upper_hbm, d_upper_ref, sems.at[0]),
        pltpu.make_async_copy(w_up_hbm, w_up_ref, sems.at[1]),
    ]
    for load in loads:
        load.start()
    spread_rows(ext_ref, wide, shifted)
    for load in loads:
        load.wait()
    d_normed[...] = lax.dot_general(
        d_upper_ref[...], w_up_ref[...], (((1,), (1,)), ((), ())), preferred_element_type=F32
    )

    def norm_step(step, gain_sum):
        rows = pl.ds(pl.multiple_of(step * 32, 32), 32)
        cells = mixed_ref[rows, :]
        center = cells - jnp.mean(cells, axis=-1, keepdims=True)
        spread = jnp.mean(center * center, axis=-1, keepdims=True)
        inverse = lax.rsqrt(spread + 1e-6)
        unit = center * inverse
        d = d_normed[rows, :]
        d_unit = d * gain_ref[...]
        along = jnp.mean(d_unit * unit, axis=-1, keepdims=True)
        d_center = (d_unit - unit * along) * inverse
        d_mixed = d_center - jnp.mean(d_center, axis=-1, keepdims=True)
        d_cells[pl.ds(step * 2, 2)] = d_mixed.reshape(2, 16, 512)
        return gain_sum + jnp.sum(d * unit, axis=0, keepdims=True)

    small_ref[49:50, :] = lax.fori_loop(0, 8, norm_step, jnp.zeros((1, 512), F32))
    small_ref[50:54, :] = bias_ref[0:4, :]
    small_ref[54:64, :] = jnp.zeros((10, 512), F32)
    def tap_step(step, carry):
        lanes = pl.ds(pl.multiple_of(step * 128, 128), 128)
        d = [d_cells[x, :, lanes] for x in range(16)]
        for b in range(7):
            totals = [jnp.zeros((8, 128), F32)] * 7
            for r in range(22):
                cells = shifted[b, r, :, lanes]
                for a in range(max(0, r - 15), min(7, r + 1)):
                    product = cells * d[r - a]
                    totals[a] = totals[a] + product[:8] + product[8:]
            for a in range(7):
                row = a * 7 + b
                small_ref[row : row + 1, lanes] = jnp.sum(totals[a], axis=0, keepdims=True)
        return carry

    lax.fori_loop(0, 4, tap_step, 0)


def rim_kernel(d_cells, kern_ref, grad_ref, west_ref, east_ref, moved):
    moved[...] = jnp.zeros_like(moved)
    for b in range(7):
        moved[b, :, b : b + 16, :] = d_cells[...]

    def rim_step(step, carry):
        lanes = pl.ds(pl.multiple_of(step * 128, 128), 128)
        for q in range(3):
            rows = slice(q * 8, q * 8 + 8)
            totals = [jnp.zeros((8, 128), F32)] * 22
            for b in range(1 if q == 2 else 0, 7):
                weights = [kern_ref[a * 7 + b : a * 7 + b + 1, lanes] for a in range(7)]
                for x in range(16):
                    cells = moved[b, x, rows, lanes]
                    for a in range(7):
                        totals[x + a] = totals[x + a] + cells * weights[a]
            for i in range(22):
                grad_ref[i, rows, lanes] = totals[i]
        return carry

    lax.fori_loop(0, 4, rim_step, 0)
    filler = jnp.zeros((3, 8, 512), F32)
    west_ref[...] = jnp.concatenate([grad_ref[0:3], filler], axis=1).astype(BF16)
    east_ref[...] = jnp.concatenate([grad_ref[19:22], filler], axis=1).astype(BF16)


VMEM_BYTES = 56 * 1024 * 1024
VMEM = pl.BlockSpec(memory_space=pltpu.VMEM)
SMEM = pl.BlockSpec(memory_space=pltpu.SMEM)
HBM = pl.BlockSpec(memory_space=pl.ANY)


def local_call(kernel, name, shapes, in_specs, out_specs, scratch, operands, flops):
    return pl.pallas_call(
        kernel,
        out_shape=[jax.ShapeDtypeStruct(s, d) for s, d in shapes],
        in_specs=in_specs,
        out_specs=out_specs,
        scratch_shapes=[pltpu.VMEM(s, d) if d else pltpu.SemaphoreType.DMA(s) for s, d in scratch],
        compiler_params=pltpu.CompilerParams(vmem_limit_bytes=VMEM_BYTES),
        cost_estimate=pl.CostEstimate(flops=flops, bytes_accessed=2000000, transcendentals=0),
        name=name,
    )(*operands)


def run_forward(at, ext, kern, gain, w_up, b_up, d_out, d_act, order):
    square, long = (256, 512), (256, 2048)
    return local_call(
        forward_kernel,
        "forward",
        [
            (square, F32), (long, BF16), ((8, 512), F32),
            ((512, 512), F32), ((3, 512, 512), BF16), ((4, 512, 512), BF16),
        ],
        [SMEM] + [VMEM] * 5 + [HBM] * 3,
        [HBM, HBM, VMEM, HBM, HBM, HBM],
        [
            ((22, 32, 512), F32), ((7, 22, 16, 512), F32), (square, BF16), (square, BF16),
            (square, F32), (square, BF16), ((512, 512), F32), (square, F32), ((512, 512), BF16),
            ((512, 2048), BF16), (long, F32), (long, BF16),
            ((512, 512), F32), ((3, 512, 512), BF16), ((4, 512, 512), BF16), ((11,), None),
        ],
        [at, ext, kern, gain, b_up, d_out, order, w_up, d_act],
        14000000000,
    )


def run_backward(ext, mixed, d_upper, w_up, gain, bias):
    return local_call(
        backward_kernel,
        "backward",
        [((64, 512), F32), ((16, 16, 512), F32)],
        [VMEM] * 4 + [HBM] * 2,
        [VMEM] * 2,
        [
            ((22, 32, 512), F32), ((7, 22, 16, 512), F32), ((256, 512), F32),
            ((256, 2048), BF16), ((512, 2048), BF16), ((2,), None),
        ],
        [ext, mixed, gain, bias, d_upper, w_up],
        8000000000,
    )


def run_rims(d_cells, kern):
    return local_call(
        rim_kernel,
        "rims",
        [((22, 24, 512), F32), ((3, 32, 512), BF16), ((3, 32, 512), BF16)],
        [VMEM] * 2,
        [VMEM] * 3,
        [((7, 16, 24, 512), F32)],
        [d_cells, kern],
        5000000000,
    )


def run_sum(kernel, shapes, operands, name, scalars=0, scratch=()):
    return local_call(
        kernel, name, shapes, [SMEM] * scalars + [VMEM] * (len(operands) - scalars),
        [VMEM] * len(shapes), scratch, operands, 800000000,
    )


def first_sum_kernel(mine_ref, keep_ref, given_ref, own_ref, *give_refs):
    own_ref[...] = mine_ref[...] + given_ref[0].astype(F32)
    for k in range(3):
        for part in range(2):
            rows = slice(part * 256, part * 256 + 256)
            total = keep_ref[k, rows, :].astype(F32) + given_ref[k + 1, rows, :].astype(F32)
            give_refs[part * 3 + k][...] = total.astype(BF16)


def two_terms(value):
    high = value.astype(BF16)
    return high, (value - high.astype(F32)).astype(BF16)


def whole(first, rest, rows):
    a, b, c = [ref[rows, :].astype(F32) for ref in rest]
    return (first + a) + (b + c)


def second_sum_kernel(own_ref, *refs):
    down, up, halves, outs = refs[:3], refs[3:6], refs[6:10], refs[10:]
    large_ref, terms_ref, over_y, over_x = outs[0], outs[1], outs[2:5], outs[5:8]
    half = (halves[0][...] + halves[1][...]) + (halves[2][...] + halves[3][...])
    high, low = two_terms(half)
    terms_ref[...] = high.astype(F32) + low.astype(F32)
    for k in range(4):
        rows = slice(k * 64, k * 64 + 64)
        total = whole(own_ref[rows, :], down, rows)
        if k == 0:
            large_ref[0:64, :] = total
        else:
            over_y[k - 1][0:64, :] = total.astype(BF16)
            over_y[k - 1][64:96, :] = high
            over_y[k - 1][96:128, :] = low
        for t in range(4):
            at = t * 64 + k * 16
            total = whole(own_ref[256 + at : 272 + at, :], up, slice(at, at + 16))
            if k == 0:
                large_ref[64 + t * 16 : 80 + t * 16, :] = total
            else:
                over_x[k - 1][t * 16 : t * 16 + 16, :] = total.astype(BF16)


def whole_terms(first, refs, at):
    a, b, c = [
        ref[at : at + 32, :].astype(F32) + ref[at + 32 : at + 64, :].astype(F32) for ref in refs
    ]
    return (first + a) + (b + c)


def third_sum_kernel(at_ref, large_ref, terms_ref, *refs):
    over_y, over_x = refs[:3], refs[3:6]
    own_ref, half_ref, outs, blocks = refs[6], refs[7], refs[8:11], refs[11]
    low_bits = at_ref[3] & 3
    high, low = two_terms(whole_terms(terms_ref[...], over_y, 64))
    half_ref[...] = high.astype(F32) + low.astype(F32)
    down = whole(large_ref[0:64, :], over_y, slice(0, 64))
    up = whole(large_ref[64:128, :], over_x, slice(0, 64))
    for z in range(8):
        rows = [up[t * 16 + z * 2 : t * 16 + z * 2 + 2] for t in range(4)]
        blocks[z] = jnp.concatenate([down[z * 8 : z * 8 + 8]] + rows, axis=0)
    for k in range(4):
        for z_high in range(2):
            block = blocks[z_high * 4 + (low_bits ^ k)]
            rows = slice(z_high * 16, z_high * 16 + 16)
            if k == 0:
                own_ref[rows, :] = block
            else:
                outs[k - 1][rows, :] = block.astype(BF16)
        if k:
            outs[k - 1][32:64, :] = high
            outs[k - 1][64:96, :] = low


def fourth_sum_kernel(at_ref, own_ref, half_ref, a_ref, b_ref, c_ref, keep_ref, sum_ref, give_ref):
    high = at_ref[3] >> 2
    refs = (a_ref, b_ref, c_ref)
    half = whole_terms(half_ref[...], refs, 32)
    first = whole(own_ref[0:16, :], refs, slice(0, 16))
    second = whole(own_ref[16:32, :], refs, slice(16, 32))
    keep_ref[...] = jnp.where(high == 0, first, second)
    give_ref[0:16, :] = jnp.where(high == 0, second, first)
    give_ref[16:48, :] = half
    sum_ref[...] = half


def last_sum_kernel(keep_ref, half_ref, got_ref, down_ref, up_ref, sum_ref):
    sum_ref[...] = half_ref[...] + got_ref[16:48, :]
    down_ref[...] = keep_ref[0:8, :] + got_ref[0:8, :]
    up = keep_ref[8:16, :] + got_ref[8:16, :]
    for t in range(4):
        up_ref[:, t * 512 : t * 512 + 512] = up[t * 2 : t * 2 + 2]


def per_device(
    field, cotangent, land_sea, fold_partner, depth_kernel, norm_gain, w_up, b_up, w_down
):
    width_lon, width_lat, channels = field.shape
    lon_at = lax.axis_index("lon")
    lat_at = lax.axis_index("lat")
    core = lon_at % 2
    z_at = (lon_at // 2) % 8
    y_at = (lat_at // 4) * 2 + lon_at // 16
    x_at = lat_at % 4
    is_north = lat_at == lax.axis_size("lat") - 1
    from_end = 511 - fold_partner[0]
    turn = 31 - from_end // 16
    shift = 16 - from_end % 16

    lat_ext = extended_2(field, (("lat", 1),), 3, False)
    top_rows = field[:, width_lat - 3 :, :]
    mine = mirror_tiles(top_rows, turn // 2)
    from_next = to_previous(mine)
    from_previous = to_next(mine)
    even = turn % 2 == 0
    low = jnp.where(even, from_next, mine)
    high = jnp.where(even, mine, from_previous)
    facing = lax.dynamic_slice_in_dim(jnp.concatenate([low, high], axis=0), shift, 16, axis=0)
    fold_band = facing[::-1, ::-1, :]
    upper_rim = jnp.where(is_north, fold_band, lat_ext[:, width_lat + 3 :, :])
    lat_ext = jnp.concatenate([lat_ext[:, : width_lat + 3, :], upper_rim], axis=1)
    extended = extended_2(lat_ext, (("lon", 0),), 3, True)
    extended = jnp.pad(extended, ((0, 0), (0, 10), (0, 0)))
    tokens = width_lon * width_lat
    d_out = cotangent.reshape(tokens, channels) * land_sea.reshape(tokens, 1).astype(jnp.bfloat16)
    d_act = lax.dot_general(
        d_out, w_down, (((1,), (1,)), ((), ())), preferred_element_type=jnp.float32
    )
    row = jnp.arange(512, dtype=jnp.int32)
    block = row >> 1
    y_of = (((block >> 2) & 1) << 1) + (block >> 7)
    goes_to = (
        (((block >> 3) & 1) ^ core) * 256
        + (y_of ^ y_at) * 64
        + ((block & 3) ^ x_at) * 16
        + ((block >> 4) & 7) * 2
        + (row & 1)
    )
    order = (goes_to[:, None] == row[None, :]).astype(jnp.bfloat16)
    at = jnp.stack([core, x_at, y_at, z_at]).astype(jnp.int32)
    gain = norm_gain.reshape(1, channels)
    mixed, d_upper, bias, mine, keep, give = run_forward(
        at, extended, depth_kernel, gain, w_up, b_up.reshape(1, 2048), d_out, d_act, order
    )

    given = send(give, CORE_MASK)
    piece = ((256, 512), BF16)
    own, *give = run_sum(
        first_sum_kernel, [((512, 512), F32)] + [piece] * 6, [mine, keep, given], "first_sum"
    )
    own, give, mixed = lax.optimization_barrier((own, give, mixed))
    taken = [send(piece, mask) for piece, mask in zip(give, X_MASKS + Y_MASKS)]

    small, d_cells = run_backward(extended, mixed, d_upper, w_up, gain, bias)

    small, taken = lax.optimization_barrier((small, taken))
    small = small.reshape(2, 32, 512)
    half = lax.dynamic_index_in_dim(small, core, 0, False) + send(
        lax.dynamic_index_in_dim(small, 1 - core, 0, False), CORE_MASK
    )
    halves = [half] + [send(half, mask) for mask in X_MASKS]
    grad_ext, west_rim, east_rim = run_rims(d_cells, depth_kernel)

    rim = jnp.bfloat16
    from_west = to_next(east_rim)[:, :22].astype(jnp.float32)
    from_east = to_previous(west_rim)[:, :22].astype(jnp.float32)
    by_cols = (
        grad_ext[3:19, :22]
        + jnp.pad(from_west, ((0, 13), (0, 0), (0, 0)))
        + jnp.pad(from_east, ((13, 0), (0, 0), (0, 0)))
    )

    top_rim = by_cols[:, 19:22].astype(rim)
    from_south = lax.ppermute(top_rim, "lat", [(i, i + 1) for i in range(7)])
    from_north = lax.ppermute(by_cols[:, 0:3].astype(rim), "lat", [(i + 1, i) for i in range(7)])
    fold_strip = jnp.where(is_north, top_rim, jnp.zeros_like(top_rim))
    spread = lax.dynamic_update_slice_in_dim(
        jnp.zeros((32, 3, channels), rim), fold_strip[::-1, ::-1, :], shift, axis=0
    )
    none = jnp.zeros_like(spread[:16])
    mine = jnp.where(even, spread[16:], spread[:16])
    mine = mine + to_next(jnp.where(even, spread[:16], none))
    mine = mine + to_previous(jnp.where(even, none, spread[16:]))
    from_fold = mirror_tiles(mine, turn >> 1)

    large, terms, *give = run_sum(
        second_sum_kernel,
        [((128, 512), F32), ((32, 512), F32)] + [((128, 512), BF16)] * 3 + [((64, 512), BF16)] * 3,
        [own, *taken, *halves],
        "second_sum",
    )
    taken = [send(piece, mask) for piece, mask in zip(give, Y_MASKS + X_MASKS)]

    own, half, *give = run_sum(
        third_sum_kernel,
        [((32, 512), F32), ((32, 512), F32)] + [((96, 512), BF16)] * 3,
        [at, large, terms, *taken],
        "third_sum",
        scalars=1,
        scratch=[((8, 16, 512), F32)],
    )
    taken = [send(piece, mask) for piece, mask in zip(give, Z_MASKS[:3])]
    keep, half, give = run_sum(
        fourth_sum_kernel,
        [((16, 512), F32), ((32, 512), F32), ((48, 512), F32)],
        [at, own, half, *taken],
        "fourth_sum",
        scalars=1,
    )
    grad_down, grad_up, half = run_sum(
        last_sum_kernel,
        [((8, 512), F32), ((2, 2048), F32), ((32, 512), F32)],
        [keep, half, send(give, Z_MASKS[3])],
        "last_sum",
    )
    other = send(half, CORE_MASK)
    small = jnp.where(
        core == 0,
        jnp.concatenate([half, other], axis=0),
        jnp.concatenate([other, half], axis=0),
    )
    grad_kernel = small[:49]
    grad_gain = small[49]
    grad_bias = small[50:54].reshape(2048)

    from_south = jnp.pad(from_south, ((0, 0), (0, 13), (0, 0)))
    from_north = jnp.pad(from_north, ((0, 0), (13, 0), (0, 0)))
    from_fold = jnp.pad(from_fold, ((0, 0), (13, 0), (0, 0)))
    owned = by_cols[:, 3:19] + from_south.astype(jnp.float32) + from_north.astype(jnp.float32)
    owned = owned + from_fold.astype(jnp.float32)
    grad_field = (cotangent.astype(jnp.float32) + owned).astype(jnp.bfloat16)
    return (grad_field, grad_up, grad_down, grad_kernel, grad_gain, grad_bias)


def solution(mesh):
    placed = (
        P("lon", "lat", None),
        P("lon", "lat", None),
        P("lon", "lat"),
        P(),
        P(),
        P(),
        P(),
        P(),
        P(),
    )
    return jax.shard_map(
        per_device,
        mesh=mesh,
        in_specs=placed,
        out_specs=(
            P("lon", "lat", None),
            P(("lon", "lat"), None),
            P(("lon", "lat"), None),
            P(),
            P(),
            P(),
        ),
        check_vma=False,
    )
```

```python
import jax
import jax.numpy as jnp
from jax import lax
from jax.experimental import pallas as pl
from jax.experimental.pallas import tpu as pltpu
from jax.sharding import PartitionSpec as P

DEVICES = ("lon", "lat")
X_MASKS = (1, 2, 3)
Y_MASKS = (128, 4, 132)
Z_MASKS = (16, 32, 48, 64)
CORE_MASK = 8


def send(value, mask):
    return lax.ppermute(value, DEVICES, [(i, i ^ mask) for i in range(256)])


def to_next(value):
    return lax.ppermute(value, "lon", [(i, (i + 1) % 32) for i in range(32)])


def to_previous(value):
    return lax.ppermute(value, "lon", [((i + 1) % 32, i) for i in range(32)])


def to_north(value):
    return lax.ppermute(value, "lat", [(i, i + 1) for i in range(7)])


def to_south(value):
    return lax.ppermute(value, "lat", [(i + 1, i) for i in range(7)])


def mirror_tiles(near, far, half_turn):
    def swap(value, k):
        pairs = [(e * 8 + 7, ((2 * k - e) % 32) * 8 + 7) for e in range(32)]
        return lax.ppermute(value, DEVICES, pairs)

    def branch(k):
        return lambda a, b: (swap(a, k), swap(b, (k - 1) % 16))

    return lax.switch(half_turn, [branch(k) for k in range(16)], near, far)


ROOT_2_PI = 0.7978845608028654
CUBIC = 0.044715
F32 = jnp.float32
BF16 = jnp.bfloat16


def spread_rows(ext_ref, wide, shifted):
    wide[...] = ext_ref[...].astype(F32)
    for b in range(7):
        shifted[b] = wide[:, b : b + 16, :]


def forward_kernel(
    at_ref, ext_ref, kern_ref, gain_ref, b_up_ref, d_out_ref, order_hbm, w_up_hbm, d_act_hbm,
    d_cells, half_ref, own_hbm, keep_hbm, send_hbm,
    wide, shifted, normed, ordered, upper, active, tile, mixed_ref, order_ref, w_up_ref, d_act_ref,
    d_upper_ref, own, keep, give, small_ref, sems,
):
    core, x_at, y_at = at_ref[0], at_ref[1], at_ref[2]
    loads = [
        pltpu.make_async_copy(order_hbm, order_ref, sems.at[0]),
        pltpu.make_async_copy(w_up_hbm, w_up_ref, sems.at[1]),
        pltpu.make_async_copy(d_act_hbm, d_act_ref, sems.at[2]),
    ]
    for load in loads:
        load.start()
    spread_rows(ext_ref, wide, shifted)

    def conv_step(step, carry):
        lanes = pl.ds(pl.multiple_of(step * 128, 128), 128)
        totals = [jnp.zeros((16, 128), F32)] * 16
        for b in range(7):
            weights = [kern_ref[a * 7 + b : a * 7 + b + 1, lanes] for a in range(7)]
            for r in range(22):
                cells = shifted[b, r, :, lanes]
                for a in range(max(0, r - 15), min(7, r + 1)):
                    totals[r - a] = totals[r - a] + cells * weights[a]
        for x in range(16):
            mixed_ref[x * 16 : x * 16 + 16, lanes] = totals[x]
        return carry

    lax.fori_loop(0, 4, conv_step, 0)

    def norm_step(step, carry):
        rows = pl.ds(pl.multiple_of(step * 32, 32), 32)
        cells = mixed_ref[rows, :]
        center = cells - jnp.mean(cells, axis=-1, keepdims=True)
        spread = jnp.mean(center * center, axis=-1, keepdims=True)
        normed[rows, :] = (center * lax.rsqrt(spread + 1e-6) * gain_ref[...]).astype(BF16)
        return carry

    lax.fori_loop(0, 8, norm_step, 0)
    for load in loads:
        load.wait()
    ordered[...] = jnp.dot(normed[...], order_ref[...], preferred_element_type=F32).astype(BF16)

    for t in range(4):
        lanes = slice(t * 512, t * 512 + 512)
        upper[...] = jnp.dot(normed[...], w_up_ref[:, lanes], preferred_element_type=F32)

        def gelu_step(step, bias):
            rows = pl.ds(pl.multiple_of(step * 32, 32), 32)
            u = upper[rows, :] + b_up_ref[:, lanes]
            square = u * u
            th = jnp.tanh(ROOT_2_PI * (u + CUBIC * (square * u)))
            half = 0.5 * (1.0 + th)
            active[rows, :] = (u * half).astype(BF16)
            slope = half + (0.5 * ROOT_2_PI) * u * (1.0 - th * th) * (1.0 + (3.0 * CUBIC) * square)
            d_up = (d_act_ref[rows, lanes] * slope).astype(BF16)
            d_upper_ref[rows, lanes] = d_up
            return bias + jnp.sum(d_up.astype(F32), axis=0, keepdims=True)

        small_ref[50 + t : 51 + t, :] = lax.fori_loop(0, 8, gelu_step, jnp.zeros((1, 512), F32))
        tile[...] = lax.dot_general(
            active[...], d_out_ref[...], (((0,), (0,)), ((), ())), preferred_element_type=F32
        )
        for y_hi in range(2):
            k_y = (y_hi * 2 + t // 2) ^ y_at
            for k_x in range(4):
                base = y_hi * 32 + (k_x ^ x_at) * 8
                for mine in range(2):
                    at = base + ((1 - core) if mine == 0 else core) * 64
                    piece = jnp.concatenate(
                        [tile[pl.ds(pl.multiple_of(at + zz * 128, 8), 8), :] for zz in range(4)],
                        axis=0,
                    )
                    at = k_y * 64 + (t % 2) * 32
                    rows = pl.ds(pl.multiple_of(at, 32), 32)
                    if mine == 0:
                        give[pl.ds(pl.multiple_of(k_x * 512 + at, 32), 32), :] = piece.astype(BF16)
                    elif k_x == 0:
                        own[rows, :] = piece
                    else:
                        keep[k_x - 1, rows, :] = piece.astype(BF16)

    for t in range(4):
        lanes = slice(t * 512, t * 512 + 512)
        tile[...] = lax.dot_general(
            ordered[...], d_upper_ref[:, lanes], (((0,), (0,)), ((), ())),
            preferred_element_type=F32,
        )
        at = 256 + t * 64
        own[at : at + 64, :] = tile[0:64, :]
        for k in range(4):
            piece = tile[256 + k * 64 : 320 + k * 64, :]
            give[k * 512 + at : k * 512 + at + 64, :] = piece.astype(BF16)
            if k:
                keep[k - 1, at : at + 64, :] = tile[k * 64 : k * 64 + 64, :].astype(BF16)
    stores = [
        pltpu.make_async_copy(give.at[0:2048], send_hbm.at[0:2048], sems.at[3]),
        pltpu.make_async_copy(keep, keep_hbm, sems.at[4]),
        pltpu.make_async_copy(own, own_hbm, sems.at[5]),
    ]
    for store in stores:
        store.start()
    upper[...] = lax.dot_general(
        d_upper_ref[...], w_up_ref[...], (((1,), (1,)), ((), ())), preferred_element_type=F32
    )

    def norm_step(step, gain_sum):
        rows = pl.ds(pl.multiple_of(step * 32, 32), 32)
        cells = mixed_ref[rows, :]
        center = cells - jnp.mean(cells, axis=-1, keepdims=True)
        spread = jnp.mean(center * center, axis=-1, keepdims=True)
        inverse = lax.rsqrt(spread + 1e-6)
        unit = center * inverse
        d = upper[rows, :]
        d_unit = d * gain_ref[...]
        along = jnp.mean(d_unit * unit, axis=-1, keepdims=True)
        d_center = (d_unit - unit * along) * inverse
        d_mixed = d_center - jnp.mean(d_center, axis=-1, keepdims=True)
        d_cells[pl.ds(step * 2, 2)] = d_mixed.reshape(2, 16, 512)
        return gain_sum + jnp.sum(d * unit, axis=0, keepdims=True)

    small_ref[49:50, :] = lax.fori_loop(0, 8, norm_step, jnp.zeros((1, 512), F32))
    small_ref[54:64, :] = jnp.zeros((10, 512), F32)
    def tap_step(step, carry):
        lanes = pl.ds(pl.multiple_of(step * 128, 128), 128)
        d = [d_cells[x, :, lanes] for x in range(16)]
        for b in range(7):
            totals = [jnp.zeros((8, 128), F32)] * 7
            for r in range(22):
                cells = shifted[b, r, :, lanes]
                for a in range(max(0, r - 15), min(7, r + 1)):
                    product = cells * d[r - a]
                    totals[a] = totals[a] + product[:8] + product[8:]
            for a in range(7):
                row = a * 7 + b
                small_ref[row : row + 1, lanes] = jnp.sum(totals[a], axis=0, keepdims=True)
        return carry

    lax.fori_loop(0, 4, tap_step, 0)

    half_ref[...] = small_ref[pl.ds(pl.multiple_of(core * 32, 32), 32), :]
    high, low = two_terms(small_ref[pl.ds(pl.multiple_of((1 - core) * 32, 32), 32), :])
    give[2048:2080, :] = high
    give[2080:2112, :] = low
    stores.append(
        pltpu.make_async_copy(give.at[2048:2112], send_hbm.at[2048:2112], sems.at[6])
    )
    stores[-1].start()
    for store in stores:
        store.wait()


def rim_kernel(d_cells, kern_ref, grad_ref, moved):
    moved[...] = jnp.zeros_like(moved)
    for b in range(7):
        moved[b, :, b : b + 16, :] = d_cells[...]

    def rim_step(step, carry):
        lanes = pl.ds(pl.multiple_of(step * 128, 128), 128)
        for q in range(3):
            rows = slice(q * 8, q * 8 + 8)
            totals = [jnp.zeros((8, 128), F32)] * 22
            for b in range(1 if q == 2 else 0, 7):
                weights = [kern_ref[a * 7 + b : a * 7 + b + 1, lanes] for a in range(7)]
                for x in range(16):
                    cells = moved[b, x, rows, lanes]
                    for a in range(7):
                        totals[x + a] = totals[x + a] + cells * weights[a]
            for i in range(22):
                grad_ref[i, rows, lanes] = totals[i]
        return carry

    lax.fori_loop(0, 4, rim_step, 0)


VMEM_BYTES = 56 * 1024 * 1024
VMEM = pl.BlockSpec(memory_space=pltpu.VMEM)
SMEM = pl.BlockSpec(memory_space=pltpu.SMEM)
HBM = pl.BlockSpec(memory_space=pl.ANY)


def local_call(kernel, name, shapes, in_specs, out_specs, scratch, operands, flops):
    return pl.pallas_call(
        kernel,
        out_shape=[jax.ShapeDtypeStruct(s, d) for s, d in shapes],
        in_specs=in_specs,
        out_specs=out_specs,
        scratch_shapes=[pltpu.VMEM(s, d) if d else pltpu.SemaphoreType.DMA(s) for s, d in scratch],
        compiler_params=pltpu.CompilerParams(vmem_limit_bytes=VMEM_BYTES),
        cost_estimate=pl.CostEstimate(flops=flops, bytes_accessed=2000000, transcendentals=0),
        name=name,
    )(*operands)


def run_forward(at, ext, kern, gain, w_up, b_up, d_out, d_act, order):
    square, long = (256, 512), (256, 2048)
    return local_call(
        forward_kernel,
        "forward",
        [
            ((16, 16, 512), F32), ((32, 512), F32),
            ((512, 512), F32), ((3, 512, 512), BF16), ((2112, 512), BF16),
        ],
        [SMEM] + [VMEM] * 5 + [HBM] * 3,
        [VMEM, VMEM, HBM, HBM, HBM],
        [
            ((22, 32, 512), F32), ((7, 22, 16, 512), F32), (square, BF16), (square, BF16),
            (square, F32), (square, BF16), ((512, 512), F32), (square, F32), ((512, 512), BF16),
            ((512, 2048), BF16), (long, F32), (long, BF16),
            ((512, 512), F32), ((3, 512, 512), BF16), ((2112, 512), BF16), ((64, 512), F32),
            ((7,), None),
        ],
        [at, ext, kern, gain, b_up, d_out, order, w_up, d_act],
        20000000000,
    )


def run_rims(d_cells, kern):
    return local_call(
        rim_kernel,
        "rims",
        [((22, 24, 512), F32)],
        [VMEM] * 2,
        [VMEM],
        [((7, 16, 24, 512), F32)],
        [d_cells, kern],
        5000000000,
    )[0]


def run_sum(kernel, shapes, operands, name, scalars=0, scratch=()):
    return local_call(
        kernel, name, shapes, [SMEM] * scalars + [VMEM] * (len(operands) - scalars),
        [VMEM] * len(shapes), scratch, operands, 800000000,
    )


def two_terms(value):
    high = value.astype(BF16)
    return high, (value - high.astype(F32)).astype(BF16)


def rounded(high, low):
    return high.astype(F32) + low.astype(F32)


def whole(first, rest, rows):
    a, b, c = [ref[rows, :].astype(F32) for ref in rest]
    return (first + a) + (b + c)


def whole_terms(first, refs, at):
    a, b, c = [rounded(ref[at : at + 32, :], ref[at + 32 : at + 64, :]) for ref in refs]
    return (first + a) + (b + c)


def first_sum_kernel(mine_ref, keep_ref, given_ref, half_ref, own_ref, terms_ref, *give_refs):
    own_ref[...] = mine_ref[...] + given_ref[0:512, :].astype(F32)
    half = half_ref[...] + rounded(given_ref[2048:2080, :], given_ref[2080:2112, :])
    high, low = two_terms(half)
    terms_ref[...] = rounded(high, low)
    for k in range(3):
        rows = slice(k * 512 + 512, k * 512 + 1024)
        total = keep_ref[k].astype(F32) + given_ref[rows, :].astype(F32)
        give_refs[k][0:512, :] = total.astype(BF16)
        give_refs[k][512:544, :] = high
        give_refs[k][544:576, :] = low


def second_sum_kernel(own_ref, terms_ref, a_ref, b_ref, c_ref, large_ref, next_ref, *give_refs):
    refs = (a_ref, b_ref, c_ref)
    high, low = two_terms(whole_terms(terms_ref[...], refs, 512))
    next_ref[...] = rounded(high, low)
    for k in range(4):
        pieces = [(0, k * 64, 64)] + [(64 + t * 16, 256 + t * 64 + k * 16, 16) for t in range(4)]
        for target, at, count in pieces:
            rows = slice(at, at + count)
            total = whole(own_ref[rows, :], refs, rows)
            if k == 0:
                large_ref[target : target + count, :] = total
            else:
                give_refs[k - 1][target : target + count, :] = total.astype(BF16)
        if k:
            give_refs[k - 1][128:160, :] = high
            give_refs[k - 1][160:192, :] = low


def third_sum_kernel(at_ref, large_ref, terms_ref, a_ref, b_ref, c_ref, *outs):
    refs = (a_ref, b_ref, c_ref)
    own_ref, half_ref, give_refs, blocks = outs[0], outs[1], outs[2:5], outs[5]
    low_bits = at_ref[3] & 3
    high, low = two_terms(whole_terms(terms_ref[...], refs, 128))
    half_ref[...] = rounded(high, low)
    down = whole(large_ref[0:64, :], refs, slice(0, 64))
    up = whole(large_ref[64:128, :], refs, slice(64, 128))
    for z in range(8):
        rows = [up[t * 16 + z * 2 : t * 16 + z * 2 + 2] for t in range(4)]
        blocks[z] = jnp.concatenate([down[z * 8 : z * 8 + 8]] + rows, axis=0)
    for k in range(4):
        for z_high in range(2):
            block = blocks[z_high * 4 + (low_bits ^ k)]
            rows = slice(z_high * 16, z_high * 16 + 16)
            if k == 0:
                own_ref[rows, :] = block
            else:
                give_refs[k - 1][rows, :] = block.astype(BF16)
        if k:
            give_refs[k - 1][32:64, :] = high
            give_refs[k - 1][64:96, :] = low


def fourth_sum_kernel(at_ref, own_ref, half_ref, a_ref, b_ref, c_ref, keep_ref, sum_ref, give_ref):
    high = at_ref[3] >> 2
    refs = (a_ref, b_ref, c_ref)
    half = whole_terms(half_ref[...], refs, 32)
    first = whole(own_ref[0:16, :], refs, slice(0, 16))
    second = whole(own_ref[16:32, :], refs, slice(16, 32))
    keep_ref[...] = jnp.where(high == 0, first, second)
    give_ref[0:16, :] = jnp.where(high == 0, second, first)
    give_ref[16:48, :] = half
    sum_ref[...] = half


def last_sum_kernel(keep_ref, half_ref, got_ref, down_ref, up_ref, sum_ref):
    sum_ref[...] = half_ref[...] + got_ref[16:48, :]
    down_ref[...] = keep_ref[0:8, :] + got_ref[0:8, :]
    up = keep_ref[8:16, :] + got_ref[8:16, :]
    for t in range(4):
        up_ref[:, t * 512 : t * 512 + 512] = up[t * 2 : t * 2 + 2]


def per_device(
    field, cotangent, land_sea, fold_partner, depth_kernel, norm_gain, w_up, b_up, w_down
):
    width_lon, width_lat, channels = field.shape
    lon_at = lax.axis_index("lon")
    lat_at = lax.axis_index("lat")
    core = lon_at & 1
    z_at = (lon_at >> 1) & 7
    y_at = ((lat_at >> 2) << 1) + (lon_at >> 4)
    x_at = lat_at & 3
    is_north = lat_at == lax.axis_size("lat") - 1
    from_end = 511 - fold_partner[0]
    turn = 31 - (from_end >> 4)
    half_turn = (turn + 1) >> 1
    shift = 32 - ((turn & 1) << 4) - (from_end & 15)

    top_rows = field[:, width_lat - 3 :, :]
    south = to_north(top_rows)
    north = to_south(field[:, 0:3, :])
    near, far = mirror_tiles(top_rows, top_rows, half_turn)
    west = to_next(field[width_lon - 3 :])
    east = to_previous(field[0:3])
    from_next = to_previous(jnp.concatenate([near, far[13:], south[:3], north[:3]], axis=0))
    from_previous = to_next(jnp.concatenate([near[:3], south[13:], north[13:]], axis=0))
    fold = jnp.concatenate([from_next[16:19], far, from_next[:16], near, from_previous[:3]], axis=0)
    band = lax.dynamic_slice_in_dim(fold, shift, 22, axis=0)[::-1, ::-1, :]
    north = jnp.concatenate([from_previous[6:9], north, from_next[22:25]], axis=0)
    extended = jnp.concatenate(
        [
            jnp.concatenate([from_previous[3:6], south, from_next[19:22]], axis=0),
            jnp.concatenate([west, field, east], axis=0),
            jnp.where(is_north, band, north),
            jnp.zeros((22, 10, channels), jnp.bfloat16),
        ],
        axis=1,
    )
    tokens = width_lon * width_lat
    d_out = cotangent.reshape(tokens, channels) * land_sea.reshape(tokens, 1).astype(jnp.bfloat16)
    d_act = lax.dot_general(
        d_out, w_down, (((1,), (1,)), ((), ())), preferred_element_type=jnp.float32
    )
    row = jnp.arange(512, dtype=jnp.int32)
    block = row >> 1
    y_of = (((block >> 2) & 1) << 1) + (block >> 7)
    goes_to = (
        (((block >> 3) & 1) ^ core) * 256
        + ((block & 3) ^ x_at) * 64
        + (y_of ^ y_at) * 16
        + ((block >> 4) & 7) * 2
        + (row & 1)
    )
    order = (goes_to[:, None] == row[None, :]).astype(jnp.bfloat16)
    at = jnp.stack([core, x_at, y_at, z_at]).astype(jnp.int32)
    gain = norm_gain.reshape(1, channels)
    d_cells, half, mine, keep, give = run_forward(
        at, extended, depth_kernel, gain, w_up, b_up.reshape(1, 2048), d_out, d_act, order
    )

    given = send(give, CORE_MASK)
    own, terms, *give = run_sum(
        first_sum_kernel,
        [((512, 512), F32), ((32, 512), F32)] + [((576, 512), BF16)] * 3,
        [mine, keep, given, half],
        "first_sum",
    )
    own, give, d_cells = lax.optimization_barrier((own, give, d_cells))
    taken = [send(piece, mask) for piece, mask in zip(give, X_MASKS)]

    grad_ext = run_rims(d_cells, depth_kernel)[:, :22]
    rim = jnp.bfloat16
    window = jnp.where(is_north, grad_ext[::-1, 19:22][:, ::-1], 0.0).astype(rim)
    fold = lax.dynamic_update_slice_in_dim(
        jnp.zeros((54, 3, channels), rim), window, shift, axis=0
    )

    def flat(value):
        return value.astype(rim).reshape(-1, channels)

    west = to_next(
        jnp.concatenate([flat(grad_ext[19:22]), flat(fold[19:35]), flat(fold[0:3])], axis=0)
    ).astype(F32)
    east = to_previous(
        jnp.concatenate([flat(grad_ext[0:3]), flat(fold[51:54])], axis=0)
    ).astype(F32)
    taken, west, east = lax.optimization_barrier((taken, west, east))
    by_cols = (
        grad_ext[3:19]
        + jnp.pad(west[:66].reshape(3, 22, channels), ((0, 13), (0, 0), (0, 0)))
        + jnp.pad(east[:66].reshape(3, 22, channels), ((13, 0), (0, 0), (0, 0)))
    )
    near = fold[35:51].astype(F32) + west[66:114].reshape(16, 3, channels)
    near = near + jnp.pad(east[66:75].reshape(3, 3, channels), ((0, 13), (0, 0), (0, 0)))
    far = fold[3:19].astype(F32) + jnp.pad(
        west[114:123].reshape(3, 3, channels), ((13, 0), (0, 0), (0, 0))
    )
    from_south = to_north(by_cols[:, 19:22].astype(rim))
    from_north = to_south(by_cols[:, 0:3].astype(rim))
    near, far = mirror_tiles(near.astype(rim), far.astype(rim), half_turn)
    from_fold = near.astype(F32) + far.astype(F32)

    large, terms, *give = run_sum(
        second_sum_kernel,
        [((128, 512), F32), ((32, 512), F32)] + [((192, 512), BF16)] * 3,
        [own, terms, *taken],
        "second_sum",
    )
    taken = [send(piece, mask) for piece, mask in zip(give, Y_MASKS)]

    own, half, *give = run_sum(
        third_sum_kernel,
        [((32, 512), F32), ((32, 512), F32)] + [((96, 512), BF16)] * 3,
        [at, large, terms, *taken],
        "third_sum",
        scalars=1,
        scratch=[((8, 16, 512), F32)],
    )
    taken = [send(piece, mask) for piece, mask in zip(give, Z_MASKS[:3])]
    keep, half, give = run_sum(
        fourth_sum_kernel,
        [((16, 512), F32), ((32, 512), F32), ((48, 512), F32)],
        [at, own, half, *taken],
        "fourth_sum",
        scalars=1,
    )
    grad_down, grad_up, half = run_sum(
        last_sum_kernel,
        [((8, 512), F32), ((2, 2048), F32), ((32, 512), F32)],
        [keep, half, send(give, Z_MASKS[3])],
        "last_sum",
    )
    other = send(half, CORE_MASK)
    small = jnp.where(
        core == 0,
        jnp.concatenate([half, other], axis=0),
        jnp.concatenate([other, half], axis=0),
    )
    grad_kernel = small[:49]
    grad_gain = small[49]
    grad_bias = small[50:54].reshape(2048)
    owned = by_cols[:, 3:19] + jnp.pad(from_south.astype(F32), ((0, 0), (0, 13), (0, 0)))
    owned = owned + jnp.pad(from_north.astype(F32) + from_fold, ((0, 0), (13, 0), (0, 0)))
    grad_field = (cotangent.astype(F32) + owned).astype(jnp.bfloat16)
    return (grad_field, grad_up, grad_down, grad_kernel, grad_gain, grad_bias)


def solution(mesh):
    placed = (
        P("lon", "lat", None),
        P("lon", "lat", None),
        P("lon", "lat"),
        P(),
        P(),
        P(),
        P(),
        P(),
        P(),
    )
    return jax.shard_map(
        per_device,
        mesh=mesh,
        in_specs=placed,
        out_specs=(
            P("lon", "lat", None),
            P(("lon", "lat"), None),
            P(("lon", "lat"), None),
            P(),
            P(),
            P(),
        ),
        check_vma=False,
    )
```

```python
import jax
import jax.numpy as jnp
from jax import lax
from jax.experimental import pallas as pl
from jax.experimental.pallas import tpu as pltpu
from jax.sharding import PartitionSpec as P

DEVICES = ("lon", "lat")
X_MASKS = (1, 2, 3)
Y_MASKS = (128, 4, 132)
Z_MASKS = (16, 32, 48, 64)
CORE_MASK = 8


def send(value, mask):
    return lax.ppermute(value, DEVICES, [(i, i ^ mask) for i in range(256)])


def to_next(value):
    return lax.ppermute(value, "lon", [(i, (i + 1) % 32) for i in range(32)])


def to_previous(value):
    return lax.ppermute(value, "lon", [((i + 1) % 32, i) for i in range(32)])


def to_north(value):
    return lax.ppermute(value, "lat", [(i, i + 1) for i in range(7)])


def to_south(value):
    return lax.ppermute(value, "lat", [(i + 1, i) for i in range(7)])


def mirror_tiles(value, half_turn):
    def branch(k):
        pairs = [(e * 8 + 7, ((2 * k - e) % 32) * 8 + 7) for e in range(32)]
        return lambda v: lax.ppermute(v, DEVICES, pairs)

    return lax.switch(half_turn, [branch(k) for k in range(16)], value)


ROOT_2_PI = 0.7978845608028654
CUBIC = 0.044715
F32 = jnp.float32
BF16 = jnp.bfloat16


def spread_rows(ext_ref, wide, shifted):
    wide[...] = ext_ref[...].astype(F32)
    for b in range(7):
        shifted[b] = wide[:, b : b + 16, :]


def forward_kernel(
    at_ref, ext_ref, kern_ref, gain_ref, b_up_ref, d_out_ref, order_hbm, w_up_hbm, d_act_hbm,
    d_cells, half_ref, own_hbm, keep_hbm, send_hbm,
    wide, shifted, normed, ordered, upper, active, tile, mixed_ref, order_ref, w_up_ref, d_act_ref,
    d_upper_ref, own, keep, give, small_ref, sems,
):
    core, x_at, y_at = at_ref[0], at_ref[1], at_ref[2]
    loads = [
        pltpu.make_async_copy(order_hbm, order_ref, sems.at[0]),
        pltpu.make_async_copy(w_up_hbm, w_up_ref, sems.at[1]),
        pltpu.make_async_copy(d_act_hbm, d_act_ref, sems.at[2]),
    ]
    for load in loads:
        load.start()
    spread_rows(ext_ref, wide, shifted)

    def conv_step(step, carry):
        lanes = pl.ds(pl.multiple_of(step * 128, 128), 128)
        totals = [jnp.zeros((16, 128), F32)] * 16
        for b in range(7):
            weights = [kern_ref[a * 7 + b : a * 7 + b + 1, lanes] for a in range(7)]
            for r in range(22):
                cells = shifted[b, r, :, lanes]
                for a in range(max(0, r - 15), min(7, r + 1)):
                    totals[r - a] = totals[r - a] + cells * weights[a]
        for x in range(16):
            mixed_ref[x * 16 : x * 16 + 16, lanes] = totals[x]
        return carry

    lax.fori_loop(0, 4, conv_step, 0)

    def norm_step(step, carry):
        rows = pl.ds(pl.multiple_of(step * 32, 32), 32)
        cells = mixed_ref[rows, :]
        center = cells - jnp.mean(cells, axis=-1, keepdims=True)
        spread = jnp.mean(center * center, axis=-1, keepdims=True)
        normed[rows, :] = (center * lax.rsqrt(spread + 1e-6) * gain_ref[...]).astype(BF16)
        return carry

    lax.fori_loop(0, 8, norm_step, 0)
    for load in loads:
        load.wait()
    ordered[...] = jnp.dot(normed[...], order_ref[...], preferred_element_type=F32).astype(BF16)

    for t in range(4):
        lanes = slice(t * 512, t * 512 + 512)
        upper[...] = jnp.dot(normed[...], w_up_ref[:, lanes], preferred_element_type=F32)

        def gelu_step(step, bias):
            rows = pl.ds(pl.multiple_of(step * 32, 32), 32)
            u = upper[rows, :] + b_up_ref[:, lanes]
            square = u * u
            th = jnp.tanh(ROOT_2_PI * (u + CUBIC * (square * u)))
            half = 0.5 * (1.0 + th)
            active[rows, :] = (u * half).astype(BF16)
            slope = half + (0.5 * ROOT_2_PI) * u * (1.0 - th * th) * (1.0 + (3.0 * CUBIC) * square)
            d_up = (d_act_ref[rows, lanes] * slope).astype(BF16)
            d_upper_ref[rows, lanes] = d_up
            return bias + jnp.sum(d_up.astype(F32), axis=0, keepdims=True)

        small_ref[50 + t : 51 + t, :] = lax.fori_loop(0, 8, gelu_step, jnp.zeros((1, 512), F32))
        tile[...] = lax.dot_general(
            active[...], d_out_ref[...], (((0,), (0,)), ((), ())), preferred_element_type=F32
        )
        for y_hi in range(2):
            k_y = (y_hi * 2 + t // 2) ^ y_at
            for k_x in range(4):
                base = y_hi * 32 + (k_x ^ x_at) * 8
                for mine in range(2):
                    at = base + ((1 - core) if mine == 0 else core) * 64
                    piece = jnp.concatenate(
                        [tile[pl.ds(pl.multiple_of(at + zz * 128, 8), 8), :] for zz in range(4)],
                        axis=0,
                    )
                    at = k_y * 64 + (t % 2) * 32
                    rows = pl.ds(pl.multiple_of(at, 32), 32)
                    if mine == 0:
                        give[pl.ds(pl.multiple_of(k_x * 512 + at, 32), 32), :] = piece.astype(BF16)
                    elif k_x == 0:
                        own[rows, :] = piece
                    else:
                        keep[k_x - 1, rows, :] = piece.astype(BF16)

    for t in range(4):
        lanes = slice(t * 512, t * 512 + 512)
        tile[...] = lax.dot_general(
            ordered[...], d_upper_ref[:, lanes], (((0,), (0,)), ((), ())),
            preferred_element_type=F32,
        )
        at = 256 + t * 64
        own[at : at + 64, :] = tile[0:64, :]
        for k in range(4):
            piece = tile[256 + k * 64 : 320 + k * 64, :]
            give[k * 512 + at : k * 512 + at + 64, :] = piece.astype(BF16)
            if k:
                keep[k - 1, at : at + 64, :] = tile[k * 64 : k * 64 + 64, :].astype(BF16)
    stores = [
        pltpu.make_async_copy(give.at[0:2048], send_hbm.at[0:2048], sems.at[3]),
        pltpu.make_async_copy(keep, keep_hbm, sems.at[4]),
        pltpu.make_async_copy(own, own_hbm, sems.at[5]),
    ]
    for store in stores:
        store.start()
    upper[...] = lax.dot_general(
        d_upper_ref[...], w_up_ref[...], (((1,), (1,)), ((), ())), preferred_element_type=F32
    )

    def norm_step(step, gain_sum):
        rows = pl.ds(pl.multiple_of(step * 32, 32), 32)
        cells = mixed_ref[rows, :]
        center = cells - jnp.mean(cells, axis=-1, keepdims=True)
        spread = jnp.mean(center * center, axis=-1, keepdims=True)
        inverse = lax.rsqrt(spread + 1e-6)
        unit = center * inverse
        d = upper[rows, :]
        d_unit = d * gain_ref[...]
        along = jnp.mean(d_unit * unit, axis=-1, keepdims=True)
        d_center = (d_unit - unit * along) * inverse
        d_mixed = d_center - jnp.mean(d_center, axis=-1, keepdims=True)
        d_cells[pl.ds(step * 2, 2)] = d_mixed.reshape(2, 16, 512)
        return gain_sum + jnp.sum(d * unit, axis=0, keepdims=True)

    small_ref[49:50, :] = lax.fori_loop(0, 8, norm_step, jnp.zeros((1, 512), F32))
    small_ref[54:64, :] = jnp.zeros((10, 512), F32)
    def tap_step(step, carry):
        lanes = pl.ds(pl.multiple_of(step * 128, 128), 128)
        d = [d_cells[x, :, lanes] for x in range(16)]
        for b in range(7):
            totals = [jnp.zeros((8, 128), F32)] * 7
            for r in range(22):
                cells = shifted[b, r, :, lanes]
                for a in range(max(0, r - 15), min(7, r + 1)):
                    product = cells * d[r - a]
                    totals[a] = totals[a] + product[:8] + product[8:]
            for a in range(7):
                row = a * 7 + b
                small_ref[row : row + 1, lanes] = jnp.sum(totals[a], axis=0, keepdims=True)
        return carry

    lax.fori_loop(0, 4, tap_step, 0)

    half_ref[...] = small_ref[pl.ds(pl.multiple_of(core * 32, 32), 32), :]
    high, low = two_terms(small_ref[pl.ds(pl.multiple_of((1 - core) * 32, 32), 32), :])
    give[2048:2080, :] = high
    give[2080:2112, :] = low
    stores.append(
        pltpu.make_async_copy(give.at[2048:2112], send_hbm.at[2048:2112], sems.at[6])
    )
    stores[-1].start()
    for store in stores:
        store.wait()


def rim_kernel(d_cells, kern_ref, grad_ref, west_ref, east_ref, moved):
    moved[...] = jnp.zeros_like(moved)
    for b in range(7):
        moved[b, :, b : b + 16, :] = d_cells[...]

    def rim_step(step, carry):
        lanes = pl.ds(pl.multiple_of(step * 128, 128), 128)
        for q in range(3):
            rows = slice(q * 8, q * 8 + 8)
            totals = [jnp.zeros((8, 128), F32)] * 22
            for b in range(1 if q == 2 else 0, 7):
                weights = [kern_ref[a * 7 + b : a * 7 + b + 1, lanes] for a in range(7)]
                for x in range(16):
                    cells = moved[b, x, rows, lanes]
                    for a in range(7):
                        totals[x + a] = totals[x + a] + cells * weights[a]
            for i in range(22):
                grad_ref[i, rows, lanes] = totals[i]
        return carry

    lax.fori_loop(0, 4, rim_step, 0)
    filler = jnp.zeros((3, 8, 512), F32)
    west_ref[...] = jnp.concatenate([grad_ref[0:3], filler], axis=1).astype(BF16)
    east_ref[...] = jnp.concatenate([grad_ref[19:22], filler], axis=1).astype(BF16)


VMEM_BYTES = 56 * 1024 * 1024
VMEM = pl.BlockSpec(memory_space=pltpu.VMEM)
SMEM = pl.BlockSpec(memory_space=pltpu.SMEM)
HBM = pl.BlockSpec(memory_space=pl.ANY)


def local_call(kernel, name, shapes, in_specs, out_specs, scratch, operands, flops):
    return pl.pallas_call(
        kernel,
        out_shape=[jax.ShapeDtypeStruct(s, d) for s, d in shapes],
        in_specs=in_specs,
        out_specs=out_specs,
        scratch_shapes=[pltpu.VMEM(s, d) if d else pltpu.SemaphoreType.DMA(s) for s, d in scratch],
        compiler_params=pltpu.CompilerParams(vmem_limit_bytes=VMEM_BYTES),
        cost_estimate=pl.CostEstimate(flops=flops, bytes_accessed=2000000, transcendentals=0),
        name=name,
    )(*operands)


def run_forward(at, ext, kern, gain, w_up, b_up, d_out, d_act, order):
    square, long = (256, 512), (256, 2048)
    return local_call(
        forward_kernel,
        "forward",
        [
            ((16, 16, 512), F32), ((32, 512), F32),
            ((512, 512), F32), ((3, 512, 512), BF16), ((2112, 512), BF16),
        ],
        [SMEM] + [VMEM] * 5 + [HBM] * 3,
        [VMEM, VMEM, HBM, HBM, HBM],
        [
            ((22, 32, 512), F32), ((7, 22, 16, 512), F32), (square, BF16), (square, BF16),
            (square, F32), (square, BF16), ((512, 512), F32), (square, F32), ((512, 512), BF16),
            ((512, 2048), BF16), (long, F32), (long, BF16),
            ((512, 512), F32), ((3, 512, 512), BF16), ((2112, 512), BF16), ((64, 512), F32),
            ((7,), None),
        ],
        [at, ext, kern, gain, b_up, d_out, order, w_up, d_act],
        20000000000,
    )


def run_rims(d_cells, kern):
    return local_call(
        rim_kernel,
        "rims",
        [((22, 24, 512), F32), ((3, 32, 512), BF16), ((3, 32, 512), BF16)],
        [VMEM] * 2,
        [VMEM] * 3,
        [((7, 16, 24, 512), F32)],
        [d_cells, kern],
        5000000000,
    )


def run_sum(kernel, shapes, operands, name, scalars=0, scratch=()):
    return local_call(
        kernel, name, shapes, [SMEM] * scalars + [VMEM] * (len(operands) - scalars),
        [VMEM] * len(shapes), scratch, operands, 800000000,
    )


def two_terms(value):
    high = value.astype(BF16)
    return high, (value - high.astype(F32)).astype(BF16)


def rounded(high, low):
    return high.astype(F32) + low.astype(F32)


def whole(first, rest, rows):
    a, b, c = [ref[rows, :].astype(F32) for ref in rest]
    return (first + a) + (b + c)


def whole_terms(first, refs, at):
    a, b, c = [rounded(ref[at : at + 32, :], ref[at + 32 : at + 64, :]) for ref in refs]
    return (first + a) + (b + c)


def first_sum_kernel(mine_ref, keep_ref, given_ref, half_ref, own_ref, terms_ref, *give_refs):
    own_ref[...] = mine_ref[...] + given_ref[0:512, :].astype(F32)
    half = half_ref[...] + rounded(given_ref[2048:2080, :], given_ref[2080:2112, :])
    high, low = two_terms(half)
    terms_ref[...] = rounded(high, low)
    for k in range(3):
        for part in range(2):
            at = part * 256
            rows = slice(k * 512 + 512 + at, k * 512 + 768 + at)
            total = keep_ref[k, at : at + 256, :].astype(F32) + given_ref[rows, :].astype(F32)
            give_refs[part * 3 + k][0:256, :] = total.astype(BF16)
        give_refs[k][256:288, :] = high
        give_refs[k][288:320, :] = low


def second_sum_kernel(own_ref, terms_ref, *refs):
    down, up, outs = refs[:3], refs[3:6], refs[6:]
    large_ref, next_ref, over_y, over_x = outs[0], outs[1], outs[2:5], outs[5:8]
    high, low = two_terms(whole_terms(terms_ref[...], down, 256))
    next_ref[...] = rounded(high, low)
    for k in range(4):
        rows = slice(k * 64, k * 64 + 64)
        total = whole(own_ref[rows, :], down, rows)
        if k == 0:
            large_ref[0:64, :] = total
        else:
            over_y[k - 1][0:64, :] = total.astype(BF16)
            over_y[k - 1][64:96, :] = high
            over_y[k - 1][96:128, :] = low
        for t in range(4):
            at = t * 64 + k * 16
            total = whole(own_ref[256 + at : 272 + at, :], up, slice(at, at + 16))
            if k == 0:
                large_ref[64 + t * 16 : 80 + t * 16, :] = total
            else:
                over_x[k - 1][t * 16 : t * 16 + 16, :] = total.astype(BF16)


def third_sum_kernel(at_ref, large_ref, terms_ref, *refs):
    over_y, over_x = refs[:3], refs[3:6]
    own_ref, half_ref, give_refs, blocks = refs[6], refs[7], refs[8:11], refs[11]
    low_bits = at_ref[3] & 3
    high, low = two_terms(whole_terms(terms_ref[...], over_y, 64))
    half_ref[...] = rounded(high, low)
    down = whole(large_ref[0:64, :], over_y, slice(0, 64))
    up = whole(large_ref[64:128, :], over_x, slice(0, 64))
    for z in range(8):
        rows = [up[t * 16 + z * 2 : t * 16 + z * 2 + 2] for t in range(4)]
        blocks[z] = jnp.concatenate([down[z * 8 : z * 8 + 8]] + rows, axis=0)
    for k in range(4):
        for z_high in range(2):
            block = blocks[z_high * 4 + (low_bits ^ k)]
            rows = slice(z_high * 16, z_high * 16 + 16)
            if k == 0:
                own_ref[rows, :] = block
            else:
                give_refs[k - 1][rows, :] = block.astype(BF16)
        if k:
            give_refs[k - 1][32:64, :] = high
            give_refs[k - 1][64:96, :] = low


def fourth_sum_kernel(at_ref, own_ref, half_ref, a_ref, b_ref, c_ref, keep_ref, sum_ref, give_ref):
    high = at_ref[3] >> 2
    refs = (a_ref, b_ref, c_ref)
    half = whole_terms(half_ref[...], refs, 32)
    first = whole(own_ref[0:16, :], refs, slice(0, 16))
    second = whole(own_ref[16:32, :], refs, slice(16, 32))
    keep_ref[...] = jnp.where(high == 0, first, second)
    give_ref[0:16, :] = jnp.where(high == 0, second, first)
    give_ref[16:48, :] = half
    sum_ref[...] = half


def last_sum_kernel(keep_ref, half_ref, got_ref, down_ref, up_ref, sum_ref):
    sum_ref[...] = half_ref[...] + got_ref[16:48, :]
    down_ref[...] = keep_ref[0:8, :] + got_ref[0:8, :]
    up = keep_ref[8:16, :] + got_ref[8:16, :]
    for t in range(4):
        up_ref[:, t * 512 : t * 512 + 512] = up[t * 2 : t * 2 + 2]


def per_device(
    field, cotangent, land_sea, fold_partner, depth_kernel, norm_gain, w_up, b_up, w_down
):
    width_lon, width_lat, channels = field.shape
    lon_at = lax.axis_index("lon")
    lat_at = lax.axis_index("lat")
    core = lon_at & 1
    z_at = (lon_at >> 1) & 7
    y_at = ((lat_at >> 2) << 1) + (lon_at >> 4)
    x_at = lat_at & 3
    is_north = lat_at == lax.axis_size("lat") - 1
    from_end = 511 - fold_partner[0]
    turn = 31 - (from_end >> 4)
    shift = 16 - (from_end & 15)
    even = (turn & 1) == 0

    top_rows = field[:, width_lat - 3 :, :]
    mine = mirror_tiles(top_rows, turn >> 1)
    south = to_north(top_rows)
    north = to_south(field[:, 0:3, :])
    low = jnp.where(even, to_previous(mine), mine)
    high = jnp.where(even, mine, to_next(mine))
    fold = lax.dynamic_slice_in_dim(jnp.concatenate([low, high], axis=0), shift, 16, axis=0)
    north = jnp.where(is_north, fold[::-1, ::-1, :], north)
    column = jnp.concatenate([south, field, north], axis=1)
    extended = jnp.concatenate(
        [to_next(column[width_lon - 3 :]), column, to_previous(column[:3])], axis=0
    )
    extended = jnp.pad(extended, ((0, 0), (0, 10), (0, 0)))
    tokens = width_lon * width_lat
    d_out = cotangent.reshape(tokens, channels) * land_sea.reshape(tokens, 1).astype(jnp.bfloat16)
    d_act = lax.dot_general(
        d_out, w_down, (((1,), (1,)), ((), ())), preferred_element_type=jnp.float32
    )
    row = jnp.arange(512, dtype=jnp.int32)
    block = row >> 1
    y_of = (((block >> 2) & 1) << 1) + (block >> 7)
    goes_to = (
        (((block >> 3) & 1) ^ core) * 256
        + (y_of ^ y_at) * 64
        + ((block & 3) ^ x_at) * 16
        + ((block >> 4) & 7) * 2
        + (row & 1)
    )
    order = (goes_to[:, None] == row[None, :]).astype(jnp.bfloat16)
    at = jnp.stack([core, x_at, y_at, z_at]).astype(jnp.int32)
    gain = norm_gain.reshape(1, channels)
    d_cells, half, mine, keep, give = run_forward(
        at, extended, depth_kernel, gain, w_up, b_up.reshape(1, 2048), d_out, d_act, order
    )

    given = send(give, CORE_MASK)
    own, terms, *give = run_sum(
        first_sum_kernel,
        [((512, 512), F32), ((32, 512), F32)] + [((320, 512), BF16)] * 3 + [((256, 512), BF16)] * 3,
        [mine, keep, given, half],
        "first_sum",
    )
    own, give, d_cells = lax.optimization_barrier((own, give, d_cells))
    taken = [send(piece, mask) for piece, mask in zip(give, X_MASKS + Y_MASKS)]
    grad_ext, west_rim, east_rim = run_rims(d_cells, depth_kernel)
    west_rim, east_rim, taken = lax.optimization_barrier((west_rim, east_rim, taken))
    large, terms, *give = run_sum(
        second_sum_kernel,
        [((128, 512), F32), ((32, 512), F32)] + [((128, 512), BF16)] * 3 + [((64, 512), BF16)] * 3,
        [own, terms, *taken],
        "second_sum",
    )
    taken = [send(piece, mask) for piece, mask in zip(give, Y_MASKS + X_MASKS)]

    rim = jnp.bfloat16
    from_west = to_next(east_rim)[:, :22].astype(F32)
    from_east = to_previous(west_rim)[:, :22].astype(F32)
    by_cols = (
        grad_ext[3:19, :22]
        + jnp.pad(from_west, ((0, 13), (0, 0), (0, 0)))
        + jnp.pad(from_east, ((13, 0), (0, 0), (0, 0)))
    )
    top_rim = by_cols[:, 19:22].astype(rim)
    from_south = to_north(top_rim)
    from_north = to_south(by_cols[:, 0:3].astype(rim))
    strip = jnp.where(is_north, top_rim, jnp.zeros_like(top_rim))[::-1, ::-1, :]
    spread = lax.dynamic_update_slice_in_dim(
        jnp.zeros((32, 3, channels), rim), strip, shift, axis=0
    )
    none = jnp.zeros_like(spread[:16])
    mine = jnp.where(even, spread[16:], spread[:16])
    mine = mine + to_next(jnp.where(even, spread[:16], none))
    mine = mine + to_previous(jnp.where(even, none, spread[16:]))
    own, half, *give = run_sum(
        third_sum_kernel,
        [((32, 512), F32), ((32, 512), F32)] + [((96, 512), BF16)] * 3,
        [at, large, terms, *taken],
        "third_sum",
        scalars=1,
        scratch=[((8, 16, 512), F32)],
    )
    taken = [send(piece, mask) for piece, mask in zip(give, Z_MASKS[:3])]
    keep, half, give = run_sum(
        fourth_sum_kernel,
        [((16, 512), F32), ((32, 512), F32), ((48, 512), F32)],
        [at, own, half, *taken],
        "fourth_sum",
        scalars=1,
    )
    mine, give = lax.optimization_barrier((mine, give))
    from_fold = mirror_tiles(mine, turn >> 1).astype(F32)
    grad_down, grad_up, half = run_sum(
        last_sum_kernel,
        [((8, 512), F32), ((2, 2048), F32), ((32, 512), F32)],
        [keep, half, send(give, Z_MASKS[3])],
        "last_sum",
    )
    other = send(half, CORE_MASK)
    small = jnp.where(
        core == 0,
        jnp.concatenate([half, other], axis=0),
        jnp.concatenate([other, half], axis=0),
    )
    grad_kernel = small[:49]
    grad_gain = small[49]
    grad_bias = small[50:54].reshape(2048)
    owned = by_cols[:, 3:19] + jnp.pad(from_south.astype(F32), ((0, 0), (0, 13), (0, 0)))
    owned = owned + jnp.pad(from_north.astype(F32) + from_fold, ((0, 0), (13, 0), (0, 0)))
    grad_field = (cotangent.astype(F32) + owned).astype(jnp.bfloat16)
    return (grad_field, grad_up, grad_down, grad_kernel, grad_gain, grad_bias)


def solution(mesh):
    placed = (
        P("lon", "lat", None),
        P("lon", "lat", None),
        P("lon", "lat"),
        P(),
        P(),
        P(),
        P(),
        P(),
        P(),
    )
    return jax.shard_map(
        per_device,
        mesh=mesh,
        in_specs=placed,
        out_specs=(
            P("lon", "lat", None),
            P(("lon", "lat"), None),
            P(("lon", "lat"), None),
            P(),
            P(),
            P(),
        ),
        check_vma=False,
    )
```

```python
import jax
import jax.numpy as jnp
from jax import lax
from jax.experimental import pallas as pl
from jax.experimental.pallas import tpu as pltpu
from jax.sharding import PartitionSpec as P

DEVICES = ("lon", "lat")
X_MASKS = (1, 2, 3)
Y_MASKS = (128, 4, 132)
Z_MASKS = (16, 32, 48, 96)
CORE_MASK = 8


def send(value, mask):
    return lax.ppermute(value, DEVICES, [(i, i ^ mask) for i in range(256)])


def to_next(value):
    return lax.ppermute(value, "lon", [(i, (i + 1) % 32) for i in range(32)])


def to_previous(value):
    return lax.ppermute(value, "lon", [((i + 1) % 32, i) for i in range(32)])


def to_north(value):
    return lax.ppermute(value, "lat", [(i, i + 1) for i in range(7)])


def to_south(value):
    return lax.ppermute(value, "lat", [(i + 1, i) for i in range(7)])


def top_to_next(value):
    pairs = [(i * 8 + 7, (i + 1) % 32 * 8 + 7) for i in range(32)]
    return lax.ppermute(value, DEVICES, pairs)


def top_to_previous(value):
    pairs = [((i + 1) % 32 * 8 + 7, i * 8 + 7) for i in range(32)]
    return lax.ppermute(value, DEVICES, pairs)


def mirror_tiles(value, half_turn, others, transfer):
    def branch(k):
        pairs = [(e * 8 + 7, ((2 * k - e) % 32) * 8 + 7) for e in range(32)]
        return lambda v, *rest: (lax.ppermute(v, DEVICES, pairs), *transfer(*rest))

    return lax.switch(half_turn, [branch(k) for k in range(16)], value, *others)


ROOT_2_PI = 0.7978845608028654
CUBIC = 0.044715
F32 = jnp.float32
BF16 = jnp.bfloat16


def spread_rows(ext_ref, wide, shifted):
    wide[...] = ext_ref[...].astype(F32)
    for b in range(7):
        shifted[b] = wide[:, b : b + 16, :]


def forward_kernel(
    at_ref, ext_ref, kern_ref, gain_ref, b_up_ref, d_out_ref, order_hbm, w_up_hbm, d_act_hbm,
    d_cells_hbm, half_ref, own_hbm, keep_hbm, send_hbm,
    wide, shifted, normed, ordered, upper, active, tile, mixed_ref, order_ref, w_up_ref, d_act_ref,
    d_upper_ref, own, keep, give, small_ref, d_cells, sems,
):
    core, x_at, y_at = at_ref[0], at_ref[1], at_ref[2]
    loads = [
        pltpu.make_async_copy(order_hbm, order_ref, sems.at[0]),
        pltpu.make_async_copy(w_up_hbm, w_up_ref, sems.at[1]),
        pltpu.make_async_copy(d_act_hbm, d_act_ref, sems.at[2]),
    ]
    for load in loads:
        load.start()
    spread_rows(ext_ref, wide, shifted)

    def conv_step(step, carry):
        lanes = pl.ds(pl.multiple_of(step * 128, 128), 128)
        totals = [jnp.zeros((16, 128), F32)] * 16
        for b in range(7):
            weights = [kern_ref[a * 7 + b : a * 7 + b + 1, lanes] for a in range(7)]
            for r in range(22):
                cells = shifted[b, r, :, lanes]
                for a in range(max(0, r - 15), min(7, r + 1)):
                    totals[r - a] = totals[r - a] + cells * weights[a]
        for x in range(16):
            mixed_ref[x * 16 : x * 16 + 16, lanes] = totals[x]
        return carry

    lax.fori_loop(0, 4, conv_step, 0)

    def norm_step(step, carry):
        rows = pl.ds(pl.multiple_of(step * 32, 32), 32)
        cells = mixed_ref[rows, :]
        center = cells - jnp.mean(cells, axis=-1, keepdims=True)
        spread = jnp.mean(center * center, axis=-1, keepdims=True)
        normed[rows, :] = (center * lax.rsqrt(spread + 1e-6) * gain_ref[...]).astype(BF16)
        return carry

    lax.fori_loop(0, 8, norm_step, 0)
    for load in loads:
        load.wait()
    ordered[...] = jnp.dot(normed[...], order_ref[...], preferred_element_type=F32).astype(BF16)

    for t in range(4):
        lanes = slice(t * 512, t * 512 + 512)
        upper[...] = jnp.dot(normed[...], w_up_ref[:, lanes], preferred_element_type=F32)

        def gelu_step(step, bias):
            rows = pl.ds(pl.multiple_of(step * 32, 32), 32)
            u = upper[rows, :] + b_up_ref[:, lanes]
            square = u * u
            th = jnp.tanh(ROOT_2_PI * (u + CUBIC * (square * u)))
            half = 0.5 * (1.0 + th)
            active[rows, :] = (u * half).astype(BF16)
            slope = half + (0.5 * ROOT_2_PI) * u * (1.0 - th * th) * (1.0 + (3.0 * CUBIC) * square)
            d_up = (d_act_ref[rows, lanes] * slope).astype(BF16)
            d_upper_ref[rows, lanes] = d_up
            return bias + jnp.sum(d_up.astype(F32), axis=0, keepdims=True)

        small_ref[50 + t : 51 + t, :] = lax.fori_loop(0, 8, gelu_step, jnp.zeros((1, 512), F32))
        tile[...] = lax.dot_general(
            active[...], d_out_ref[...], (((0,), (0,)), ((), ())), preferred_element_type=F32
        )
        for y_hi in range(2):
            k_y = (y_hi * 2 + t // 2) ^ y_at
            for k_x in range(4):
                base = y_hi * 32 + (k_x ^ x_at) * 8
                for mine in range(2):
                    at = base + ((1 - core) if mine == 0 else core) * 64
                    piece = jnp.concatenate(
                        [tile[pl.ds(pl.multiple_of(at + zz * 128, 8), 8), :] for zz in range(4)],
                        axis=0,
                    )
                    at = k_y * 64 + (t % 2) * 32
                    rows = pl.ds(pl.multiple_of(at, 32), 32)
                    if mine == 0:
                        give[pl.ds(pl.multiple_of(k_x * 512 + at, 32), 32), :] = piece.astype(BF16)
                    elif k_x == 0:
                        own[rows, :] = piece
                    else:
                        keep[k_x - 1, rows, :] = piece.astype(BF16)

    for t in range(4):
        lanes = slice(t * 512, t * 512 + 512)
        tile[...] = lax.dot_general(
            ordered[...], d_upper_ref[:, lanes], (((0,), (0,)), ((), ())),
            preferred_element_type=F32,
        )
        at = 256 + t * 64
        own[at : at + 64, :] = tile[0:64, :]
        for k in range(4):
            piece = tile[256 + k * 64 : 320 + k * 64, :]
            give[k * 512 + at : k * 512 + at + 64, :] = piece.astype(BF16)
            if k:
                keep[k - 1, at : at + 64, :] = tile[k * 64 : k * 64 + 64, :].astype(BF16)
    stores = [
        pltpu.make_async_copy(give.at[0:2048], send_hbm.at[0:2048], sems.at[3]),
        pltpu.make_async_copy(keep, keep_hbm, sems.at[4]),
        pltpu.make_async_copy(own, own_hbm, sems.at[5]),
    ]
    for store in stores:
        store.start()
    upper[...] = lax.dot_general(
        d_upper_ref[...], w_up_ref[...], (((1,), (1,)), ((), ())), preferred_element_type=F32
    )

    def norm_step(step, gain_sum):
        rows = pl.ds(pl.multiple_of(step * 32, 32), 32)
        cells = mixed_ref[rows, :]
        center = cells - jnp.mean(cells, axis=-1, keepdims=True)
        spread = jnp.mean(center * center, axis=-1, keepdims=True)
        inverse = lax.rsqrt(spread + 1e-6)
        unit = center * inverse
        d = upper[rows, :]
        d_unit = d * gain_ref[...]
        along = jnp.mean(d_unit * unit, axis=-1, keepdims=True)
        d_center = (d_unit - unit * along) * inverse
        d_mixed = d_center - jnp.mean(d_center, axis=-1, keepdims=True)
        d_cells[pl.ds(step * 2, 2)] = d_mixed.reshape(2, 16, 512)
        return gain_sum + jnp.sum(d * unit, axis=0, keepdims=True)

    small_ref[49:50, :] = lax.fori_loop(0, 8, norm_step, jnp.zeros((1, 512), F32))
    small_ref[54:64, :] = jnp.zeros((10, 512), F32)
    stores.append(pltpu.make_async_copy(d_cells, d_cells_hbm, sems.at[7]))
    stores[-1].start()

    def tap_step(step, carry):
        lanes = pl.ds(pl.multiple_of(step * 128, 128), 128)
        d = [d_cells[x, :, lanes] for x in range(16)]
        for b in range(7):
            totals = [jnp.zeros((8, 128), F32)] * 7
            for r in range(22):
                cells = shifted[b, r, :, lanes]
                for a in range(max(0, r - 15), min(7, r + 1)):
                    product = cells * d[r - a]
                    totals[a] = totals[a] + product[:8] + product[8:]
            for a in range(7):
                row = a * 7 + b
                small_ref[row : row + 1, lanes] = jnp.sum(totals[a], axis=0, keepdims=True)
        return carry

    lax.fori_loop(0, 4, tap_step, 0)

    half_ref[...] = small_ref[pl.ds(pl.multiple_of(core * 32, 32), 32), :]
    high, low = two_terms(small_ref[pl.ds(pl.multiple_of((1 - core) * 32, 32), 32), :])
    give[2048:2080, :] = high
    give[2080:2112, :] = low
    stores.append(
        pltpu.make_async_copy(give.at[2048:2112], send_hbm.at[2048:2112], sems.at[6])
    )
    stores[-1].start()
    for store in stores:
        store.wait()


def rim_kernel(d_cells, kern_ref, grad_ref, west_ref, east_ref, moved):
    moved[...] = jnp.zeros_like(moved)
    for b in range(7):
        moved[b, :, b : b + 16, :] = d_cells[...]

    def rim_step(step, carry):
        lanes = pl.ds(pl.multiple_of(step * 128, 128), 128)
        for q in range(3):
            rows = slice(q * 8, q * 8 + 8)
            totals = [jnp.zeros((8, 128), F32)] * 22
            for b in range(1 if q == 2 else 0, 7):
                weights = [kern_ref[a * 7 + b : a * 7 + b + 1, lanes] for a in range(7)]
                for x in range(16):
                    cells = moved[b, x, rows, lanes]
                    for a in range(7):
                        totals[x + a] = totals[x + a] + cells * weights[a]
            for i in range(22):
                grad_ref[i, rows, lanes] = totals[i]
        return carry

    lax.fori_loop(0, 4, rim_step, 0)
    filler = jnp.zeros((3, 8, 512), F32)
    west_ref[...] = jnp.concatenate([grad_ref[0:3], filler], axis=1).astype(BF16)
    east_ref[...] = jnp.concatenate([grad_ref[19:22], filler], axis=1).astype(BF16)


VMEM_BYTES = 56 * 1024 * 1024
VMEM = pl.BlockSpec(memory_space=pltpu.VMEM)
SMEM = pl.BlockSpec(memory_space=pltpu.SMEM)
HBM = pl.BlockSpec(memory_space=pl.ANY)


def local_call(kernel, name, shapes, in_specs, out_specs, scratch, operands, flops):
    return pl.pallas_call(
        kernel,
        out_shape=[jax.ShapeDtypeStruct(s, d) for s, d in shapes],
        in_specs=in_specs,
        out_specs=out_specs,
        scratch_shapes=[pltpu.VMEM(s, d) if d else pltpu.SemaphoreType.DMA(s) for s, d in scratch],
        compiler_params=pltpu.CompilerParams(vmem_limit_bytes=VMEM_BYTES),
        cost_estimate=pl.CostEstimate(flops=flops, bytes_accessed=2000000, transcendentals=0),
        name=name,
    )(*operands)


def run_forward(at, ext, kern, gain, w_up, b_up, d_out, d_act, order):
    square, long = (256, 512), (256, 2048)
    return local_call(
        forward_kernel,
        "forward",
        [
            ((16, 16, 512), F32), ((32, 512), F32),
            ((512, 512), F32), ((3, 512, 512), BF16), ((2112, 512), BF16),
        ],
        [SMEM] + [VMEM] * 5 + [HBM] * 3,
        [HBM, VMEM, HBM, HBM, HBM],
        [
            ((22, 32, 512), F32), ((7, 22, 16, 512), F32), (square, BF16), (square, BF16),
            (square, F32), (square, BF16), ((512, 512), F32), (square, F32), ((512, 512), BF16),
            ((512, 2048), BF16), (long, F32), (long, BF16),
            ((512, 512), F32), ((3, 512, 512), BF16), ((2112, 512), BF16), ((64, 512), F32),
            ((16, 16, 512), F32), ((8,), None),
        ],
        [at, ext, kern, gain, b_up, d_out, order, w_up, d_act],
        20000000000,
    )


def run_rims(d_cells, kern):
    return local_call(
        rim_kernel,
        "rims",
        [((22, 24, 512), F32), ((3, 32, 512), BF16), ((3, 32, 512), BF16)],
        [VMEM] * 2,
        [VMEM] * 3,
        [((7, 16, 24, 512), F32)],
        [d_cells, kern],
        5000000000,
    )


def run_sum(kernel, shapes, operands, name, scalars=0, scratch=()):
    return local_call(
        kernel, name, shapes, [SMEM] * scalars + [VMEM] * (len(operands) - scalars),
        [VMEM] * len(shapes), scratch, operands, 800000000,
    )


def two_terms(value):
    high = value.astype(BF16)
    return high, (value - high.astype(F32)).astype(BF16)


def rounded(high, low):
    return high.astype(F32) + low.astype(F32)


def whole(first, rest, rows):
    a, b, c = [ref[rows, :].astype(F32) for ref in rest]
    return (first + a) + (b + c)


def whole_terms(first, refs, at):
    a, b, c = [rounded(ref[at : at + 32, :], ref[at + 32 : at + 64, :]) for ref in refs]
    return (first + a) + (b + c)


def first_sum_kernel(mine_ref, keep_ref, given_ref, half_ref, own_ref, terms_ref, *give_refs):
    own_ref[...] = mine_ref[...] + given_ref[0:512, :].astype(F32)
    half = half_ref[...] + rounded(given_ref[2048:2080, :], given_ref[2080:2112, :])
    high, low = two_terms(half)
    terms_ref[...] = rounded(high, low)
    for k in range(3):
        for part in range(2):
            at = part * 256
            rows = slice(k * 512 + 512 + at, k * 512 + 768 + at)
            total = keep_ref[k, at : at + 256, :].astype(F32) + given_ref[rows, :].astype(F32)
            give_refs[part * 3 + k][0:256, :] = total.astype(BF16)
        give_refs[k][256:288, :] = high
        give_refs[k][288:320, :] = low


def second_sum_kernel(own_ref, terms_ref, *refs):
    down, up, outs = refs[:3], refs[3:6], refs[6:]
    large_ref, next_ref, over_y, over_x = outs[0], outs[1], outs[2:5], outs[5:8]
    high, low = two_terms(whole_terms(terms_ref[...], down, 256))
    next_ref[...] = rounded(high, low)
    for k in range(4):
        rows = slice(k * 64, k * 64 + 64)
        total = whole(own_ref[rows, :], down, rows)
        if k == 0:
            large_ref[0:64, :] = total
        else:
            over_y[k - 1][0:64, :] = total.astype(BF16)
            over_y[k - 1][64:96, :] = high
            over_y[k - 1][96:128, :] = low
        for t in range(4):
            at = t * 64 + k * 16
            total = whole(own_ref[256 + at : 272 + at, :], up, slice(at, at + 16))
            if k == 0:
                large_ref[64 + t * 16 : 80 + t * 16, :] = total
            else:
                over_x[k - 1][t * 16 : t * 16 + 16, :] = total.astype(BF16)


def third_sum_kernel(at_ref, large_ref, terms_ref, *refs):
    over_y, over_x = refs[:3], refs[3:6]
    own_ref, half_ref, give_refs, blocks = refs[6], refs[7], refs[8:11], refs[11]
    z_at = at_ref[3]
    high, low = two_terms(whole_terms(terms_ref[...], over_y, 64))
    half_ref[...] = rounded(high, low)
    down = whole(large_ref[0:64, :], over_y, slice(0, 64))
    up = whole(large_ref[64:128, :], over_x, slice(0, 64))
    for z in range(8):
        rows = [up[t * 16 + z * 2 : t * 16 + z * 2 + 2] for t in range(4)]
        blocks[z] = jnp.concatenate([down[z * 8 : z * 8 + 8]] + rows, axis=0)
    for k in range(4):
        for part in range(2):
            block = blocks[z_at ^ k ^ (part * 6)]
            rows = slice(part * 16, part * 16 + 16)
            if k == 0:
                own_ref[rows, :] = block
            else:
                give_refs[k - 1][rows, :] = block.astype(BF16)
        if k:
            give_refs[k - 1][32:64, :] = high
            give_refs[k - 1][64:96, :] = low


def fourth_sum_kernel(own_ref, half_ref, a_ref, b_ref, c_ref, keep_ref, sum_ref, give_ref):
    refs = (a_ref, b_ref, c_ref)
    half = whole_terms(half_ref[...], refs, 32)
    keep_ref[...] = whole(own_ref[0:16, :], refs, slice(0, 16))
    give_ref[0:16, :] = whole(own_ref[16:32, :], refs, slice(16, 32))
    give_ref[16:48, :] = half
    sum_ref[...] = half


def last_sum_kernel(keep_ref, half_ref, got_ref, down_ref, up_ref, sum_ref):
    sum_ref[...] = half_ref[...] + got_ref[16:48, :]
    down_ref[...] = keep_ref[0:8, :] + got_ref[0:8, :]
    up = keep_ref[8:16, :] + got_ref[8:16, :]
    for t in range(4):
        up_ref[:, t * 512 : t * 512 + 512] = up[t * 2 : t * 2 + 2]


def split_kernel(at_ref, half_ref, other_ref, kernel_ref, gain_ref, bias_ref):
    first = at_ref[0] == 0
    half, other = half_ref[...], other_ref[...]
    low, high = jnp.where(first, half, other), jnp.where(first, other, half)
    kernel_ref[0:32, :] = low
    kernel_ref[32:49, :] = high[0:17]
    gain_ref[...] = high[17:18]
    for t in range(4):
        bias_ref[:, t * 512 : t * 512 + 512] = high[18 + t : 19 + t]


def per_device(
    field, cotangent, land_sea, fold_partner, depth_kernel, norm_gain, w_up, b_up, w_down
):
    width_lon, width_lat, channels = field.shape
    lon_at = lax.axis_index("lon")
    lat_at = lax.axis_index("lat")
    core = lon_at & 1
    z_at = (lon_at >> 1) & 7
    y_at = ((lat_at >> 2) << 1) + (lon_at >> 4)
    x_at = lat_at & 3
    is_north = lat_at == lax.axis_size("lat") - 1
    from_end = 511 - fold_partner[0]
    turn = 31 - (from_end >> 4)
    shift = 16 - (from_end & 15)
    even = (turn & 1) == 0

    top_rows = field[:, width_lat - 3 :, :]
    mine, south, north = mirror_tiles(
        top_rows, turn >> 1, (top_rows, field[:, 0:3, :]), lambda a, b: (to_north(a), to_south(b))
    )
    low = jnp.where(even, top_to_previous(mine), mine)
    high = jnp.where(even, mine, top_to_next(mine))
    fold = lax.dynamic_slice_in_dim(jnp.concatenate([low, high], axis=0), shift, 16, axis=0)
    north = jnp.where(is_north, fold[::-1, ::-1, :], north)
    column = jnp.concatenate([south, field, north], axis=1)
    last, first, cotangent, core = lax.optimization_barrier(
        (column[width_lon - 3 :], column[:3], cotangent, core)
    )
    extended = jnp.concatenate([to_next(last), column, to_previous(first)], axis=0)
    extended = jnp.pad(extended, ((0, 0), (0, 10), (0, 0)))
    tokens = width_lon * width_lat
    d_out = cotangent.reshape(tokens, channels) * land_sea.reshape(tokens, 1).astype(jnp.bfloat16)
    d_act = lax.dot_general(
        d_out, w_down, (((1,), (1,)), ((), ())), preferred_element_type=jnp.float32
    )
    row = jnp.arange(512, dtype=jnp.int32)
    block = row >> 1
    y_of = (((block >> 2) & 1) << 1) + (block >> 7)
    goes_to = (
        (((block >> 3) & 1) ^ core) * 256
        + (y_of ^ y_at) * 64
        + ((block & 3) ^ x_at) * 16
        + ((block >> 4) & 7) * 2
        + (row & 1)
    )
    order = (goes_to[:, None] == row[None, :]).astype(jnp.bfloat16)
    at = jnp.stack([core, x_at, y_at, z_at]).astype(jnp.int32)
    gain = norm_gain.reshape(1, channels)
    d_cells, half, mine, keep, give = run_forward(
        at, extended, depth_kernel, gain, w_up, b_up.reshape(1, 2048), d_out, d_act, order
    )

    given = send(give, CORE_MASK)
    own, terms, *give = run_sum(
        first_sum_kernel,
        [((512, 512), F32), ((32, 512), F32)] + [((320, 512), BF16)] * 3 + [((256, 512), BF16)] * 3,
        [mine, keep, given, half],
        "first_sum",
    )
    own, give, d_cells = lax.optimization_barrier((own, give, d_cells))
    taken = [send(piece, mask) for piece, mask in zip(give, X_MASKS + Y_MASKS)]
    grad_ext, west_rim, east_rim = run_rims(d_cells, depth_kernel)
    west_rim, east_rim, taken = lax.optimization_barrier((west_rim, east_rim, taken))
    large, terms, *give = run_sum(
        second_sum_kernel,
        [((128, 512), F32), ((32, 512), F32)] + [((128, 512), BF16)] * 3 + [((64, 512), BF16)] * 3,
        [own, terms, *taken],
        "second_sum",
    )
    taken = [send(piece, mask) for piece, mask in zip(give, Y_MASKS + X_MASKS)]

    rim = jnp.bfloat16
    from_west = to_next(east_rim)[:, :22].astype(F32)
    from_east = to_previous(west_rim)[:, :22].astype(F32)
    by_cols = (
        grad_ext[3:19, :22]
        + jnp.pad(from_west, ((0, 13), (0, 0), (0, 0)))
        + jnp.pad(from_east, ((13, 0), (0, 0), (0, 0)))
    )
    top_rim = by_cols[:, 19:22].astype(rim)
    from_south = to_north(top_rim)
    from_north = to_south(by_cols[:, 0:3].astype(rim))
    strip = jnp.where(is_north, top_rim, jnp.zeros_like(top_rim))[::-1, ::-1, :]
    spread = lax.dynamic_update_slice_in_dim(
        jnp.zeros((32, 3, channels), rim), strip, shift, axis=0
    )
    none = jnp.zeros_like(spread[:16])
    mine = jnp.where(even, spread[16:], spread[:16])
    mine = mine + top_to_next(jnp.where(even, spread[:16], none))
    mine = mine + top_to_previous(jnp.where(even, none, spread[16:]))

    own, half, *give = run_sum(
        third_sum_kernel,
        [((32, 512), F32), ((32, 512), F32)] + [((96, 512), BF16)] * 3,
        [at, large, terms, *taken],
        "third_sum",
        scalars=1,
        scratch=[((8, 16, 512), F32)],
    )
    taken = [send(piece, mask) for piece, mask in zip(give, Z_MASKS[:3])]
    keep, half, give = run_sum(
        fourth_sum_kernel,
        [((16, 512), F32), ((32, 512), F32), ((48, 512), F32)],
        [own, half, *taken],
        "fourth_sum",
    )
    from_fold, got = mirror_tiles(mine, turn >> 1, (give,), lambda v: (send(v, Z_MASKS[3]),))
    from_fold = from_fold.astype(F32)
    grad_down, grad_up, half = run_sum(
        last_sum_kernel,
        [((8, 512), F32), ((2, 2048), F32), ((32, 512), F32)],
        [keep, half, got],
        "last_sum",
    )
    other = send(half, CORE_MASK)
    grad_kernel, grad_gain, grad_bias = run_sum(
        split_kernel,
        [((49, 512), F32), ((1, 512), F32), ((1, 2048), F32)],
        [at, half, other],
        "split",
        scalars=1,
    )
    grad_gain = grad_gain.reshape(512)
    grad_bias = grad_bias.reshape(2048)
    owned = by_cols[:, 3:19] + jnp.pad(from_south.astype(F32), ((0, 0), (0, 13), (0, 0)))
    owned = owned + jnp.pad(from_north.astype(F32) + from_fold, ((0, 0), (13, 0), (0, 0)))
    grad_field = (cotangent.astype(F32) + owned).astype(jnp.bfloat16)
    return (grad_field, grad_up, grad_down, grad_kernel, grad_gain, grad_bias)


def solution(mesh):
    placed = (
        P("lon", "lat", None),
        P("lon", "lat", None),
        P("lon", "lat"),
        P(),
        P(),
        P(),
        P(),
        P(),
        P(),
    )
    return jax.shard_map(
        per_device,
        mesh=mesh,
        in_specs=placed,
        out_specs=(
            P("lon", "lat", None),
            P(("lon", "lat"), None),
            P(("lon", "lat"), None),
            P(),
            P(),
            P(),
        ),
        check_vma=False,
    )
```

```python
import jax
import jax.numpy as jnp
from jax import lax
from jax.experimental import pallas as pl
from jax.experimental.pallas import tpu as pltpu
from jax.sharding import PartitionSpec as P

DEVICES = ("lon", "lat")
X_MASKS = (1, 2, 3)
Y_MASKS = (128, 4, 132)
Z_MASKS = (16, 32, 48, 96)
CORE_MASK = 8


def send(value, mask):
    return lax.ppermute(value, DEVICES, [(i, i ^ mask) for i in range(256)])


def to_next(value):
    return lax.ppermute(value, "lon", [(i, (i + 1) % 32) for i in range(32)])


def to_previous(value):
    return lax.ppermute(value, "lon", [((i + 1) % 32, i) for i in range(32)])


def to_north(value):
    return lax.ppermute(value, "lat", [(i, i + 1) for i in range(7)])


def to_south(value):
    return lax.ppermute(value, "lat", [(i + 1, i) for i in range(7)])


def top_to_next(value):
    pairs = [(i * 8 + 7, (i + 1) % 32 * 8 + 7) for i in range(32)]
    return lax.ppermute(value, DEVICES, pairs)


def top_to_previous(value):
    pairs = [((i + 1) % 32 * 8 + 7, i * 8 + 7) for i in range(32)]
    return lax.ppermute(value, DEVICES, pairs)


def mirror_tiles(value, half_turn, others, transfer):
    def branch(k):
        pairs = [(e * 8 + 7, ((2 * k - e) % 32) * 8 + 7) for e in range(32)]
        return lambda v, *rest: (lax.ppermute(v, DEVICES, pairs), *transfer(*rest))

    return lax.switch(half_turn, [branch(k) for k in range(16)], value, *others)


ROOT_2_PI = 0.7978845608028654
CUBIC = 0.044715
F32 = jnp.float32
BF16 = jnp.bfloat16


def spread_rows(ext_ref, wide, shifted):
    wide[...] = ext_ref[...].astype(F32)
    for b in range(7):
        shifted[b] = wide[:, b : b + 16, :]


def forward_kernel(
    at_ref, ext_ref, kern_ref, gain_ref, b_up_ref, d_out_ref, order_hbm, w_up_hbm, d_act_hbm,
    d_cells_hbm, half_ref, own_hbm, keep_hbm, send_hbm,
    wide, shifted, normed, ordered, upper, active, tile, mixed_ref, order_ref, w_up_ref, d_act_ref,
    d_upper_ref, own, keep, give, small_ref, d_cells, sems,
):
    core, x_at, y_at = at_ref[0], at_ref[1], at_ref[2]
    loads = [
        pltpu.make_async_copy(order_hbm, order_ref, sems.at[0]),
        pltpu.make_async_copy(w_up_hbm, w_up_ref, sems.at[1]),
        pltpu.make_async_copy(d_act_hbm, d_act_ref, sems.at[2]),
    ]
    for load in loads:
        load.start()
    spread_rows(ext_ref, wide, shifted)

    def conv_step(step, carry):
        lanes = pl.ds(pl.multiple_of(step * 128, 128), 128)
        totals = [jnp.zeros((16, 128), F32)] * 16
        for b in range(7):
            weights = [kern_ref[a * 7 + b : a * 7 + b + 1, lanes] for a in range(7)]
            for r in range(22):
                cells = shifted[b, r, :, lanes]
                for a in range(max(0, r - 15), min(7, r + 1)):
                    totals[r - a] = totals[r - a] + cells * weights[a]
        for x in range(16):
            mixed_ref[x * 16 : x * 16 + 16, lanes] = totals[x]
        return carry

    lax.fori_loop(0, 4, conv_step, 0)

    def norm_step(step, carry):
        rows = pl.ds(pl.multiple_of(step * 32, 32), 32)
        cells = mixed_ref[rows, :]
        center = cells - jnp.mean(cells, axis=-1, keepdims=True)
        spread = jnp.mean(center * center, axis=-1, keepdims=True)
        normed[rows, :] = (center * lax.rsqrt(spread + 1e-6) * gain_ref[...]).astype(BF16)
        return carry

    lax.fori_loop(0, 8, norm_step, 0)
    for load in loads:
        load.wait()
    ordered[...] = jnp.dot(normed[...], order_ref[...], preferred_element_type=F32).astype(BF16)

    for t in range(4):
        lanes = slice(t * 512, t * 512 + 512)
        upper[...] = jnp.dot(normed[...], w_up_ref[:, lanes], preferred_element_type=F32)

        def gelu_step(step, bias):
            rows = pl.ds(pl.multiple_of(step * 32, 32), 32)
            u = upper[rows, :] + b_up_ref[:, lanes]
            square = u * u
            th = jnp.tanh(ROOT_2_PI * (u + CUBIC * (square * u)))
            half = 0.5 * (1.0 + th)
            active[rows, :] = (u * half).astype(BF16)
            slope = half + (0.5 * ROOT_2_PI) * u * (1.0 - th * th) * (1.0 + (3.0 * CUBIC) * square)
            d_up = (d_act_ref[rows, lanes] * slope).astype(BF16)
            d_upper_ref[rows, lanes] = d_up
            return bias + jnp.sum(d_up.astype(F32), axis=0, keepdims=True)

        small_ref[50 + t : 51 + t, :] = lax.fori_loop(0, 8, gelu_step, jnp.zeros((1, 512), F32))
        tile[...] = lax.dot_general(
            active[...], d_out_ref[...], (((0,), (0,)), ((), ())), preferred_element_type=F32
        )
        for y_hi in range(2):
            k_y = (y_hi * 2 + t // 2) ^ y_at
            for k_x in range(4):
                base = y_hi * 32 + (k_x ^ x_at) * 8
                for mine in range(2):
                    at = base + ((1 - core) if mine == 0 else core) * 64
                    piece = jnp.concatenate(
                        [tile[pl.ds(pl.multiple_of(at + zz * 128, 8), 8), :] for zz in range(4)],
                        axis=0,
                    )
                    at = k_y * 64 + (t % 2) * 32
                    rows = pl.ds(pl.multiple_of(at, 32), 32)
                    if mine == 0:
                        give[pl.ds(pl.multiple_of(k_x * 512 + at, 32), 32), :] = piece.astype(BF16)
                    elif k_x == 0:
                        own[rows, :] = piece
                    else:
                        keep[k_x - 1, rows, :] = piece.astype(BF16)

    for t in range(4):
        lanes = slice(t * 512, t * 512 + 512)
        tile[...] = lax.dot_general(
            ordered[...], d_upper_ref[:, lanes], (((0,), (0,)), ((), ())),
            preferred_element_type=F32,
        )
        at = 256 + t * 64
        own[at : at + 64, :] = tile[0:64, :]
        for k in range(4):
            piece = tile[256 + k * 64 : 320 + k * 64, :]
            give[k * 512 + at : k * 512 + at + 64, :] = piece.astype(BF16)
            if k:
                keep[k - 1, at : at + 64, :] = tile[k * 64 : k * 64 + 64, :].astype(BF16)
    stores = [
        pltpu.make_async_copy(give.at[0:2048], send_hbm.at[0:2048], sems.at[3]),
        pltpu.make_async_copy(keep, keep_hbm, sems.at[4]),
        pltpu.make_async_copy(own, own_hbm, sems.at[5]),
    ]
    for store in stores:
        store.start()
    upper[...] = lax.dot_general(
        d_upper_ref[...], w_up_ref[...], (((1,), (1,)), ((), ())), preferred_element_type=F32
    )

    def norm_step(step, gain_sum):
        rows = pl.ds(pl.multiple_of(step * 32, 32), 32)
        cells = mixed_ref[rows, :]
        center = cells - jnp.mean(cells, axis=-1, keepdims=True)
        spread = jnp.mean(center * center, axis=-1, keepdims=True)
        inverse = lax.rsqrt(spread + 1e-6)
        unit = center * inverse
        d = upper[rows, :]
        d_unit = d * gain_ref[...]
        along = jnp.mean(d_unit * unit, axis=-1, keepdims=True)
        d_center = (d_unit - unit * along) * inverse
        d_mixed = d_center - jnp.mean(d_center, axis=-1, keepdims=True)
        d_cells[pl.ds(step * 2, 2)] = d_mixed.reshape(2, 16, 512)
        return gain_sum + jnp.sum(d * unit, axis=0, keepdims=True)

    small_ref[49:50, :] = lax.fori_loop(0, 8, norm_step, jnp.zeros((1, 512), F32))
    small_ref[54:64, :] = jnp.zeros((10, 512), F32)
    stores.append(pltpu.make_async_copy(d_cells, d_cells_hbm, sems.at[7]))
    stores[-1].start()

    def tap_step(step, carry):
        lanes = pl.ds(pl.multiple_of(step * 128, 128), 128)
        d = [d_cells[x, :, lanes] for x in range(16)]
        for b in range(7):
            totals = [jnp.zeros((8, 128), F32)] * 7
            for r in range(22):
                cells = shifted[b, r, :, lanes]
                for a in range(max(0, r - 15), min(7, r + 1)):
                    product = cells * d[r - a]
                    totals[a] = totals[a] + product[:8] + product[8:]
            for a in range(7):
                row = a * 7 + b
                small_ref[row : row + 1, lanes] = jnp.sum(totals[a], axis=0, keepdims=True)
        return carry

    lax.fori_loop(0, 4, tap_step, 0)

    half_ref[...] = small_ref[pl.ds(pl.multiple_of(core * 32, 32), 32), :]
    high, low = two_terms(small_ref[pl.ds(pl.multiple_of((1 - core) * 32, 32), 32), :])
    give[2048:2080, :] = high
    give[2080:2112, :] = low
    stores.append(
        pltpu.make_async_copy(give.at[2048:2112], send_hbm.at[2048:2112], sems.at[6])
    )
    stores[-1].start()
    for store in stores:
        store.wait()


def rim_kernel(d_cells, kern_ref, grad_ref, west_ref, east_ref, moved):
    moved[...] = jnp.zeros_like(moved)
    for b in range(7):
        moved[b, :, b : b + 16, :] = d_cells[...]

    def rim_step(step, carry):
        lanes = pl.ds(pl.multiple_of(step * 128, 128), 128)
        for q in range(3):
            rows = slice(q * 8, q * 8 + 8)
            totals = [jnp.zeros((8, 128), F32)] * 22
            for b in range(1 if q == 2 else 0, 7):
                weights = [kern_ref[a * 7 + b : a * 7 + b + 1, lanes] for a in range(7)]
                for x in range(16):
                    cells = moved[b, x, rows, lanes]
                    for a in range(7):
                        totals[x + a] = totals[x + a] + cells * weights[a]
            for i in range(22):
                grad_ref[i, rows, lanes] = totals[i]
        return carry

    lax.fori_loop(0, 4, rim_step, 0)
    filler = jnp.zeros((3, 8, 512), F32)
    west_ref[...] = jnp.concatenate([grad_ref[0:3], filler], axis=1).astype(BF16)
    east_ref[...] = jnp.concatenate([grad_ref[19:22], filler], axis=1).astype(BF16)


MIB = 1024 * 1024
VMEM = pl.BlockSpec(memory_space=pltpu.VMEM)
SMEM = pl.BlockSpec(memory_space=pltpu.SMEM)
HBM = pl.BlockSpec(memory_space=pl.ANY)


def local_call(kernel, name, shapes, in_specs, out_specs, scratch, operands, flops, room):
    return pl.pallas_call(
        kernel,
        out_shape=[jax.ShapeDtypeStruct(s, d) for s, d in shapes],
        in_specs=in_specs,
        out_specs=out_specs,
        scratch_shapes=[pltpu.VMEM(s, d) if d else pltpu.SemaphoreType.DMA(s) for s, d in scratch],
        compiler_params=pltpu.CompilerParams(vmem_limit_bytes=room * MIB),
        cost_estimate=pl.CostEstimate(flops=flops, bytes_accessed=2000000, transcendentals=0),
        name=name,
    )(*operands)


def run_forward(at, ext, kern, gain, w_up, b_up, d_out, d_act, order):
    square, long = (256, 512), (256, 2048)
    return local_call(
        forward_kernel,
        "forward",
        [
            ((16, 16, 512), F32), ((32, 512), F32),
            ((512, 512), F32), ((3, 512, 512), BF16), ((2112, 512), BF16),
        ],
        [SMEM] + [VMEM] * 5 + [HBM] * 3,
        [HBM, VMEM, HBM, HBM, HBM],
        [
            ((22, 32, 512), F32), ((7, 22, 16, 512), F32), (square, BF16), (square, BF16),
            (square, F32), (square, BF16), ((512, 512), F32), (square, F32), ((512, 512), BF16),
            ((512, 2048), BF16), (long, F32), (long, BF16),
            ((512, 512), F32), ((3, 512, 512), BF16), ((2112, 512), BF16), ((64, 512), F32),
            ((16, 16, 512), F32), ((8,), None),
        ],
        [at, ext, kern, gain, b_up, d_out, order, w_up, d_act],
        20000000000,
        56,
    )


def run_rims(d_cells, kern):
    return local_call(
        rim_kernel,
        "rims",
        [((22, 24, 512), F32), ((3, 32, 512), BF16), ((3, 32, 512), BF16)],
        [VMEM] * 2,
        [VMEM] * 3,
        [((7, 16, 24, 512), F32)],
        [d_cells, kern],
        5000000000,
        16,
    )


def run_sum(kernel, shapes, operands, name, scalars=0, scratch=(), room=4):
    return local_call(
        kernel, name, shapes, [SMEM] * scalars + [VMEM] * (len(operands) - scalars),
        [VMEM] * len(shapes), scratch, operands, 800000000, room,
    )


def two_terms(value):
    high = value.astype(BF16)
    return high, (value - high.astype(F32)).astype(BF16)


def rounded(high, low):
    return high.astype(F32) + low.astype(F32)


def whole(first, rest, rows):
    a, b, c = [ref[rows, :].astype(F32) for ref in rest]
    return (first + a) + (b + c)


def whole_terms(first, refs, at):
    a, b, c = [rounded(ref[at : at + 32, :], ref[at + 32 : at + 64, :]) for ref in refs]
    return (first + a) + (b + c)


def first_sum_kernel(mine_ref, keep_ref, given_ref, half_ref, own_ref, terms_ref, *give_refs):
    own_ref[...] = mine_ref[...] + given_ref[0:512, :].astype(F32)
    half = half_ref[...] + rounded(given_ref[2048:2080, :], given_ref[2080:2112, :])
    high, low = two_terms(half)
    terms_ref[...] = rounded(high, low)
    for k in range(3):
        rows = slice(k * 512 + 512, k * 512 + 1024)
        total = keep_ref[k].astype(F32) + given_ref[rows, :].astype(F32)
        give_refs[k][0:512, :] = total.astype(BF16)
        give_refs[k][512:544, :] = high
        give_refs[k][544:576, :] = low


def second_sum_kernel(own_ref, terms_ref, a_ref, b_ref, c_ref, large_ref, next_ref, *give_refs):
    refs = (a_ref, b_ref, c_ref)
    high, low = two_terms(whole_terms(terms_ref[...], refs, 512))
    next_ref[...] = rounded(high, low)
    for k in range(4):
        pieces = [(0, k * 64, 64)] + [(64 + t * 16, 256 + t * 64 + k * 16, 16) for t in range(4)]
        for target, at, count in pieces:
            rows = slice(at, at + count)
            total = whole(own_ref[rows, :], refs, rows)
            if k == 0:
                large_ref[target : target + count, :] = total
            else:
                give_refs[k - 1][target : target + count, :] = total.astype(BF16)
        if k:
            give_refs[k - 1][128:160, :] = high
            give_refs[k - 1][160:192, :] = low


def third_sum_kernel(at_ref, large_ref, terms_ref, a_ref, b_ref, c_ref, *outs):
    refs = (a_ref, b_ref, c_ref)
    own_ref, half_ref, give_refs, blocks = outs[0], outs[1], outs[2:5], outs[5]
    z_at = at_ref[3]
    high, low = two_terms(whole_terms(terms_ref[...], refs, 128))
    half_ref[...] = rounded(high, low)
    down = whole(large_ref[0:64, :], refs, slice(0, 64))
    up = whole(large_ref[64:128, :], refs, slice(64, 128))
    for z in range(8):
        rows = [up[t * 16 + z * 2 : t * 16 + z * 2 + 2] for t in range(4)]
        blocks[z] = jnp.concatenate([down[z * 8 : z * 8 + 8]] + rows, axis=0)
    for k in range(4):
        for part in range(2):
            block = blocks[z_at ^ k ^ (part * 6)]
            rows = slice(part * 16, part * 16 + 16)
            if k == 0:
                own_ref[rows, :] = block
            else:
                give_refs[k - 1][rows, :] = block.astype(BF16)
        if k:
            give_refs[k - 1][32:64, :] = high
            give_refs[k - 1][64:96, :] = low


def fourth_sum_kernel(own_ref, half_ref, a_ref, b_ref, c_ref, keep_ref, sum_ref, give_ref):
    refs = (a_ref, b_ref, c_ref)
    half = whole_terms(half_ref[...], refs, 32)
    keep_ref[...] = whole(own_ref[0:16, :], refs, slice(0, 16))
    give_ref[0:16, :] = whole(own_ref[16:32, :], refs, slice(16, 32))
    give_ref[16:48, :] = half
    sum_ref[...] = half


def last_sum_kernel(keep_ref, half_ref, got_ref, down_ref, up_ref, sum_ref):
    sum_ref[...] = half_ref[...] + got_ref[16:48, :]
    down_ref[...] = keep_ref[0:8, :] + got_ref[0:8, :]
    up = keep_ref[8:16, :] + got_ref[8:16, :]
    for t in range(4):
        up_ref[:, t * 512 : t * 512 + 512] = up[t * 2 : t * 2 + 2]


def split_kernel(at_ref, half_ref, other_ref, kernel_ref, gain_ref, bias_ref):
    first = at_ref[0] == 0
    half, other = half_ref[...], other_ref[...]
    low, high = jnp.where(first, half, other), jnp.where(first, other, half)
    kernel_ref[0:32, :] = low
    kernel_ref[32:49, :] = high[0:17]
    gain_ref[...] = high[17:18]
    for t in range(4):
        bias_ref[:, t * 512 : t * 512 + 512] = high[18 + t : 19 + t]


def per_device(
    field, cotangent, land_sea, fold_partner, depth_kernel, norm_gain, w_up, b_up, w_down
):
    width_lon, width_lat, channels = field.shape
    lon_at = lax.axis_index("lon")
    lat_at = lax.axis_index("lat")
    core = lon_at & 1
    z_at = (lon_at >> 1) & 7
    y_at = ((lat_at >> 2) << 1) + (lon_at >> 4)
    x_at = lat_at & 3
    is_north = lat_at == lax.axis_size("lat") - 1
    from_end = 511 - fold_partner[0]
    turn = 31 - (from_end >> 4)
    shift = 16 - (from_end & 15)
    even = (turn & 1) == 0

    top_rows = field[:, width_lat - 3 :, :]
    mine, south, north = mirror_tiles(
        top_rows, turn >> 1, (top_rows, field[:, 0:3, :]), lambda a, b: (to_north(a), to_south(b))
    )
    low = jnp.where(even, top_to_previous(mine), mine)
    high = jnp.where(even, mine, top_to_next(mine))
    fold = lax.dynamic_slice_in_dim(jnp.concatenate([low, high], axis=0), shift, 16, axis=0)
    north = jnp.where(is_north, fold[::-1, ::-1, :], north)
    column = jnp.concatenate([south, field, north], axis=1)
    extended = jnp.concatenate(
        [to_next(column[width_lon - 3 :]), column, to_previous(column[:3])], axis=0
    )
    extended = jnp.pad(extended, ((0, 0), (0, 10), (0, 0)))
    tokens = width_lon * width_lat
    d_out = cotangent.reshape(tokens, channels) * land_sea.reshape(tokens, 1).astype(jnp.bfloat16)
    d_act = lax.dot_general(
        d_out, w_down, (((1,), (1,)), ((), ())), preferred_element_type=jnp.float32
    )
    row = jnp.arange(512, dtype=jnp.int32)
    block = row >> 1
    y_of = (((block >> 2) & 1) << 1) + (block >> 7)
    goes_to = (
        (((block >> 3) & 1) ^ core) * 256
        + ((block & 3) ^ x_at) * 64
        + (y_of ^ y_at) * 16
        + ((block >> 4) & 7) * 2
        + (row & 1)
    )
    order = (goes_to[:, None] == row[None, :]).astype(jnp.bfloat16)
    at = jnp.stack([core, x_at, y_at, z_at]).astype(jnp.int32)
    gain = norm_gain.reshape(1, channels)
    d_cells, half, mine, keep, give = run_forward(
        at, extended, depth_kernel, gain, w_up, b_up.reshape(1, 2048), d_out, d_act, order
    )

    given = send(give, CORE_MASK)
    grad_ext, west_rim, east_rim = run_rims(d_cells, depth_kernel)
    given, west_rim, east_rim = lax.optimization_barrier((given, west_rim, east_rim))
    own, terms, *give = run_sum(
        first_sum_kernel,
        [((512, 512), F32), ((32, 512), F32)] + [((576, 512), BF16)] * 3,
        [mine, keep, given, half],
        "first_sum",
        room=16,
    )
    taken = [send(piece, mask) for piece, mask in zip(give, X_MASKS)]

    rim = jnp.bfloat16
    from_west, from_east = to_next(east_rim), to_previous(west_rim)
    from_west, from_east = from_west[:, :22].astype(F32), from_east[:, :22].astype(F32)
    by_cols = (
        grad_ext[3:19, :22]
        + jnp.pad(from_west, ((0, 13), (0, 0), (0, 0)))
        + jnp.pad(from_east, ((13, 0), (0, 0), (0, 0)))
    )
    top_rim = by_cols[:, 19:22].astype(rim)
    from_south = to_north(top_rim)
    from_north = to_south(by_cols[:, 0:3].astype(rim))
    strip = jnp.where(is_north, top_rim, jnp.zeros_like(top_rim))[::-1, ::-1, :]
    spread = lax.dynamic_update_slice_in_dim(
        jnp.zeros((32, 3, channels), rim), strip, shift, axis=0
    )
    none = jnp.zeros_like(spread[:16])
    mine = jnp.where(even, spread[16:], spread[:16])
    mine = mine + top_to_next(jnp.where(even, spread[:16], none))
    mine = mine + top_to_previous(jnp.where(even, none, spread[16:]))
    mine, from_south, from_north, taken = lax.optimization_barrier(
        (mine, from_south, from_north, taken)
    )

    large, terms, *give = run_sum(
        second_sum_kernel,
        [((128, 512), F32), ((32, 512), F32)] + [((192, 512), BF16)] * 3,
        [own, terms, *taken],
        "second_sum",
        room=8,
    )
    taken = [send(piece, mask) for piece, mask in zip(give, Y_MASKS)]

    own, half, *give = run_sum(
        third_sum_kernel,
        [((32, 512), F32), ((32, 512), F32)] + [((96, 512), BF16)] * 3,
        [at, large, terms, *taken],
        "third_sum",
        scalars=1,
        scratch=[((8, 16, 512), F32)],
    )
    taken = [send(piece, mask) for piece, mask in zip(give, Z_MASKS[:3])]
    keep, half, give = run_sum(
        fourth_sum_kernel,
        [((16, 512), F32), ((32, 512), F32), ((48, 512), F32)],
        [own, half, *taken],
        "fourth_sum",
    )
    from_fold, got = mirror_tiles(mine, turn >> 1, (give,), lambda v: (send(v, Z_MASKS[3]),))
    from_fold = from_fold.astype(F32)
    grad_down, grad_up, half = run_sum(
        last_sum_kernel,
        [((8, 512), F32), ((2, 2048), F32), ((32, 512), F32)],
        [keep, half, got],
        "last_sum",
    )
    other = send(half, CORE_MASK)
    grad_kernel, grad_gain, grad_bias = run_sum(
        split_kernel,
        [((49, 512), F32), ((1, 512), F32), ((1, 2048), F32)],
        [at, half, other],
        "split",
        scalars=1,
    )
    grad_gain = grad_gain.reshape(512)
    grad_bias = grad_bias.reshape(2048)
    owned = by_cols[:, 3:19] + jnp.pad(from_south.astype(F32), ((0, 0), (0, 13), (0, 0)))
    owned = owned + jnp.pad(from_north.astype(F32) + from_fold, ((0, 0), (13, 0), (0, 0)))
    grad_field = (cotangent.astype(F32) + owned).astype(jnp.bfloat16)
    return (grad_field, grad_up, grad_down, grad_kernel, grad_gain, grad_bias)


def solution(mesh):
    placed = (
        P("lon", "lat", None),
        P("lon", "lat", None),
        P("lon", "lat"),
        P(),
        P(),
        P(),
        P(),
        P(),
        P(),
    )
    return jax.shard_map(
        per_device,
        mesh=mesh,
        in_specs=placed,
        out_specs=(
            P("lon", "lat", None),
            P(("lon", "lat"), None),
            P(("lon", "lat"), None),
            P(),
            P(),
            P(),
        ),
        check_vma=False,
    )
```

```python
import jax
import jax.numpy as jnp
from jax import lax
from jax.experimental import pallas as pl
from jax.experimental.pallas import tpu as pltpu
from jax.sharding import PartitionSpec as P

DEVICES = ("lon", "lat")
X_MASKS = (1, 2, 3)
Y_MASKS = (128, 4, 132)
Z_MASKS = (16, 32, 48, 96)
CORE_MASK = 8


def send(value, mask):
    return lax.ppermute(value, DEVICES, [(i, i ^ mask) for i in range(256)])


def to_next(value):
    return lax.ppermute(value, "lon", [(i, (i + 1) % 32) for i in range(32)])


def to_previous(value):
    return lax.ppermute(value, "lon", [((i + 1) % 32, i) for i in range(32)])


def to_north(value):
    return lax.ppermute(value, "lat", [(i, i + 1) for i in range(7)])


def to_south(value):
    return lax.ppermute(value, "lat", [(i + 1, i) for i in range(7)])


def top_to_next(value):
    pairs = [(i * 8 + 7, (i + 1) % 32 * 8 + 7) for i in range(32)]
    return lax.ppermute(value, DEVICES, pairs)


def top_to_previous(value):
    pairs = [((i + 1) % 32 * 8 + 7, i * 8 + 7) for i in range(32)]
    return lax.ppermute(value, DEVICES, pairs)


def mirror_tiles(value, half_turn):
    def branch(k):
        pairs = [(e * 8 + 7, ((2 * k - e) % 32) * 8 + 7) for e in range(32)]
        return lambda v: lax.ppermute(v, DEVICES, pairs)

    return lax.switch(half_turn, [branch(k) for k in range(16)], value)


ROOT_2_PI = 0.7978845608028654
CUBIC = 0.044715
F32 = jnp.float32
BF16 = jnp.bfloat16


def spread_rows(ext_ref, wide, shifted):
    wide[...] = ext_ref[...].astype(F32)
    for b in range(7):
        shifted[b] = wide[:, b : b + 16, :]


def forward_kernel(
    at_ref, ext_ref, kern_ref, gain_ref, b_up_ref, d_out_ref, order_hbm, w_up_hbm, d_act_hbm,
    d_cells_hbm, half_ref, own_hbm, keep_hbm, send_hbm,
    wide, shifted, normed, ordered, upper, active, tile, mixed_ref, order_ref, w_up_ref, d_act_ref,
    d_upper_ref, own, keep, give, small_ref, d_cells, sems,
):
    core, x_at, y_at = at_ref[0], at_ref[1], at_ref[2]
    loads = [
        pltpu.make_async_copy(order_hbm, order_ref, sems.at[0]),
        pltpu.make_async_copy(w_up_hbm, w_up_ref, sems.at[1]),
        pltpu.make_async_copy(d_act_hbm, d_act_ref, sems.at[2]),
    ]
    for load in loads:
        load.start()
    spread_rows(ext_ref, wide, shifted)

    def conv_step(step, carry):
        lanes = pl.ds(pl.multiple_of(step * 128, 128), 128)
        totals = [jnp.zeros((16, 128), F32)] * 16
        for b in range(7):
            weights = [kern_ref[a * 7 + b : a * 7 + b + 1, lanes] for a in range(7)]
            for r in range(22):
                cells = shifted[b, r, :, lanes]
                for a in range(max(0, r - 15), min(7, r + 1)):
                    totals[r - a] = totals[r - a] + cells * weights[a]
        for x in range(16):
            mixed_ref[x * 16 : x * 16 + 16, lanes] = totals[x]
        return carry

    lax.fori_loop(0, 4, conv_step, 0)

    def norm_step(step, carry):
        rows = pl.ds(pl.multiple_of(step * 32, 32), 32)
        cells = mixed_ref[rows, :]
        center = cells - jnp.mean(cells, axis=-1, keepdims=True)
        spread = jnp.mean(center * center, axis=-1, keepdims=True)
        normed[rows, :] = (center * lax.rsqrt(spread + 1e-6) * gain_ref[...]).astype(BF16)
        return carry

    lax.fori_loop(0, 8, norm_step, 0)
    for load in loads:
        load.wait()
    ordered[...] = jnp.dot(normed[...], order_ref[...], preferred_element_type=F32).astype(BF16)

    for t in range(4):
        lanes = slice(t * 512, t * 512 + 512)
        upper[...] = jnp.dot(normed[...], w_up_ref[:, lanes], preferred_element_type=F32)

        def gelu_step(step, bias):
            rows = pl.ds(pl.multiple_of(step * 32, 32), 32)
            u = upper[rows, :] + b_up_ref[:, lanes]
            square = u * u
            th = jnp.tanh(ROOT_2_PI * (u + CUBIC * (square * u)))
            half = 0.5 * (1.0 + th)
            active[rows, :] = (u * half).astype(BF16)
            slope = half + (0.5 * ROOT_2_PI) * u * (1.0 - th * th) * (1.0 + (3.0 * CUBIC) * square)
            d_up = (d_act_ref[rows, lanes] * slope).astype(BF16)
            d_upper_ref[rows, lanes] = d_up
            return bias + jnp.sum(d_up.astype(F32), axis=0, keepdims=True)

        small_ref[50 + t : 51 + t, :] = lax.fori_loop(0, 8, gelu_step, jnp.zeros((1, 512), F32))
        tile[...] = lax.dot_general(
            active[...], d_out_ref[...], (((0,), (0,)), ((), ())), preferred_element_type=F32
        )
        for y_hi in range(2):
            k_y = (y_hi * 2 + t // 2) ^ y_at
            for k_x in range(4):
                base = y_hi * 32 + (k_x ^ x_at) * 8
                for mine in range(2):
                    at = base + ((1 - core) if mine == 0 else core) * 64
                    piece = jnp.concatenate(
                        [tile[pl.ds(pl.multiple_of(at + zz * 128, 8), 8), :] for zz in range(4)],
                        axis=0,
                    )
                    at = k_y * 64 + (t % 2) * 32
                    rows = pl.ds(pl.multiple_of(at, 32), 32)
                    if mine == 0:
                        give[pl.ds(pl.multiple_of(k_x * 512 + at, 32), 32), :] = piece.astype(BF16)
                    elif k_x == 0:
                        own[rows, :] = piece
                    else:
                        keep[k_x - 1, rows, :] = piece.astype(BF16)

    for t in range(4):
        lanes = slice(t * 512, t * 512 + 512)
        tile[...] = lax.dot_general(
            ordered[...], d_upper_ref[:, lanes], (((0,), (0,)), ((), ())),
            preferred_element_type=F32,
        )
        at = 256 + t * 64
        own[at : at + 64, :] = tile[0:64, :]
        for k in range(4):
            piece = tile[256 + k * 64 : 320 + k * 64, :]
            give[k * 512 + at : k * 512 + at + 64, :] = piece.astype(BF16)
            if k:
                keep[k - 1, at : at + 64, :] = tile[k * 64 : k * 64 + 64, :].astype(BF16)
    stores = [
        pltpu.make_async_copy(give.at[0:2048], send_hbm.at[0:2048], sems.at[3]),
        pltpu.make_async_copy(keep, keep_hbm, sems.at[4]),
        pltpu.make_async_copy(own, own_hbm, sems.at[5]),
    ]
    for store in stores:
        store.start()
    upper[...] = lax.dot_general(
        d_upper_ref[...], w_up_ref[...], (((1,), (1,)), ((), ())), preferred_element_type=F32
    )

    def norm_step(step, gain_sum):
        rows = pl.ds(pl.multiple_of(step * 32, 32), 32)
        cells = mixed_ref[rows, :]
        center = cells - jnp.mean(cells, axis=-1, keepdims=True)
        spread = jnp.mean(center * center, axis=-1, keepdims=True)
        inverse = lax.rsqrt(spread + 1e-6)
        unit = center * inverse
        d = upper[rows, :]
        d_unit = d * gain_ref[...]
        along = jnp.mean(d_unit * unit, axis=-1, keepdims=True)
        d_center = (d_unit - unit * along) * inverse
        d_mixed = d_center - jnp.mean(d_center, axis=-1, keepdims=True)
        d_cells[pl.ds(step * 2, 2)] = d_mixed.reshape(2, 16, 512)
        return gain_sum + jnp.sum(d * unit, axis=0, keepdims=True)

    small_ref[49:50, :] = lax.fori_loop(0, 8, norm_step, jnp.zeros((1, 512), F32))
    small_ref[54:64, :] = jnp.zeros((10, 512), F32)
    stores.append(pltpu.make_async_copy(d_cells, d_cells_hbm, sems.at[7]))
    stores[-1].start()

    def tap_step(step, carry):
        lanes = pl.ds(pl.multiple_of(step * 128, 128), 128)
        d = [d_cells[x, :, lanes] for x in range(16)]
        for b in range(7):
            totals = [jnp.zeros((8, 128), F32)] * 7
            for r in range(22):
                cells = shifted[b, r, :, lanes]
                for a in range(max(0, r - 15), min(7, r + 1)):
                    product = cells * d[r - a]
                    totals[a] = totals[a] + product[:8] + product[8:]
            for a in range(7):
                row = a * 7 + b
                small_ref[row : row + 1, lanes] = jnp.sum(totals[a], axis=0, keepdims=True)
        return carry

    lax.fori_loop(0, 4, tap_step, 0)

    half_ref[...] = small_ref[pl.ds(pl.multiple_of(core * 32, 32), 32), :]
    high, low = two_terms(small_ref[pl.ds(pl.multiple_of((1 - core) * 32, 32), 32), :])
    give[2048:2080, :] = high
    give[2080:2112, :] = low
    stores.append(
        pltpu.make_async_copy(give.at[2048:2112], send_hbm.at[2048:2112], sems.at[6])
    )
    stores[-1].start()
    for store in stores:
        store.wait()


def rim_kernel(d_cells, kern_ref, grad_ref, west_ref, east_ref, moved):
    moved[...] = jnp.zeros_like(moved)
    for b in range(7):
        moved[b, :, b : b + 16, :] = d_cells[...]

    def rim_step(step, carry):
        lanes = pl.ds(pl.multiple_of(step * 128, 128), 128)
        for q in range(3):
            rows = slice(q * 8, q * 8 + 8)
            totals = [jnp.zeros((8, 128), F32)] * 22
            for b in range(1 if q == 2 else 0, 7):
                weights = [kern_ref[a * 7 + b : a * 7 + b + 1, lanes] for a in range(7)]
                for x in range(16):
                    cells = moved[b, x, rows, lanes]
                    for a in range(7):
                        totals[x + a] = totals[x + a] + cells * weights[a]
            for i in range(22):
                grad_ref[i, rows, lanes] = totals[i]
        return carry

    lax.fori_loop(0, 4, rim_step, 0)
    filler = jnp.zeros((3, 8, 512), F32)
    west_ref[...] = jnp.concatenate([grad_ref[0:3], filler], axis=1).astype(BF16)
    east_ref[...] = jnp.concatenate([grad_ref[19:22], filler], axis=1).astype(BF16)


MIB = 1024 * 1024
VMEM = pl.BlockSpec(memory_space=pltpu.VMEM)
SMEM = pl.BlockSpec(memory_space=pltpu.SMEM)
HBM = pl.BlockSpec(memory_space=pl.ANY)


def local_call(kernel, name, shapes, in_specs, out_specs, scratch, operands, flops, room):
    return pl.pallas_call(
        kernel,
        out_shape=[jax.ShapeDtypeStruct(s, d) for s, d in shapes],
        in_specs=in_specs,
        out_specs=out_specs,
        scratch_shapes=[pltpu.VMEM(s, d) if d else pltpu.SemaphoreType.DMA(s) for s, d in scratch],
        compiler_params=pltpu.CompilerParams(vmem_limit_bytes=room * MIB),
        cost_estimate=pl.CostEstimate(flops=flops, bytes_accessed=2000000, transcendentals=0),
        name=name,
    )(*operands)


def run_forward(at, ext, kern, gain, w_up, b_up, d_out, d_act, order):
    square, long = (256, 512), (256, 2048)
    return local_call(
        forward_kernel,
        "forward",
        [
            ((16, 16, 512), F32), ((32, 512), F32),
            ((512, 512), F32), ((3, 512, 512), BF16), ((2112, 512), BF16),
        ],
        [SMEM] + [VMEM] * 5 + [HBM] * 3,
        [HBM, VMEM, HBM, HBM, HBM],
        [
            ((22, 32, 512), F32), ((7, 22, 16, 512), F32), (square, BF16), (square, BF16),
            (square, F32), (square, BF16), ((512, 512), F32), (square, F32), ((512, 512), BF16),
            ((512, 2048), BF16), (long, F32), (long, BF16),
            ((512, 512), F32), ((3, 512, 512), BF16), ((2112, 512), BF16), ((64, 512), F32),
            ((16, 16, 512), F32), ((8,), None),
        ],
        [at, ext, kern, gain, b_up, d_out, order, w_up, d_act],
        20000000000,
        56,
    )


def run_rims(d_cells, kern):
    return local_call(
        rim_kernel,
        "rims",
        [((22, 24, 512), F32), ((3, 32, 512), BF16), ((3, 32, 512), BF16)],
        [VMEM] * 2,
        [VMEM] * 3,
        [((7, 16, 24, 512), F32)],
        [d_cells, kern],
        5000000000,
        16,
    )


def run_sum(kernel, shapes, operands, name, scalars=0, scratch=(), room=4):
    return local_call(
        kernel, name, shapes, [SMEM] * scalars + [VMEM] * (len(operands) - scalars),
        [VMEM] * len(shapes), scratch, operands, 800000000, room,
    )


def two_terms(value):
    high = value.astype(BF16)
    return high, (value - high.astype(F32)).astype(BF16)


def rounded(high, low):
    return high.astype(F32) + low.astype(F32)


def whole(first, rest, rows):
    a, b, c = [ref[rows, :].astype(F32) for ref in rest]
    return (first + a) + (b + c)


def whole_terms(first, refs, at):
    a, b, c = [rounded(ref[at : at + 32, :], ref[at + 32 : at + 64, :]) for ref in refs]
    return (first + a) + (b + c)


def first_sum_kernel(mine_ref, keep_ref, given_ref, half_ref, own_ref, terms_ref, *give_refs):
    own_ref[...] = mine_ref[...] + given_ref[0:512, :].astype(F32)
    half = half_ref[...] + rounded(given_ref[2048:2080, :], given_ref[2080:2112, :])
    high, low = two_terms(half)
    terms_ref[...] = rounded(high, low)
    for k in range(3):
        rows = slice(k * 512 + 512, k * 512 + 1024)
        total = keep_ref[k].astype(F32) + given_ref[rows, :].astype(F32)
        give_refs[k][0:512, :] = total.astype(BF16)
        give_refs[k][512:544, :] = high
        give_refs[k][544:576, :] = low


def second_sum_kernel(own_ref, terms_ref, a_ref, b_ref, c_ref, large_ref, next_ref, *give_refs):
    refs = (a_ref, b_ref, c_ref)
    high, low = two_terms(whole_terms(terms_ref[...], refs, 512))
    next_ref[...] = rounded(high, low)
    for k in range(4):
        pieces = [(0, k * 64, 64)] + [(64 + t * 16, 256 + t * 64 + k * 16, 16) for t in range(4)]
        for target, at, count in pieces:
            rows = slice(at, at + count)
            total = whole(own_ref[rows, :], refs, rows)
            if k == 0:
                large_ref[target : target + count, :] = total
            else:
                give_refs[k - 1][target : target + count, :] = total.astype(BF16)
        if k:
            give_refs[k - 1][128:160, :] = high
            give_refs[k - 1][160:192, :] = low


def third_sum_kernel(at_ref, large_ref, terms_ref, a_ref, b_ref, c_ref, *outs):
    refs = (a_ref, b_ref, c_ref)
    own_ref, half_ref, give_refs, blocks = outs[0], outs[1], outs[2:5], outs[5]
    z_at = at_ref[3]
    high, low = two_terms(whole_terms(terms_ref[...], refs, 128))
    half_ref[...] = rounded(high, low)
    down = whole(large_ref[0:64, :], refs, slice(0, 64))
    up = whole(large_ref[64:128, :], refs, slice(64, 128))
    for z in range(8):
        rows = [up[t * 16 + z * 2 : t * 16 + z * 2 + 2] for t in range(4)]
        blocks[z] = jnp.concatenate([down[z * 8 : z * 8 + 8]] + rows, axis=0)
    for k in range(4):
        for part in range(2):
            block = blocks[z_at ^ k ^ (part * 6)]
            rows = slice(part * 16, part * 16 + 16)
            if k == 0:
                own_ref[rows, :] = block
            else:
                give_refs[k - 1][rows, :] = block.astype(BF16)
        if k:
            give_refs[k - 1][32:64, :] = high
            give_refs[k - 1][64:96, :] = low


def fourth_sum_kernel(own_ref, half_ref, a_ref, b_ref, c_ref, keep_ref, sum_ref, give_ref):
    refs = (a_ref, b_ref, c_ref)
    half = whole_terms(half_ref[...], refs, 32)
    keep_ref[...] = whole(own_ref[0:16, :], refs, slice(0, 16))
    give_ref[0:16, :] = whole(own_ref[16:32, :], refs, slice(16, 32))
    give_ref[16:48, :] = half
    sum_ref[...] = half


def last_sum_kernel(keep_ref, half_ref, got_ref, down_ref, up_ref, sum_ref):
    sum_ref[...] = half_ref[...] + got_ref[16:48, :]
    down_ref[...] = keep_ref[0:8, :] + got_ref[0:8, :]
    up = keep_ref[8:16, :] + got_ref[8:16, :]
    for t in range(4):
        up_ref[:, t * 512 : t * 512 + 512] = up[t * 2 : t * 2 + 2]


def split_kernel(at_ref, half_ref, other_ref, kernel_ref, gain_ref, bias_ref):
    first = at_ref[0] == 0
    half, other = half_ref[...], other_ref[...]
    low, high = jnp.where(first, half, other), jnp.where(first, other, half)
    kernel_ref[0:32, :] = low
    kernel_ref[32:49, :] = high[0:17]
    gain_ref[...] = high[17:18]
    for t in range(4):
        bias_ref[:, t * 512 : t * 512 + 512] = high[18 + t : 19 + t]


def per_device(
    field, cotangent, land_sea, fold_partner, depth_kernel, norm_gain, w_up, b_up, w_down
):
    width_lon, width_lat, channels = field.shape
    lon_at = lax.axis_index("lon")
    lat_at = lax.axis_index("lat")
    core = lon_at & 1
    z_at = (lon_at >> 1) & 7
    y_at = ((lat_at >> 2) << 1) + (lon_at >> 4)
    x_at = lat_at & 3
    is_north = lat_at == lax.axis_size("lat") - 1
    from_end = 511 - fold_partner[0]
    turn = 31 - (from_end >> 4)
    shift = 16 - (from_end & 15)
    even = (turn & 1) == 0

    top_rows = field[:, width_lat - 3 :, :]
    mine = mirror_tiles(top_rows, turn >> 1)
    south = to_north(top_rows)
    north = to_south(field[:, 0:3, :])
    low = jnp.where(even, to_previous(mine), mine)
    high = jnp.where(even, mine, to_next(mine))
    fold = lax.dynamic_slice_in_dim(jnp.concatenate([low, high], axis=0), shift, 16, axis=0)
    north = jnp.where(is_north, fold[::-1, ::-1, :], north)
    column = jnp.concatenate([south, field, north], axis=1)
    extended = jnp.concatenate(
        [to_next(column[width_lon - 3 :]), column, to_previous(column[:3])], axis=0
    )
    extended = jnp.pad(extended, ((0, 0), (0, 10), (0, 0)))
    tokens = width_lon * width_lat
    d_out = cotangent.reshape(tokens, channels) * land_sea.reshape(tokens, 1).astype(jnp.bfloat16)
    d_act = lax.dot_general(
        d_out, w_down, (((1,), (1,)), ((), ())), preferred_element_type=jnp.float32
    )
    row = jnp.arange(512, dtype=jnp.int32)
    block = row >> 1
    y_of = (((block >> 2) & 1) << 1) + (block >> 7)
    goes_to = (
        (((block >> 3) & 1) ^ core) * 256
        + ((block & 3) ^ x_at) * 64
        + (y_of ^ y_at) * 16
        + ((block >> 4) & 7) * 2
        + (row & 1)
    )
    order = (goes_to[:, None] == row[None, :]).astype(jnp.bfloat16)
    at = jnp.stack([core, x_at, y_at, z_at]).astype(jnp.int32)
    gain = norm_gain.reshape(1, channels)
    d_cells, half, mine, keep, give = run_forward(
        at, extended, depth_kernel, gain, w_up, b_up.reshape(1, 2048), d_out, d_act, order
    )

    given = send(give, CORE_MASK)
    grad_ext, west_rim, east_rim = run_rims(d_cells, depth_kernel)
    given, west_rim, east_rim = lax.optimization_barrier((given, west_rim, east_rim))
    own, terms, *give = run_sum(
        first_sum_kernel,
        [((512, 512), F32), ((32, 512), F32)] + [((576, 512), BF16)] * 3,
        [mine, keep, given, half],
        "first_sum",
        room=16,
    )
    taken = [send(piece, mask) for piece, mask in zip(give, X_MASKS)]

    rim = jnp.bfloat16
    from_west, from_east = to_next(east_rim), to_previous(west_rim)
    from_west, from_east = from_west[:, :22].astype(F32), from_east[:, :22].astype(F32)
    by_cols = (
        grad_ext[3:19, :22]
        + jnp.pad(from_west, ((0, 13), (0, 0), (0, 0)))
        + jnp.pad(from_east, ((13, 0), (0, 0), (0, 0)))
    )
    top_rim = by_cols[:, 19:22].astype(rim)
    from_south = to_north(top_rim)
    from_north = to_south(by_cols[:, 0:3].astype(rim))
    strip = jnp.where(is_north, top_rim, jnp.zeros_like(top_rim))[::-1, ::-1, :]
    spread = lax.dynamic_update_slice_in_dim(
        jnp.zeros((32, 3, channels), rim), strip, shift, axis=0
    )
    none = jnp.zeros_like(spread[:16])
    mine = jnp.where(even, spread[16:], spread[:16])
    mine = mine + top_to_next(jnp.where(even, spread[:16], none))
    mine = mine + top_to_previous(jnp.where(even, none, spread[16:]))
    mine, from_south, from_north, taken = lax.optimization_barrier(
        (mine, from_south, from_north, taken)
    )

    large, terms, *give = run_sum(
        second_sum_kernel,
        [((128, 512), F32), ((32, 512), F32)] + [((192, 512), BF16)] * 3,
        [own, terms, *taken],
        "second_sum",
        room=8,
    )
    taken = [send(piece, mask) for piece, mask in zip(give, Y_MASKS)]
    from_fold, taken = lax.optimization_barrier((mirror_tiles(mine, turn >> 1), taken))
    from_fold = from_fold.astype(F32)

    own, half, *give = run_sum(
        third_sum_kernel,
        [((32, 512), F32), ((32, 512), F32)] + [((96, 512), BF16)] * 3,
        [at, large, terms, *taken],
        "third_sum",
        scalars=1,
        scratch=[((8, 16, 512), F32)],
    )
    taken = [send(piece, mask) for piece, mask in zip(give, Z_MASKS[:3])]
    keep, half, give = run_sum(
        fourth_sum_kernel,
        [((16, 512), F32), ((32, 512), F32), ((48, 512), F32)],
        [own, half, *taken],
        "fourth_sum",
    )
    grad_down, grad_up, half = run_sum(
        last_sum_kernel,
        [((8, 512), F32), ((2, 2048), F32), ((32, 512), F32)],
        [keep, half, send(give, Z_MASKS[3])],
        "last_sum",
    )
    other = send(half, CORE_MASK)
    grad_kernel, grad_gain, grad_bias = run_sum(
        split_kernel,
        [((49, 512), F32), ((1, 512), F32), ((1, 2048), F32)],
        [at, half, other],
        "split",
        scalars=1,
    )
    grad_gain = grad_gain.reshape(512)
    grad_bias = grad_bias.reshape(2048)
    owned = by_cols[:, 3:19] + jnp.pad(from_south.astype(F32), ((0, 0), (0, 13), (0, 0)))
    owned = owned + jnp.pad(from_north.astype(F32) + from_fold, ((0, 0), (13, 0), (0, 0)))
    grad_field = (cotangent.astype(F32) + owned).astype(jnp.bfloat16)
    return (grad_field, grad_up, grad_down, grad_kernel, grad_gain, grad_bias)


def solution(mesh):
    placed = (
        P("lon", "lat", None),
        P("lon", "lat", None),
        P("lon", "lat"),
        P(),
        P(),
        P(),
        P(),
        P(),
        P(),
    )
    return jax.shard_map(
        per_device,
        mesh=mesh,
        in_specs=placed,
        out_specs=(
            P("lon", "lat", None),
            P(("lon", "lat"), None),
            P(("lon", "lat"), None),
            P(),
            P(),
            P(),
        ),
        check_vma=False,
    )
```

```python
import jax
import jax.numpy as jnp
from jax import lax
from jax.experimental import pallas as pl
from jax.experimental.pallas import tpu as pltpu
from jax.sharding import PartitionSpec as P

DEVICES = ("lon", "lat")
X_MASKS = (1, 2, 3)
Y_MASKS = (128, 4, 132)
Z_MASKS = (16, 32, 48, 96)
CORE_MASK = 8


def send(value, mask):
    return lax.ppermute(value, DEVICES, [(i, i ^ mask) for i in range(256)])


def to_next(value):
    return lax.ppermute(value, "lon", [(i, (i + 1) % 32) for i in range(32)])


def to_previous(value):
    return lax.ppermute(value, "lon", [((i + 1) % 32, i) for i in range(32)])


def to_north(value):
    return lax.ppermute(value, "lat", [(i, i + 1) for i in range(7)])


def to_south(value):
    return lax.ppermute(value, "lat", [(i + 1, i) for i in range(7)])


def top_to_next(value):
    pairs = [(i * 8 + 7, (i + 1) % 32 * 8 + 7) for i in range(32)]
    return lax.ppermute(value, DEVICES, pairs)


def top_to_previous(value):
    pairs = [((i + 1) % 32 * 8 + 7, i * 8 + 7) for i in range(32)]
    return lax.ppermute(value, DEVICES, pairs)


def mirror_tiles(value, half_turn):
    def branch(k):
        pairs = [(e * 8 + 7, ((2 * k - e) % 32) * 8 + 7) for e in range(32)]
        return lambda v: lax.ppermute(v, DEVICES, pairs)

    return lax.switch(half_turn, [branch(k) for k in range(16)], value)


ROOT_2_PI = 0.7978845608028654
CUBIC = 0.044715
F32 = jnp.float32
BF16 = jnp.bfloat16


def spread_rows(ext_ref, wide, shifted):
    wide[...] = ext_ref[...].astype(F32)
    for b in range(7):
        shifted[b] = wide[:, b : b + 16, :]


def forward_kernel(
    at_ref, ext_ref, kern_ref, gain_ref, b_up_ref, d_out_ref, order_hbm, w_up_hbm, d_act_hbm,
    d_cells_hbm, half_ref, own_hbm, keep_hbm, send_hbm,
    wide, shifted, normed, ordered, upper, active, tile, mixed_ref, order_ref, w_up_ref, d_act_ref,
    d_upper_ref, own, keep, give, small_ref, d_cells, sems,
):
    core, x_at, y_at = at_ref[0], at_ref[1], at_ref[2]
    loads = [
        pltpu.make_async_copy(order_hbm, order_ref, sems.at[0]),
        pltpu.make_async_copy(w_up_hbm, w_up_ref, sems.at[1]),
        pltpu.make_async_copy(d_act_hbm, d_act_ref, sems.at[2]),
    ]
    for load in loads:
        load.start()
    spread_rows(ext_ref, wide, shifted)

    def conv_step(step, carry):
        lanes = pl.ds(pl.multiple_of(step * 128, 128), 128)
        totals = [jnp.zeros((16, 128), F32)] * 16
        for b in range(7):
            weights = [kern_ref[a * 7 + b : a * 7 + b + 1, lanes] for a in range(7)]
            for r in range(22):
                cells = shifted[b, r, :, lanes]
                for a in range(max(0, r - 15), min(7, r + 1)):
                    totals[r - a] = totals[r - a] + cells * weights[a]
        for x in range(16):
            mixed_ref[x * 16 : x * 16 + 16, lanes] = totals[x]
        return carry

    lax.fori_loop(0, 4, conv_step, 0)

    def norm_step(step, carry):
        rows = pl.ds(pl.multiple_of(step * 32, 32), 32)
        cells = mixed_ref[rows, :]
        center = cells - jnp.mean(cells, axis=-1, keepdims=True)
        spread = jnp.mean(center * center, axis=-1, keepdims=True)
        normed[rows, :] = (center * lax.rsqrt(spread + 1e-6) * gain_ref[...]).astype(BF16)
        return carry

    lax.fori_loop(0, 8, norm_step, 0, unroll=8)
    for load in loads:
        load.wait()
    ordered[...] = jnp.dot(normed[...], order_ref[...], preferred_element_type=F32).astype(BF16)

    for t in range(4):
        lanes = slice(t * 512, t * 512 + 512)
        upper[...] = jnp.dot(normed[...], w_up_ref[:, lanes], preferred_element_type=F32)

        def gelu_step(step, bias):
            rows = pl.ds(pl.multiple_of(step * 32, 32), 32)
            u = upper[rows, :] + b_up_ref[:, lanes]
            square = u * u
            th = jnp.tanh(ROOT_2_PI * (u + CUBIC * (square * u)))
            half = 0.5 * (1.0 + th)
            active[rows, :] = (u * half).astype(BF16)
            slope = half + (0.5 * ROOT_2_PI) * u * (1.0 - th * th) * (1.0 + (3.0 * CUBIC) * square)
            d_up = (d_act_ref[rows, lanes] * slope).astype(BF16)
            d_upper_ref[rows, lanes] = d_up
            return bias + jnp.sum(d_up.astype(F32), axis=0, keepdims=True)

        small_ref[50 + t : 51 + t, :] = lax.fori_loop(0, 8, gelu_step, jnp.zeros((1, 512), F32), unroll=4)
        tile[...] = lax.dot_general(
            active[...], d_out_ref[...], (((0,), (0,)), ((), ())), preferred_element_type=F32
        )
        for y_hi in range(2):
            k_y = (y_hi * 2 + t // 2) ^ y_at
            for k_x in range(4):
                base = y_hi * 32 + (k_x ^ x_at) * 8
                for mine in range(2):
                    at = base + ((1 - core) if mine == 0 else core) * 64
                    piece = jnp.concatenate(
                        [tile[pl.ds(pl.multiple_of(at + zz * 128, 8), 8), :] for zz in range(4)],
                        axis=0,
                    )
                    at = k_y * 64 + (t % 2) * 32
                    rows = pl.ds(pl.multiple_of(at, 32), 32)
                    if mine == 0:
                        give[pl.ds(pl.multiple_of(k_x * 512 + at, 32), 32), :] = piece.astype(BF16)
                    elif k_x == 0:
                        own[rows, :] = piece
                    else:
                        keep[k_x - 1, rows, :] = piece.astype(BF16)

    for t in range(4):
        lanes = slice(t * 512, t * 512 + 512)
        tile[...] = lax.dot_general(
            ordered[...], d_upper_ref[:, lanes], (((0,), (0,)), ((), ())),
            preferred_element_type=F32,
        )
        at = 256 + t * 64
        own[at : at + 64, :] = tile[0:64, :]
        for k in range(4):
            piece = tile[256 + k * 64 : 320 + k * 64, :]
            give[k * 512 + at : k * 512 + at + 64, :] = piece.astype(BF16)
            if k:
                keep[k - 1, at : at + 64, :] = tile[k * 64 : k * 64 + 64, :].astype(BF16)
    stores = [
        pltpu.make_async_copy(give.at[0:2048], send_hbm.at[0:2048], sems.at[3]),
        pltpu.make_async_copy(keep, keep_hbm, sems.at[4]),
        pltpu.make_async_copy(own, own_hbm, sems.at[5]),
    ]
    for store in stores:
        store.start()
    upper[...] = lax.dot_general(
        d_upper_ref[...], w_up_ref[...], (((1,), (1,)), ((), ())), preferred_element_type=F32
    )

    def norm_step(step, gain_sum):
        rows = pl.ds(pl.multiple_of(step * 32, 32), 32)
        cells = mixed_ref[rows, :]
        center = cells - jnp.mean(cells, axis=-1, keepdims=True)
        spread = jnp.mean(center * center, axis=-1, keepdims=True)
        inverse = lax.rsqrt(spread + 1e-6)
        unit = center * inverse
        d = upper[rows, :]
        d_unit = d * gain_ref[...]
        along = jnp.mean(d_unit * unit, axis=-1, keepdims=True)
        d_center = (d_unit - unit * along) * inverse
        d_mixed = d_center - jnp.mean(d_center, axis=-1, keepdims=True)
        d_cells[pl.ds(step * 2, 2)] = d_mixed.reshape(2, 16, 512)
        return gain_sum + jnp.sum(d * unit, axis=0, keepdims=True)

    small_ref[49:50, :] = lax.fori_loop(0, 8, norm_step, jnp.zeros((1, 512), F32), unroll=8)
    small_ref[54:64, :] = jnp.zeros((10, 512), F32)
    stores.append(pltpu.make_async_copy(d_cells, d_cells_hbm, sems.at[7]))
    stores[-1].start()

    def tap_step(step, carry):
        lanes = pl.ds(pl.multiple_of(step * 128, 128), 128)
        d = [d_cells[x, :, lanes] for x in range(16)]
        for b in range(7):
            totals = [jnp.zeros((8, 128), F32)] * 7
            for r in range(22):
                cells = shifted[b, r, :, lanes]
                for a in range(max(0, r - 15), min(7, r + 1)):
                    product = cells * d[r - a]
                    totals[a] = totals[a] + product[:8] + product[8:]
            for a in range(7):
                row = a * 7 + b
                small_ref[row : row + 1, lanes] = jnp.sum(totals[a], axis=0, keepdims=True)
        return carry

    lax.fori_loop(0, 4, tap_step, 0)

    half_ref[...] = small_ref[pl.ds(pl.multiple_of(core * 32, 32), 32), :]
    high, low = two_terms(small_ref[pl.ds(pl.multiple_of((1 - core) * 32, 32), 32), :])
    give[2048:2080, :] = high
    give[2080:2112, :] = low
    stores.append(
        pltpu.make_async_copy(give.at[2048:2112], send_hbm.at[2048:2112], sems.at[6])
    )
    stores[-1].start()
    for store in stores:
        store.wait()


def rim_kernel(d_cells, kern_ref, grad_ref, west_ref, east_ref, moved):
    moved[...] = jnp.zeros_like(moved)
    for b in range(7):
        moved[b, :, b : b + 16, :] = d_cells[...]

    def rim_step(step, carry):
        lanes = pl.ds(pl.multiple_of(step * 128, 128), 128)
        for q in range(3):
            rows = slice(q * 8, q * 8 + 8)
            totals = [jnp.zeros((8, 128), F32)] * 22
            for b in range(1 if q == 2 else 0, 7):
                weights = [kern_ref[a * 7 + b : a * 7 + b + 1, lanes] for a in range(7)]
                for x in range(16):
                    cells = moved[b, x, rows, lanes]
                    for a in range(7):
                        totals[x + a] = totals[x + a] + cells * weights[a]
            for i in range(22):
                grad_ref[i, rows, lanes] = totals[i]
        return carry

    lax.fori_loop(0, 4, rim_step, 0)
    filler = jnp.zeros((3, 8, 512), F32)
    west_ref[...] = jnp.concatenate([grad_ref[0:3], filler], axis=1).astype(BF16)
    east_ref[...] = jnp.concatenate([grad_ref[19:22], filler], axis=1).astype(BF16)


MIB = 1024 * 1024
VMEM = pl.BlockSpec(memory_space=pltpu.VMEM)
SMEM = pl.BlockSpec(memory_space=pltpu.SMEM)
HBM = pl.BlockSpec(memory_space=pl.ANY)


def local_call(kernel, name, shapes, in_specs, out_specs, scratch, operands, flops, room):
    return pl.pallas_call(
        kernel,
        out_shape=[jax.ShapeDtypeStruct(s, d) for s, d in shapes],
        in_specs=in_specs,
        out_specs=out_specs,
        scratch_shapes=[pltpu.VMEM(s, d) if d else pltpu.SemaphoreType.DMA(s) for s, d in scratch],
        compiler_params=pltpu.CompilerParams(vmem_limit_bytes=room * MIB),
        cost_estimate=pl.CostEstimate(flops=flops, bytes_accessed=2000000, transcendentals=0),
        name=name,
    )(*operands)


def run_forward(at, ext, kern, gain, w_up, b_up, d_out, d_act, order):
    square, long = (256, 512), (256, 2048)
    return local_call(
        forward_kernel,
        "forward",
        [
            ((16, 16, 512), F32), ((32, 512), F32),
            ((512, 512), F32), ((3, 512, 512), BF16), ((2112, 512), BF16),
        ],
        [SMEM] + [VMEM] * 5 + [HBM] * 3,
        [HBM, VMEM, HBM, HBM, HBM],
        [
            ((22, 32, 512), F32), ((7, 22, 16, 512), F32), (square, BF16), (square, BF16),
            (square, F32), (square, BF16), ((512, 512), F32), (square, F32), ((512, 512), BF16),
            ((512, 2048), BF16), (long, F32), (long, BF16),
            ((512, 512), F32), ((3, 512, 512), BF16), ((2112, 512), BF16), ((64, 512), F32),
            ((16, 16, 512), F32), ((8,), None),
        ],
        [at, ext, kern, gain, b_up, d_out, order, w_up, d_act],
        20000000000,
        56,
    )


def run_rims(d_cells, kern):
    return local_call(
        rim_kernel,
        "rims",
        [((22, 24, 512), F32), ((3, 32, 512), BF16), ((3, 32, 512), BF16)],
        [VMEM] * 2,
        [VMEM] * 3,
        [((7, 16, 24, 512), F32)],
        [d_cells, kern],
        5000000000,
        16,
    )


def run_sum(kernel, shapes, operands, name, scalars=0, scratch=(), room=4):
    return local_call(
        kernel, name, shapes, [SMEM] * scalars + [VMEM] * (len(operands) - scalars),
        [VMEM] * len(shapes), scratch, operands, 800000000, room,
    )


def two_terms(value):
    high = value.astype(BF16)
    return high, (value - high.astype(F32)).astype(BF16)


def rounded(high, low):
    return high.astype(F32) + low.astype(F32)


def whole(first, rest, rows):
    a, b, c = [ref[rows, :].astype(F32) for ref in rest]
    return (first + a) + (b + c)


def whole_terms(first, refs, at):
    a, b, c = [rounded(ref[at : at + 32, :], ref[at + 32 : at + 64, :]) for ref in refs]
    return (first + a) + (b + c)


def first_sum_kernel(mine_ref, keep_ref, given_ref, half_ref, own_ref, terms_ref, *give_refs):
    own_ref[...] = mine_ref[...] + given_ref[0:512, :].astype(F32)
    half = half_ref[...] + rounded(given_ref[2048:2080, :], given_ref[2080:2112, :])
    high, low = two_terms(half)
    terms_ref[...] = rounded(high, low)
    for k in range(3):
        rows = slice(k * 512 + 512, k * 512 + 1024)
        total = keep_ref[k].astype(F32) + given_ref[rows, :].astype(F32)
        give_refs[k][0:512, :] = total.astype(BF16)
        give_refs[k][512:544, :] = high
        give_refs[k][544:576, :] = low


def second_sum_kernel(own_ref, terms_ref, a_ref, b_ref, c_ref, large_ref, next_ref, *give_refs):
    refs = (a_ref, b_ref, c_ref)
    high, low = two_terms(whole_terms(terms_ref[...], refs, 512))
    next_ref[...] = rounded(high, low)
    for k in range(4):
        pieces = [(0, k * 64, 64)] + [(64 + t * 16, 256 + t * 64 + k * 16, 16) for t in range(4)]
        for target, at, count in pieces:
            rows = slice(at, at + count)
            total = whole(own_ref[rows, :], refs, rows)
            if k == 0:
                large_ref[target : target + count, :] = total
            else:
                give_refs[k - 1][target : target + count, :] = total.astype(BF16)
        if k:
            give_refs[k - 1][128:160, :] = high
            give_refs[k - 1][160:192, :] = low


def third_sum_kernel(at_ref, large_ref, terms_ref, a_ref, b_ref, c_ref, *outs):
    refs = (a_ref, b_ref, c_ref)
    own_ref, half_ref, give_refs, blocks = outs[0], outs[1], outs[2:5], outs[5]
    z_at = at_ref[3]
    high, low = two_terms(whole_terms(terms_ref[...], refs, 128))
    half_ref[...] = rounded(high, low)
    down = whole(large_ref[0:64, :], refs, slice(0, 64))
    up = whole(large_ref[64:128, :], refs, slice(64, 128))
    for z in range(8):
        rows = [up[t * 16 + z * 2 : t * 16 + z * 2 + 2] for t in range(4)]
        blocks[z] = jnp.concatenate([down[z * 8 : z * 8 + 8]] + rows, axis=0)
    for k in range(4):
        for part in range(2):
            block = blocks[z_at ^ k ^ (part * 6)]
            rows = slice(part * 16, part * 16 + 16)
            if k == 0:
                own_ref[rows, :] = block
            else:
                give_refs[k - 1][rows, :] = block.astype(BF16)
        if k:
            give_refs[k - 1][32:64, :] = high
            give_refs[k - 1][64:96, :] = low


def fourth_sum_kernel(own_ref, half_ref, a_ref, b_ref, c_ref, keep_ref, sum_ref, give_ref):
    refs = (a_ref, b_ref, c_ref)
    half = whole_terms(half_ref[...], refs, 32)
    keep_ref[...] = whole(own_ref[0:16, :], refs, slice(0, 16))
    give_ref[0:16, :] = whole(own_ref[16:32, :], refs, slice(16, 32))
    give_ref[16:48, :] = half
    sum_ref[...] = half


def last_sum_kernel(keep_ref, half_ref, got_ref, down_ref, up_ref, sum_ref):
    sum_ref[...] = half_ref[...] + got_ref[16:48, :]
    down_ref[...] = keep_ref[0:8, :] + got_ref[0:8, :]
    up = keep_ref[8:16, :] + got_ref[8:16, :]
    for t in range(4):
        up_ref[:, t * 512 : t * 512 + 512] = up[t * 2 : t * 2 + 2]


def split_kernel(at_ref, half_ref, other_ref, kernel_ref, gain_ref, bias_ref):
    first = at_ref[0] == 0
    half, other = half_ref[...], other_ref[...]
    low, high = jnp.where(first, half, other), jnp.where(first, other, half)
    kernel_ref[0:32, :] = low
    kernel_ref[32:49, :] = high[0:17]
    gain_ref[...] = high[17:18]
    for t in range(4):
        bias_ref[:, t * 512 : t * 512 + 512] = high[18 + t : 19 + t]


def per_device(
    field, cotangent, land_sea, fold_partner, depth_kernel, norm_gain, w_up, b_up, w_down
):
    width_lon, width_lat, channels = field.shape
    lon_at = lax.axis_index("lon")
    lat_at = lax.axis_index("lat")
    core = lon_at & 1
    z_at = (lon_at >> 1) & 7
    y_at = ((lat_at >> 2) << 1) + (lon_at >> 4)
    x_at = lat_at & 3
    is_north = lat_at == lax.axis_size("lat") - 1
    from_end = 511 - fold_partner[0]
    turn = 31 - (from_end >> 4)
    shift = 16 - (from_end & 15)
    even = (turn & 1) == 0

    top_rows = field[:, width_lat - 3 :, :]
    mine = mirror_tiles(top_rows, turn >> 1)
    south = to_north(top_rows)
    north = to_south(field[:, 0:3, :])
    low = jnp.where(even, to_previous(mine), mine)
    high = jnp.where(even, mine, to_next(mine))
    fold = lax.dynamic_slice_in_dim(jnp.concatenate([low, high], axis=0), shift, 16, axis=0)
    north = jnp.where(is_north, fold[::-1, ::-1, :], north)
    column = jnp.concatenate([south, field, north], axis=1)
    extended = jnp.concatenate(
        [to_next(column[width_lon - 3 :]), column, to_previous(column[:3])], axis=0
    )
    extended = jnp.pad(extended, ((0, 0), (0, 10), (0, 0)))
    tokens = width_lon * width_lat
    d_out = cotangent.reshape(tokens, channels) * land_sea.reshape(tokens, 1).astype(jnp.bfloat16)
    d_act = lax.dot_general(
        d_out, w_down, (((1,), (1,)), ((), ())), preferred_element_type=jnp.float32
    )
    row = jnp.arange(512, dtype=jnp.int32)
    block = row >> 1
    y_of = (((block >> 2) & 1) << 1) + (block >> 7)
    goes_to = (
        (((block >> 3) & 1) ^ core) * 256
        + ((block & 3) ^ x_at) * 64
        + (y_of ^ y_at) * 16
        + ((block >> 4) & 7) * 2
        + (row & 1)
    )
    order = (goes_to[:, None] == row[None, :]).astype(jnp.bfloat16)
    at = jnp.stack([core, x_at, y_at, z_at]).astype(jnp.int32)
    gain = norm_gain.reshape(1, channels)
    d_cells, half, mine, keep, give = run_forward(
        at, extended, depth_kernel, gain, w_up, b_up.reshape(1, 2048), d_out, d_act, order
    )

    given = send(give, CORE_MASK)
    grad_ext, west_rim, east_rim = run_rims(d_cells, depth_kernel)
    given, west_rim, east_rim = lax.optimization_barrier((given, west_rim, east_rim))
    own, terms, *give = run_sum(
        first_sum_kernel,
        [((512, 512), F32), ((32, 512), F32)] + [((576, 512), BF16)] * 3,
        [mine, keep, given, half],
        "first_sum",
        room=16,
    )
    taken = [send(piece, mask) for piece, mask in zip(give, X_MASKS)]

    rim = jnp.bfloat16
    from_west, from_east = to_next(east_rim), to_previous(west_rim)
    from_west, from_east = from_west[:, :22].astype(F32), from_east[:, :22].astype(F32)
    by_cols = (
        grad_ext[3:19, :22]
        + jnp.pad(from_west, ((0, 13), (0, 0), (0, 0)))
        + jnp.pad(from_east, ((13, 0), (0, 0), (0, 0)))
    )
    top_rim = by_cols[:, 19:22].astype(rim)
    from_south = to_north(top_rim)
    from_north = to_south(by_cols[:, 0:3].astype(rim))
    strip = jnp.where(is_north, top_rim, jnp.zeros_like(top_rim))[::-1, ::-1, :]
    spread = lax.dynamic_update_slice_in_dim(
        jnp.zeros((32, 3, channels), rim), strip, shift, axis=0
    )
    none = jnp.zeros_like(spread[:16])
    mine = jnp.where(even, spread[16:], spread[:16])
    mine = mine + top_to_next(jnp.where(even, spread[:16], none))
    mine = mine + top_to_previous(jnp.where(even, none, spread[16:]))
    mine, from_south, from_north, taken = lax.optimization_barrier(
        (mine, from_south, from_north, taken)
    )

    large, terms, *give = run_sum(
        second_sum_kernel,
        [((128, 512), F32), ((32, 512), F32)] + [((192, 512), BF16)] * 3,
        [own, terms, *taken],
        "second_sum",
        room=8,
    )
    taken = [send(piece, mask) for piece, mask in zip(give, Y_MASKS)]
    from_fold, taken = lax.optimization_barrier((mirror_tiles(mine, turn >> 1), taken))
    from_fold = from_fold.astype(F32)

    own, half, *give = run_sum(
        third_sum_kernel,
        [((32, 512), F32), ((32, 512), F32)] + [((96, 512), BF16)] * 3,
        [at, large, terms, *taken],
        "third_sum",
        scalars=1,
        scratch=[((8, 16, 512), F32)],
    )
    taken = [send(piece, mask) for piece, mask in zip(give, Z_MASKS[:3])]
    keep, half, give = run_sum(
        fourth_sum_kernel,
        [((16, 512), F32), ((32, 512), F32), ((48, 512), F32)],
        [own, half, *taken],
        "fourth_sum",
    )
    grad_down, grad_up, half = run_sum(
        last_sum_kernel,
        [((8, 512), F32), ((2, 2048), F32), ((32, 512), F32)],
        [keep, half, send(give, Z_MASKS[3])],
        "last_sum",
    )
    other = send(half, CORE_MASK)
    grad_kernel, grad_gain, grad_bias = run_sum(
        split_kernel,
        [((49, 512), F32), ((1, 512), F32), ((1, 2048), F32)],
        [at, half, other],
        "split",
        scalars=1,
    )
    grad_gain = grad_gain.reshape(512)
    grad_bias = grad_bias.reshape(2048)
    owned = by_cols[:, 3:19] + jnp.pad(from_south.astype(F32), ((0, 0), (0, 13), (0, 0)))
    owned = owned + jnp.pad(from_north.astype(F32) + from_fold, ((0, 0), (13, 0), (0, 0)))
    grad_field = (cotangent.astype(F32) + owned).astype(jnp.bfloat16)
    return (grad_field, grad_up, grad_down, grad_kernel, grad_gain, grad_bias)


def solution(mesh):
    placed = (
        P("lon", "lat", None),
        P("lon", "lat", None),
        P("lon", "lat"),
        P(),
        P(),
        P(),
        P(),
        P(),
        P(),
    )
    return jax.shard_map(
        per_device,
        mesh=mesh,
        in_specs=placed,
        out_specs=(
            P("lon", "lat", None),
            P(("lon", "lat"), None),
            P(("lon", "lat"), None),
            P(),
            P(),
            P(),
        ),
        check_vma=False,
    )
```

```python
import jax
import jax.numpy as jnp
from jax import lax
from jax.experimental import pallas as pl
from jax.experimental.pallas import tpu as pltpu
from jax.sharding import PartitionSpec as P

DEVICES = ("lon", "lat")
X_MASKS = (1, 2, 3)
Y_MASKS = (128, 4, 132)
Z_MASKS = (16, 32, 48, 96)
CORE_MASK = 8


def send(value, mask):
    return lax.ppermute(value, DEVICES, [(i, i ^ mask) for i in range(256)])


def to_next(value):
    return lax.ppermute(value, "lon", [(i, (i + 1) % 32) for i in range(32)])


def to_previous(value):
    return lax.ppermute(value, "lon", [((i + 1) % 32, i) for i in range(32)])


def to_north(value):
    return lax.ppermute(value, "lat", [(i, i + 1) for i in range(7)])


def to_south(value):
    return lax.ppermute(value, "lat", [(i + 1, i) for i in range(7)])


def top_to_next(value):
    pairs = [(i * 8 + 7, (i + 1) % 32 * 8 + 7) for i in range(32)]
    return lax.ppermute(value, DEVICES, pairs)


def top_to_previous(value):
    pairs = [((i + 1) % 32 * 8 + 7, i * 8 + 7) for i in range(32)]
    return lax.ppermute(value, DEVICES, pairs)


def mirror_tiles(value, half_turn):
    def branch(k):
        pairs = [(e * 8 + 7, ((2 * k - e) % 32) * 8 + 7) for e in range(32)]
        return lambda v: lax.ppermute(v, DEVICES, pairs)

    return lax.switch(half_turn, [branch(k) for k in range(16)], value)


ROOT_2_PI = 0.7978845608028654
CUBIC = 0.044715
F32 = jnp.float32
BF16 = jnp.bfloat16


def spread_rows(ext_ref, wide, shifted):
    wide[...] = ext_ref[...].astype(F32)
    for b in range(7):
        shifted[b] = wide[:, b : b + 16, :]


def forward_kernel(
    at_ref, ext_ref, kern_ref, gain_ref, b_up_ref, d_out_ref, order_hbm, w_up_hbm, d_act_hbm,
    d_cells_hbm, half_ref, own_hbm, keep_hbm, send_hbm,
    wide, shifted, normed, ordered, upper, active, tile, mixed_ref, order_ref, w_up_ref, d_act_ref,
    d_upper_ref, own, keep, give, small_ref, d_cells, sems,
):
    core, x_at, y_at = at_ref[0], at_ref[1], at_ref[2]
    loads = [
        pltpu.make_async_copy(order_hbm, order_ref, sems.at[0]),
        pltpu.make_async_copy(w_up_hbm, w_up_ref, sems.at[1]),
        pltpu.make_async_copy(d_act_hbm, d_act_ref, sems.at[2]),
    ]
    for load in loads:
        load.start()
    spread_rows(ext_ref, wide, shifted)

    def conv_step(step, carry):
        lanes = pl.ds(pl.multiple_of(step * 128, 128), 128)
        totals = [jnp.zeros((16, 128), F32)] * 16
        for b in range(7):
            weights = [kern_ref[a * 7 + b : a * 7 + b + 1, lanes] for a in range(7)]
            for r in range(22):
                cells = shifted[b, r, :, lanes]
                for a in range(max(0, r - 15), min(7, r + 1)):
                    totals[r - a] = totals[r - a] + cells * weights[a]
        for x in range(16):
            mixed_ref[x * 16 : x * 16 + 16, lanes] = totals[x]
        return carry

    lax.fori_loop(0, 4, conv_step, 0)

    def norm_step(step, carry):
        rows = pl.ds(pl.multiple_of(step * 32, 32), 32)
        cells = mixed_ref[rows, :]
        center = cells - jnp.mean(cells, axis=-1, keepdims=True)
        spread = jnp.mean(center * center, axis=-1, keepdims=True)
        normed[rows, :] = (center * lax.rsqrt(spread + 1e-6) * gain_ref[...]).astype(BF16)
        return carry

    lax.fori_loop(0, 8, norm_step, 0, unroll=8)
    for load in loads:
        load.wait()
    ordered[...] = jnp.dot(normed[...], order_ref[...], preferred_element_type=F32).astype(BF16)

    for t in range(4):
        lanes = slice(t * 512, t * 512 + 512)
        upper[...] = jnp.dot(normed[...], w_up_ref[:, lanes], preferred_element_type=F32)

        def gelu_step(step, bias):
            rows = pl.ds(pl.multiple_of(step * 32, 32), 32)
            u = upper[rows, :] + b_up_ref[:, lanes]
            square = u * u
            th = jnp.tanh(ROOT_2_PI * (u + CUBIC * (square * u)))
            half = 0.5 * (1.0 + th)
            active[rows, :] = (u * half).astype(BF16)
            slope = half + (0.5 * ROOT_2_PI) * u * (1.0 - th * th) * (1.0 + (3.0 * CUBIC) * square)
            d_up = (d_act_ref[rows, lanes] * slope).astype(BF16)
            d_upper_ref[rows, lanes] = d_up
            return bias + jnp.sum(d_up.astype(F32), axis=0, keepdims=True)

        small_ref[50 + t : 51 + t, :] = lax.fori_loop(0, 8, gelu_step, jnp.zeros((1, 512), F32), unroll=4)
        tile[...] = lax.dot_general(
            active[...], d_out_ref[...], (((0,), (0,)), ((), ())), preferred_element_type=F32
        )
        for y_hi in range(2):
            k_y = (y_hi * 2 + t // 2) ^ y_at
            for k_x in range(4):
                base = y_hi * 32 + (k_x ^ x_at) * 8
                for mine in range(2):
                    at = base + ((1 - core) if mine == 0 else core) * 64
                    piece = jnp.concatenate(
                        [tile[pl.ds(pl.multiple_of(at + zz * 128, 8), 8), :] for zz in range(4)],
                        axis=0,
                    )
                    at = k_y * 64 + (t % 2) * 32
                    rows = pl.ds(pl.multiple_of(at, 32), 32)
                    if mine == 0:
                        give[pl.ds(pl.multiple_of(k_x * 512 + at, 32), 32), :] = piece.astype(BF16)
                    elif k_x == 0:
                        own[rows, :] = piece
                    else:
                        keep[k_x - 1, rows, :] = piece.astype(BF16)

    for t in range(4):
        lanes = slice(t * 512, t * 512 + 512)
        tile[...] = lax.dot_general(
            ordered[...], d_upper_ref[:, lanes], (((0,), (0,)), ((), ())),
            preferred_element_type=F32,
        )
        at = 256 + t * 64
        own[at : at + 64, :] = tile[0:64, :]
        for k in range(4):
            piece = tile[256 + k * 64 : 320 + k * 64, :]
            give[k * 512 + at : k * 512 + at + 64, :] = piece.astype(BF16)
            if k:
                keep[k - 1, at : at + 64, :] = tile[k * 64 : k * 64 + 64, :].astype(BF16)
    stores = [
        pltpu.make_async_copy(give.at[0:2048], send_hbm.at[0:2048], sems.at[3]),
        pltpu.make_async_copy(keep, keep_hbm, sems.at[4]),
        pltpu.make_async_copy(own, own_hbm, sems.at[5]),
    ]
    for store in stores:
        store.start()
    upper[...] = lax.dot_general(
        d_upper_ref[...], w_up_ref[...], (((1,), (1,)), ((), ())), preferred_element_type=F32
    )

    def norm_step(step, gain_sum):
        rows = pl.ds(pl.multiple_of(step * 32, 32), 32)
        cells = mixed_ref[rows, :]
        center = cells - jnp.mean(cells, axis=-1, keepdims=True)
        spread = jnp.mean(center * center, axis=-1, keepdims=True)
        inverse = lax.rsqrt(spread + 1e-6)
        unit = center * inverse
        d = upper[rows, :]
        d_unit = d * gain_ref[...]
        along = jnp.mean(d_unit * unit, axis=-1, keepdims=True)
        d_center = (d_unit - unit * along) * inverse
        d_mixed = d_center - jnp.mean(d_center, axis=-1, keepdims=True)
        d_cells[pl.ds(step * 2, 2)] = d_mixed.reshape(2, 16, 512)
        return gain_sum + jnp.sum(d * unit, axis=0, keepdims=True)

    small_ref[49:50, :] = lax.fori_loop(0, 8, norm_step, jnp.zeros((1, 512), F32), unroll=8)
    small_ref[54:64, :] = jnp.zeros((10, 512), F32)
    stores.append(pltpu.make_async_copy(d_cells, d_cells_hbm, sems.at[7]))
    stores[-1].start()

    def tap_step(step, carry):
        lanes = pl.ds(pl.multiple_of(step * 128, 128), 128)
        d = [d_cells[x, :, lanes] for x in range(16)]
        for b in range(7):
            totals = [jnp.zeros((8, 128), F32)] * 7
            for r in range(22):
                cells = shifted[b, r, :, lanes]
                for a in range(max(0, r - 15), min(7, r + 1)):
                    product = cells * d[r - a]
                    totals[a] = totals[a] + product[:8] + product[8:]
            for a in range(7):
                row = a * 7 + b
                small_ref[row : row + 1, lanes] = jnp.sum(totals[a], axis=0, keepdims=True)
        return carry

    lax.fori_loop(0, 4, tap_step, 0)

    half_ref[...] = small_ref[pl.ds(pl.multiple_of(core * 32, 32), 32), :]
    high, low = two_terms(small_ref[pl.ds(pl.multiple_of((1 - core) * 32, 32), 32), :])
    give[2048:2080, :] = high
    give[2080:2112, :] = low
    stores.append(
        pltpu.make_async_copy(give.at[2048:2112], send_hbm.at[2048:2112], sems.at[6])
    )
    stores[-1].start()
    for store in stores:
        store.wait()


def rim_kernel(d_cells, kern_ref, grad_ref, west_ref, east_ref, moved):
    moved[...] = jnp.zeros_like(moved)
    for b in range(7):
        moved[b, :, b : b + 16, :] = d_cells[...]

    def rim_step(step, carry):
        lanes = pl.ds(pl.multiple_of(step * 128, 128), 128)
        for q in range(3):
            rows = slice(q * 8, q * 8 + 8)
            totals = [jnp.zeros((8, 128), F32)] * 22
            for b in range(1 if q == 2 else 0, 7):
                weights = [kern_ref[a * 7 + b : a * 7 + b + 1, lanes] for a in range(7)]
                for x in range(16):
                    cells = moved[b, x, rows, lanes]
                    for a in range(7):
                        totals[x + a] = totals[x + a] + cells * weights[a]
            for i in range(22):
                grad_ref[i, rows, lanes] = totals[i]
        return carry

    lax.fori_loop(0, 4, rim_step, 0)
    filler = jnp.zeros((3, 8, 512), F32)
    west_ref[...] = jnp.concatenate([grad_ref[0:3], filler], axis=1).astype(BF16)
    east_ref[...] = jnp.concatenate([grad_ref[19:22], filler], axis=1).astype(BF16)


MIB = 1024 * 1024
VMEM = pl.BlockSpec(memory_space=pltpu.VMEM)
SMEM = pl.BlockSpec(memory_space=pltpu.SMEM)
HBM = pl.BlockSpec(memory_space=pl.ANY)


def local_call(kernel, name, shapes, in_specs, out_specs, scratch, operands, flops, room):
    return pl.pallas_call(
        kernel,
        out_shape=[jax.ShapeDtypeStruct(s, d) for s, d in shapes],
        in_specs=in_specs,
        out_specs=out_specs,
        scratch_shapes=[pltpu.VMEM(s, d) if d else pltpu.SemaphoreType.DMA(s) for s, d in scratch],
        compiler_params=pltpu.CompilerParams(vmem_limit_bytes=room * MIB),
        cost_estimate=pl.CostEstimate(flops=flops, bytes_accessed=2000000, transcendentals=0),
        name=name,
    )(*operands)


def run_forward(at, ext, kern, gain, w_up, b_up, d_out, d_act, order):
    square, long = (256, 512), (256, 2048)
    return local_call(
        forward_kernel,
        "forward",
        [
            ((16, 16, 512), F32), ((32, 512), F32),
            ((512, 512), F32), ((3, 512, 512), BF16), ((2112, 512), BF16),
        ],
        [SMEM] + [VMEM] * 5 + [HBM] * 3,
        [HBM, VMEM, HBM, HBM, HBM],
        [
            ((22, 32, 512), F32), ((7, 22, 16, 512), F32), (square, BF16), (square, BF16),
            (square, F32), (square, BF16), ((512, 512), F32), (square, F32), ((512, 512), BF16),
            ((512, 2048), BF16), (long, F32), (long, BF16),
            ((512, 512), F32), ((3, 512, 512), BF16), ((2112, 512), BF16), ((64, 512), F32),
            ((16, 16, 512), F32), ((8,), None),
        ],
        [at, ext, kern, gain, b_up, d_out, order, w_up, d_act],
        20000000000,
        56,
    )


def run_rims(d_cells, kern):
    return local_call(
        rim_kernel,
        "rims",
        [((22, 24, 512), F32), ((3, 32, 512), BF16), ((3, 32, 512), BF16)],
        [VMEM] * 2,
        [VMEM] * 3,
        [((7, 16, 24, 512), F32)],
        [d_cells, kern],
        5000000000,
        16,
    )


def run_sum(kernel, shapes, operands, name, scalars=0, scratch=(), room=4):
    return local_call(
        kernel, name, shapes, [SMEM] * scalars + [VMEM] * (len(operands) - scalars),
        [VMEM] * len(shapes), scratch, operands, 800000000, room,
    )


def two_terms(value):
    high = value.astype(BF16)
    return high, (value - high.astype(F32)).astype(BF16)


def rounded(high, low):
    return high.astype(F32) + low.astype(F32)


def whole(first, rest, rows):
    a, b, c = [ref[rows, :].astype(F32) for ref in rest]
    return (first + a) + (b + c)


def whole_terms(first, refs, at):
    a, b, c = [rounded(ref[at : at + 32, :], ref[at + 32 : at + 64, :]) for ref in refs]
    return (first + a) + (b + c)


def first_sum_kernel(mine_ref, keep_ref, given_ref, half_ref, own_ref, terms_ref, *give_refs):
    own_ref[...] = mine_ref[...] + given_ref[0:512, :].astype(F32)
    half = half_ref[...] + rounded(given_ref[2048:2080, :], given_ref[2080:2112, :])
    high, low = two_terms(half)
    terms_ref[...] = rounded(high, low)
    for k in range(3):
        rows = slice(k * 512 + 512, k * 512 + 1024)
        total = keep_ref[k].astype(F32) + given_ref[rows, :].astype(F32)
        give_refs[k][0:512, :] = total.astype(BF16)
        give_refs[k][512:544, :] = high
        give_refs[k][544:576, :] = low


def second_sum_kernel(own_ref, terms_ref, a_ref, b_ref, c_ref, large_ref, next_ref, *give_refs):
    refs = (a_ref, b_ref, c_ref)
    high, low = two_terms(whole_terms(terms_ref[...], refs, 512))
    next_ref[...] = rounded(high, low)
    for k in range(4):
        pieces = [(0, k * 64, 64)] + [(64 + t * 16, 256 + t * 64 + k * 16, 16) for t in range(4)]
        for target, at, count in pieces:
            rows = slice(at, at + count)
            total = whole(own_ref[rows, :], refs, rows)
            if k == 0:
                large_ref[target : target + count, :] = total
            else:
                give_refs[k - 1][target : target + count, :] = total.astype(BF16)
        if k:
            give_refs[k - 1][128:160, :] = high
            give_refs[k - 1][160:192, :] = low


def third_sum_kernel(at_ref, large_ref, terms_ref, a_ref, b_ref, c_ref, *outs):
    refs = (a_ref, b_ref, c_ref)
    own_ref, half_ref, give_refs, blocks = outs[0], outs[1], outs[2:5], outs[5]
    z_at = at_ref[3]
    high, low = two_terms(whole_terms(terms_ref[...], refs, 128))
    half_ref[...] = rounded(high, low)
    down = whole(large_ref[0:64, :], refs, slice(0, 64))
    up = whole(large_ref[64:128, :], refs, slice(64, 128))
    for z in range(8):
        rows = [up[t * 16 + z * 2 : t * 16 + z * 2 + 2] for t in range(4)]
        blocks[z] = jnp.concatenate([down[z * 8 : z * 8 + 8]] + rows, axis=0)
    for k in range(4):
        for part in range(2):
            block = blocks[z_at ^ k ^ (part * 6)]
            rows = slice(part * 16, part * 16 + 16)
            if k == 0:
                own_ref[rows, :] = block
            else:
                give_refs[k - 1][rows, :] = block.astype(BF16)
        if k:
            give_refs[k - 1][32:64, :] = high
            give_refs[k - 1][64:96, :] = low


def fourth_sum_kernel(own_ref, half_ref, a_ref, b_ref, c_ref, keep_ref, sum_ref, give_ref):
    refs = (a_ref, b_ref, c_ref)
    half = whole_terms(half_ref[...], refs, 32)
    keep_ref[...] = whole(own_ref[0:16, :], refs, slice(0, 16))
    give_ref[0:16, :] = whole(own_ref[16:32, :], refs, slice(16, 32))
    give_ref[16:48, :] = half
    sum_ref[...] = half


def last_sum_kernel(keep_ref, half_ref, got_ref, down_ref, up_ref, sum_ref):
    sum_ref[...] = half_ref[...] + got_ref[16:48, :]
    down_ref[...] = keep_ref[0:8, :] + got_ref[0:8, :]
    up = keep_ref[8:16, :] + got_ref[8:16, :]
    for t in range(4):
        up_ref[:, t * 512 : t * 512 + 512] = up[t * 2 : t * 2 + 2]


def split_kernel(at_ref, half_ref, other_ref, kernel_ref, gain_ref, bias_ref):
    first = at_ref[0] == 0
    half, other = half_ref[...], other_ref[...]
    low, high = jnp.where(first, half, other), jnp.where(first, other, half)
    kernel_ref[0:32, :] = low
    kernel_ref[32:49, :] = high[0:17]
    gain_ref[...] = high[17:18]
    for t in range(4):
        bias_ref[:, t * 512 : t * 512 + 512] = high[18 + t : 19 + t]


def per_device(
    field, cotangent, land_sea, fold_partner, depth_kernel, norm_gain, w_up, b_up, w_down
):
    width_lon, width_lat, channels = field.shape
    lon_at = lax.axis_index("lon")
    lat_at = lax.axis_index("lat")
    core = lon_at & 1
    z_at = (lon_at >> 1) & 7
    y_at = ((lat_at >> 2) << 1) + (lon_at >> 4)
    x_at = lat_at & 3
    is_north = lat_at == lax.axis_size("lat") - 1
    from_end = 511 - fold_partner[0]
    turn = 31 - (from_end >> 4)
    shift = 16 - (from_end & 15)
    even = (turn & 1) == 0

    top_rows = field[:, width_lat - 3 :, :]
    mine = mirror_tiles(top_rows, turn >> 1)
    south = to_north(top_rows)
    north = to_south(field[:, 0:3, :])
    low = jnp.where(even, to_previous(mine), mine)
    high = jnp.where(even, mine, to_next(mine))
    fold = lax.dynamic_slice_in_dim(jnp.concatenate([low, high], axis=0), shift, 16, axis=0)
    north = jnp.where(is_north, fold[::-1, ::-1, :], north)
    column = jnp.concatenate([south, field, north], axis=1)
    extended = jnp.concatenate(
        [to_next(column[width_lon - 3 :]), column, to_previous(column[:3])], axis=0
    )
    extended = jnp.pad(extended, ((0, 0), (0, 10), (0, 0)))
    tokens = width_lon * width_lat
    d_out = cotangent.reshape(tokens, channels) * land_sea.reshape(tokens, 1).astype(jnp.bfloat16)
    d_act = lax.dot_general(
        d_out, w_down, (((1,), (1,)), ((), ())), preferred_element_type=jnp.float32
    )
    row = jnp.arange(512, dtype=jnp.int32)
    block = row >> 1
    y_of = (((block >> 2) & 1) << 1) + (block >> 7)
    goes_to = (
        (((block >> 3) & 1) ^ core) * 256
        + ((block & 3) ^ x_at) * 64
        + (y_of ^ y_at) * 16
        + ((block >> 4) & 7) * 2
        + (row & 1)
    )
    order = (goes_to[:, None] == row[None, :]).astype(jnp.bfloat16)
    at = jnp.stack([core, x_at, y_at, z_at]).astype(jnp.int32)
    gain = norm_gain.reshape(1, channels)
    d_cells, half, mine, keep, give = run_forward(
        at, extended, depth_kernel, gain, w_up, b_up.reshape(1, 2048), d_out, d_act, order
    )

    given = send(give, CORE_MASK)
    grad_ext, west_rim, east_rim = run_rims(d_cells, depth_kernel)
    given, west_rim, east_rim = lax.optimization_barrier((given, west_rim, east_rim))
    own, terms, *give = run_sum(
        first_sum_kernel,
        [((512, 512), F32), ((32, 512), F32)] + [((576, 512), BF16)] * 3,
        [mine, keep, given, half],
        "first_sum",
        room=16,
    )
    taken = [send(piece, mask) for piece, mask in zip(give, X_MASKS)]

    rim = jnp.bfloat16
    from_west, from_east = to_next(east_rim), to_previous(west_rim)
    from_west, from_east = from_west[:, :22].astype(F32), from_east[:, :22].astype(F32)
    by_cols = (
        grad_ext[3:19, :22]
        + jnp.pad(from_west, ((0, 13), (0, 0), (0, 0)))
        + jnp.pad(from_east, ((13, 0), (0, 0), (0, 0)))
    )
    top_rim = by_cols[:, 19:22].astype(rim)
    from_south = to_north(top_rim)
    from_north = to_south(by_cols[:, 0:3].astype(rim))
    strip = jnp.where(is_north, top_rim, jnp.zeros_like(top_rim))[::-1, ::-1, :]
    spread = lax.dynamic_update_slice_in_dim(
        jnp.zeros((32, 3, channels), rim), strip, shift, axis=0
    )
    none = jnp.zeros_like(spread[:16])
    mine = jnp.where(even, spread[16:], spread[:16])
    mine = mine + top_to_next(jnp.where(even, spread[:16], none))
    mine = mine + top_to_previous(jnp.where(even, none, spread[16:]))
    mine, from_south, from_north, taken = lax.optimization_barrier(
        (mine, from_south, from_north, taken)
    )

    large, terms, *give = run_sum(
        second_sum_kernel,
        [((128, 512), F32), ((32, 512), F32)] + [((192, 512), BF16)] * 3,
        [own, terms, *taken],
        "second_sum",
        room=56,
    )
    taken = [send(piece, mask) for piece, mask in zip(give, Y_MASKS)]
    from_fold, taken = lax.optimization_barrier((mirror_tiles(mine, turn >> 1), taken))
    from_fold = from_fold.astype(F32)

    own, half, *give = run_sum(
        third_sum_kernel,
        [((32, 512), F32), ((32, 512), F32)] + [((96, 512), BF16)] * 3,
        [at, large, terms, *taken],
        "third_sum",
        scalars=1,
        scratch=[((8, 16, 512), F32)],
        room=56,
    )
    taken = [send(piece, mask) for piece, mask in zip(give, Z_MASKS[:3])]
    keep, half, give = run_sum(
        fourth_sum_kernel,
        [((16, 512), F32), ((32, 512), F32), ((48, 512), F32)],
        [own, half, *taken],
        "fourth_sum",
    )
    grad_down, grad_up, half = run_sum(
        last_sum_kernel,
        [((8, 512), F32), ((2, 2048), F32), ((32, 512), F32)],
        [keep, half, send(give, Z_MASKS[3])],
        "last_sum",
    )
    other = send(half, CORE_MASK)
    grad_kernel, grad_gain, grad_bias = run_sum(
        split_kernel,
        [((49, 512), F32), ((1, 512), F32), ((1, 2048), F32)],
        [at, half, other],
        "split",
        scalars=1,
    )
    grad_gain = grad_gain.reshape(512)
    grad_bias = grad_bias.reshape(2048)
    owned = by_cols[:, 3:19] + jnp.pad(from_south.astype(F32), ((0, 0), (0, 13), (0, 0)))
    owned = owned + jnp.pad(from_north.astype(F32) + from_fold, ((0, 0), (13, 0), (0, 0)))
    grad_field = (cotangent.astype(F32) + owned).astype(jnp.bfloat16)
    return (grad_field, grad_up, grad_down, grad_kernel, grad_gain, grad_bias)


def solution(mesh):
    placed = (
        P("lon", "lat", None),
        P("lon", "lat", None),
        P("lon", "lat"),
        P(),
        P(),
        P(),
        P(),
        P(),
        P(),
    )
    return jax.shard_map(
        per_device,
        mesh=mesh,
        in_specs=placed,
        out_specs=(
            P("lon", "lat", None),
            P(("lon", "lat"), None),
            P(("lon", "lat"), None),
            P(),
            P(),
            P(),
        ),
        check_vma=False,
    )
```
